32 devices in a mesh: row: 4 (over x, core), col: 8 (over z, y).
Axes of the slice: x: 2, y: 2, z: 4, core: 2. Of those that a mesh axis runs over, the one named last changes fastest.
Arguments:
- x_in: bfloat16 [12608, 512], P(('col', 'row')), may hold values from -6 to 6
- cotangent: bfloat16 [12608, 512], P(('col', 'row')), may hold values from -6 to 6
- teacher: bfloat16 [12608, 512], P(('col', 'row')), may hold values from -6 to 6
- valid_mask: int32 [12608], P('col'), may hold values from 0 to 1, as said below
- routes: int32 [2, 12608], replicated, may hold values from 0 to 31, as said below
- gate_weights: float32 [2, 12608], replicated, may hold values from 0.2 to 1
- norm_params: float32 [4, 512], P(None, 'row'), may hold values from -1 to 1.8, as said below
- qkv_weight: float32 [512, 1536], P('row', 'col'), may hold values from -0.25 to 0.25
- out_weight: float32 [512, 512], P('col', 'row'), may hold values from -0.75 to 0.75
- up_weight: float32 [32, 512, 2048], P('col', 'row'), may hold values from -0.25 to 0.25
- down_weight: float32 [32, 512, 2048], P('col', 'row'), may hold values from -0.125 to 0.125
- norm_first: float32 [4, 512], P(None, 'row'), may hold values from -40 to 40
- norm_second: float32 [4, 512], P(None, 'row'), may hold values from 3.152 to 12.608
- qkv_first: float32 [512, 1536], P('row', 'col'), may hold values from -20 to 20
- qkv_second: float32 [512, 1536], P('row', 'col'), may hold values from 1.13472 to 4.53888
- out_first: float32 [512, 512], P('col', 'row'), may hold values from -12 to 12
- out_second: float32 [512, 512], P('col', 'row'), may hold values from 0.289984 to 1.13472
- up_first: float32 [32, 512, 2048], P('col', 'row'), may hold values from -6 to 6
- up_second: float32 [32, 512, 2048], P('col', 'row'), may hold values from 0.07092 to 0.28368
- down_first: float32 [32, 512, 2048], P('col', 'row'), may hold values from -7 to 7
- down_second: float32 [32, 512, 2048], P('col', 'row'), may hold values from 0.10244 to 0.40976
Outputs:
- mixed_out: bfloat16 [12608, 512], P(('col', 'row'))
- input_grad: float32 [12608, 512], P(('col', 'row'))
- loss_value: float32 [], replicated
- norm_first_new: float32 [4, 512], P(None, 'row')
- norm_second_new: float32 [4, 512], P(None, 'row')
- norm_new: float32 [4, 512], P(None, 'row')
- qkv_first_new: float32 [512, 1536], P('row', 'col')
- qkv_second_new: float32 [512, 1536], P('row', 'col')
- qkv_new: float32 [512, 1536], P('row', 'col')
- out_first_new: float32 [512, 512], P('col', 'row')
- out_second_new: float32 [512, 512], P('col', 'row')
- out_new: float32 [512, 512], P('col', 'row')
- up_first_new: float32 [32, 512, 2048], P('col', 'row')
- up_second_new: float32 [32, 512, 2048], P('col', 'row')
- up_new: float32 [32, 512, 2048], P('col', 'row')
- down_first_new: float32 [32, 512, 2048], P('col', 'row')
- down_second_new: float32 [32, 512, 2048], P('col', 'row')
- down_new: float32 [32, 512, 2048], P('col', 'row')
The draws below stay inside these ranges and needn't reach their ends.
Inputs may be any that keep to these rules, and one draw needn't show every extreme that they name: `valid_mask`: 1 marks a valid token; the last token is always valid. `routes`: each column names 2 different experts; over all tokens no expert is named more than 984 times, and one exactly 984 times; every expert is named. `norm_params`: rows 0 and 2 are gains, rows 1 and 3 biases.
All inputs are finite; a program needn't handle non-finite values.
Results may differ from the reference program's by a relative error of at most 0.01.
Values may be sent and summed in bfloat16 or wider, within the bound.
No kernel may reach another device: no remote copies, remote signals or barrier semaphores. Data moves between devices by JAX's collectives and lax.ppermute only.
A program may use at most 320 MiB of HBM per device.

```python
import math
import jax
import jax.numpy as jnp
from jax import lax

D = 512
HEADS = 8
HEAD_DIM = 64
FF = 2048
EXPERTS = 32
TOP = 2
IMG_LEN = 197
IMG_DEV = 8
STEP = 5
TOKENS = 12608
CAP = 984


def draw_valid_mask(key, part):
    key = jax.random.fold_in(key, 7)
    coin = jax.random.randint(key, (TOKENS,), 0, 4 * TOKENS)
    position = jnp.arange(TOKENS, dtype=jnp.int32)
    chosen = (coin < TOKENS + 2 * position) | (position == TOKENS - 1)
    return chosen.astype(jnp.int32)


def draw_routes(key, part):
    key = jax.random.fold_in(key, 5)
    expert_key, token_key, swap_key = jax.random.split(key, 3)
    picks_total = TOKENS * TOP
    rest_picks = picks_total - CAP
    base_load = rest_picks // (EXPERTS - 1)
    extra_load = rest_picks - base_load * (EXPERTS - 1)
    expert_ids = jnp.arange(EXPERTS, dtype=jnp.int32)
    loads = jnp.where(expert_ids == 0, CAP, base_load + (expert_ids - 1 < extra_load).astype(jnp.int32)).astype(jnp.int32)
    ends_at = jnp.cumsum(loads).astype(jnp.int32)
    position = jnp.arange(picks_total, dtype=jnp.int32)
    labels = jnp.sum((position[:, None] >= ends_at[None, :]).astype(jnp.int32), axis=1).astype(jnp.int32)
    relabel = jax.random.permutation(expert_key, EXPERTS).astype(jnp.int32)
    labels = relabel[labels]
    first_pick = labels[:TOKENS]
    second_pick = labels[TOKENS:]
    swapped = jax.random.randint(swap_key, (TOKENS,), 0, 2)
    upper = jnp.where(swapped == 1, second_pick, first_pick)
    lower = jnp.where(swapped == 1, first_pick, second_pick)
    order = jax.random.permutation(token_key, TOKENS)
    return jnp.stack([upper[order], lower[order]], axis=0).astype(jnp.int32)


def draw_norm_params(key, part):
    key = jax.random.fold_in(key, 11)
    gain_key, shift_key = jax.random.split(key)
    ramp = 0.5 + jnp.arange(D, dtype=jnp.float32) / D
    gains = ramp[None, :] * jax.random.uniform(gain_key, (2, D), jnp.float32, 0.8, 1.2)
    shifts = jnp.clip(0.1 * jax.random.normal(shift_key, (2, D), jnp.float32), -0.5, 0.5)
    return jnp.stack([gains[0], shifts[0], gains[1], shifts[1]], axis=0)


def steps_of(own_key, dims, cuts, least, largest):
    gain = 1.0
    for dim, parts in cuts:
        draws = jax.random.uniform(jax.random.fold_in(jax.random.fold_in(own_key, 6), dim), (parts,), jnp.float32, least / len(cuts), largest / len(cuts))
        gain = gain * jnp.repeat(jnp.exp(draws), dims[dim] // parts).reshape((-1,) + (1,) * (len(dims) - 1 - dim))
    return gain


def gaussian(rng, dims, deviation, reach, shards=(), kind=jnp.bfloat16):
    gain = steps_of(rng, dims, shards, -0.22, 0.18) if shards else 1.0
    values = jax.random.normal(rng, dims, jnp.float32) * deviation * gain
    return jnp.minimum(jnp.maximum(values, -reach), reach).astype(kind)


def setup_inputs(seed: int = 0) -> dict:
    streams_of = jax.random.split(jax.random.key(seed), 22)
    return {
        "x_in": gaussian(streams_of[0], (TOKENS, D), 1.0, 6.0, ((0, 32),)),
        "cotangent": gaussian(streams_of[1], (TOKENS, D), 1.0, 6.0, ((0, 32),)),
        "teacher": gaussian(streams_of[2], (TOKENS, D), 1.0, 6.0, ((0, 32),)),
        "valid_mask": draw_valid_mask(jax.random.fold_in(streams_of[21], 71), 0),
        "routes": draw_routes(jax.random.fold_in(streams_of[21], 71), 0),
        "gate_weights": jnp.clip(jax.random.uniform(streams_of[5], (TOP, TOKENS), jnp.float32, 0.2, 1.0), 0.2, 1.0),
        "norm_params": draw_norm_params(jax.random.fold_in(streams_of[21], 71), 0),
        "qkv_weight": gaussian(streams_of[7], (D, 3 * D), D ** -0.5, 0.25, ((0, 4), (1, 8)), jnp.float32),
        "out_weight": gaussian(streams_of[8], (D, D), (D // 8) ** -0.5, 0.75, ((0, 8), (1, 4)), jnp.float32),
        "up_weight": gaussian(streams_of[9], (EXPERTS, D, FF), D ** -0.5, 0.25, ((0, 8), (1, 4)), jnp.float32),
        "down_weight": gaussian(streams_of[10], (EXPERTS, D, FF), FF ** -0.5, 0.125, ((0, 8), (1, 4)), jnp.float32),
        "norm_first": gaussian(streams_of[11], (4, D), (0.055 * TOKENS ** 0.5), 40.0, ((1, 4),), jnp.float32),
        "norm_second": jnp.clip(jnp.exp(math.log(12.608) - 1.3862944 * jax.random.uniform(streams_of[12], (4, D), jnp.float32) ** steps_of(streams_of[12], (4, D), ((1, 4),), -0.2, 0.2)), 3.152, 12.608),
        "qkv_first": gaussian(streams_of[13], (D, 3 * D), (0.03 * TOKENS ** 0.5), 20.0, ((0, 4), (1, 8)), jnp.float32),
        "qkv_second": jnp.clip(jnp.exp(math.log(4.53888) - 1.3862944 * jax.random.uniform(streams_of[14], (D, 3 * D), jnp.float32) ** steps_of(streams_of[14], (D, 3 * D), ((0, 4), (1, 8)), -0.2, 0.2)), 1.13472, 4.53888),
        "out_first": gaussian(streams_of[15], (D, D), (0.017 * TOKENS ** 0.5), 12.0, ((0, 8), (1, 4)), jnp.float32),
        "out_second": jnp.clip(jnp.exp(math.log(1.13472) - 1.3643155 * jax.random.uniform(streams_of[16], (D, D), jnp.float32) ** steps_of(streams_of[16], (D, D), ((0, 8), (1, 4)), -0.2, 0.2)), 0.289984, 1.13472),
        "up_first": gaussian(streams_of[17], (EXPERTS, D, FF), (0.033 * (TOKENS * TOP // EXPERTS) ** 0.5), 6.0, ((0, 8), (1, 4)), jnp.float32),
        "up_second": jnp.clip(jnp.exp(math.log(0.28368) - 1.3862944 * jax.random.uniform(streams_of[18], (EXPERTS, D, FF), jnp.float32) ** steps_of(streams_of[18], (EXPERTS, D, FF), ((0, 8), (1, 4)), -0.2, 0.2)), 0.07092, 0.28368),
        "down_first": gaussian(streams_of[19], (EXPERTS, D, FF), (0.04 * (TOKENS * TOP // EXPERTS) ** 0.5), 7.0, ((0, 8), (1, 4)), jnp.float32),
        "down_second": jnp.clip(jnp.exp(math.log(0.40976) - 1.3862944 * jax.random.uniform(streams_of[20], (EXPERTS, D, FF), jnp.float32) ** steps_of(streams_of[20], (EXPERTS, D, FF), ((0, 8), (1, 4)), -0.2, 0.2)), 0.10244, 0.40976),
    }


@jax.custom_vjp
def low(v):
    return lax.optimization_barrier(v.astype(jnp.bfloat16)).astype(jnp.float32)

@jax.custom_vjp
def low_back(v):
    return v

def low_keep(v):
    return (low(v), None)

def low_pass(kept, grad):
    return (grad,)

def back_keep(v):
    return (v, None)

def back_low(kept, grad):
    return (low(grad),)
low.defvjp(low_keep, low_pass)
low_back.defvjp(back_keep, back_low)
highest = lax.Precision.HIGHEST
norm_eps = 1e-06
beta_one = 0.9
beta_two = 0.999
adam_eps = 1e-08
decay_matrix = 0.1
rate_norm = 0.4
rate_qkv = 0.02
rate_out = 0.06
rate_up = 0.02
rate_down = 0.01

def layer_norm(stream, gain_row, shift_row):
    center = lax.optimization_barrier(jnp.mean(stream, axis=-1, keepdims=True))
    offset = stream - center
    spread = lax.optimization_barrier(jnp.mean(offset * offset, axis=-1, keepdims=True))
    return offset * lax.rsqrt(spread + norm_eps) * gain_row + shift_row

def dispatch_tables(routes, capacity):
    flat_routes = routes.reshape(-1)
    picks_total = flat_routes.shape[0]
    order_idx = jnp.argsort(flat_routes, stable=True).astype(jnp.int32)
    sorted_experts = flat_routes[order_idx]
    expert_ids = jnp.arange(EXPERTS, dtype=jnp.int32)
    expert_load = lax.optimization_barrier(jnp.sum((flat_routes[:, None] == expert_ids[None, :]).astype(jnp.int32), axis=0)).astype(jnp.int32)
    starts_at = (jnp.cumsum(expert_load) - expert_load).astype(jnp.int32)
    position = jnp.arange(picks_total, dtype=jnp.int32)
    slot_index = (sorted_experts * capacity + position - starts_at[sorted_experts]).astype(jnp.int32)
    slot_token = jnp.zeros((EXPERTS * capacity,), jnp.int32).at[slot_index].set(order_idx // TOP)
    slot_used = jnp.zeros((EXPERTS * capacity,), jnp.int32).at[slot_index].set(1)
    pick_slot = jnp.zeros((picks_total,), jnp.int32).at[order_idx].set(slot_index)
    return (slot_token, slot_used, order_idx, slot_index, pick_slot.reshape(-1, TOP))

def attend_group(group_qkv):
    images = group_qkv.shape[0]
    split_heads = group_qkv.reshape(images, IMG_LEN, 3, HEADS, HEAD_DIM)
    queries = split_heads[:, :, 0]
    key_part = split_heads[:, :, 1]
    value_part = split_heads[:, :, 2]
    scores = low_back(jnp.einsum('gqhd,gkhd->ghqk', queries, key_part, precision=highest) * HEAD_DIM ** (-0.5))
    weights = low(jax.nn.softmax(scores, axis=-1))
    mixed_heads = jnp.einsum('ghqk,gkhd->gqhd', weights, value_part, precision=highest)
    return mixed_heads.reshape(images, IMG_LEN, HEADS * HEAD_DIM)

def expert_pass(operands):
    slot_rows, weight_up, weight_down = operands
    hidden_pre = low_back(jnp.dot(slot_rows, low(weight_up), precision=highest))
    hidden_act = low(jax.nn.gelu(hidden_pre, approximate=True))
    return low_back(jnp.dot(hidden_act, jnp.transpose(low(weight_down)), precision=highest))

def forward(stream, norm_params, qkv_weight, out_weight, up_weight, down_weight, gate_rows, tables):
    slot_token, slot_used, pick_slot = tables
    normed = low(layer_norm(stream, norm_params[0], norm_params[1]))
    projected = low_back(low(jnp.dot(normed, low(qkv_weight), precision=highest)))
    grouped = projected.reshape(-1, IMG_DEV, IMG_LEN, 3 * D)
    attended = lax.map(jax.checkpoint(attend_group), grouped).reshape(-1, D)
    attended = low_back(low(attended))
    branch_out = low_back(jnp.dot(attended, low(out_weight), precision=highest))
    middle = stream + branch_out
    second = low(layer_norm(middle, norm_params[2], norm_params[3]))
    slot_rows = (second[slot_token] * slot_used.astype(jnp.float32)[:, None]).reshape(EXPERTS, -1, D)
    expert_out = lax.map(jax.checkpoint(expert_pass), (slot_rows, up_weight, down_weight)).reshape(-1, D)
    combined = lax.optimization_barrier(jnp.sum(expert_out[pick_slot] * gate_rows[:, :, None], axis=1))
    return middle + low_back(combined)

def adam_update(weight, first_moment, second_moment, gradient, step_rate, decay_factor):
    first_new = beta_one * first_moment + (1.0 - beta_one) * gradient
    second_new = beta_two * second_moment + (1.0 - beta_two) * gradient * gradient
    first_hat = first_new / (1.0 - beta_one ** STEP)
    second_hat = second_new / (1.0 - beta_two ** STEP)
    weight_new = weight - step_rate * (first_hat / (jnp.sqrt(second_hat) + adam_eps) + decay_factor * weight)
    return (first_new, second_new, weight_new)

def reference(x_in, cotangent, teacher, valid_mask, routes, gate_weights, norm_params, qkv_weight, out_weight, up_weight, down_weight, norm_first, norm_second, qkv_first, qkv_second, out_first, out_second, up_first, up_second, down_first, down_second):
    route_rows = jnp.transpose(routes).astype(jnp.int32)
    gate_rows = jnp.transpose(gate_weights)
    slot_token, slot_used, order_idx, slot_index, pick_slot = dispatch_tables(route_rows, CAP)
    tables = (slot_token, slot_used, pick_slot)
    stream = x_in.astype(jnp.float32)

    def whole_layer(stream_in, norm_in, qkv_in, out_in, up_in, down_in):
        return forward(stream_in, norm_in, qkv_in, out_in, up_in, down_in, gate_rows, tables)
    result, pullback = jax.vjp(whole_layer, stream, norm_params, qkv_weight, out_weight, up_weight, down_weight)
    valid_rows = valid_mask.astype(jnp.float32)[:, None]
    mismatch = result - teacher.astype(jnp.float32)
    valid_total = jnp.sum(valid_mask.astype(jnp.float32))
    loss_value = jnp.sum(valid_rows * mismatch * mismatch) / valid_total
    grad_out = cotangent.astype(jnp.float32) + 2.0 / valid_total * valid_rows * mismatch
    input_grad, norm_grad, qkv_grad, out_grad, up_grad, down_grad = pullback(grad_out)
    norm_one, norm_two, norm_new = adam_update(norm_params, norm_first, norm_second, norm_grad, rate_norm, 0.0)
    qkv_one, qkv_two, qkv_new = adam_update(qkv_weight, qkv_first, qkv_second, qkv_grad, rate_qkv, decay_matrix)
    out_one, out_two, out_new = adam_update(out_weight, out_first, out_second, out_grad, rate_out, decay_matrix)
    up_one, up_two, up_new = adam_update(up_weight, up_first, up_second, up_grad, rate_up, decay_matrix)
    down_one, down_two, down_new = adam_update(down_weight, down_first, down_second, down_grad, rate_down, decay_matrix)
    return (result.astype(jnp.bfloat16), input_grad, loss_value, norm_one, norm_two, norm_new, qkv_one, qkv_two, qkv_new, out_one, out_two, out_new, up_one, up_two, up_new, down_one, down_two, down_new)
```

```python
import functools

import jax
import jax.numpy as jnp
from jax import lax
from jax.experimental import pallas as pl
from jax.experimental.pallas import tpu as pltpu
from jax.sharding import PartitionSpec as P

HEADS = 8
HEAD_DIM = 64
EXPERTS = 32
TOP = 2
IMG_LEN = 197
STEP = 5
IMG_PAD = 256
BOTH = ("col", "row")
VMEM_BYTES = 56 * 1024 * 1024

norm_eps = 1e-06
beta_one = 0.9
beta_two = 0.999
adam_eps = 1e-08
decay_matrix = 0.1
rate_norm = 0.4
rate_qkv = 0.02
rate_out = 0.06
rate_up = 0.02
rate_down = 0.01


def dispatch_tables(routes, capacity):
    flat_routes = routes.reshape(-1)
    picks_total = flat_routes.shape[0]
    order_idx = jnp.argsort(flat_routes, stable=True)
    sorted_experts = flat_routes[order_idx]
    expert_ids = jnp.arange(EXPERTS, dtype=jnp.int32)
    expert_load = jnp.sum((flat_routes[:, None] == expert_ids[None, :]).astype(jnp.int32), axis=0)
    starts_at = jnp.cumsum(expert_load) - expert_load
    position = jnp.arange(picks_total, dtype=jnp.int32)
    slot_index = sorted_experts * capacity + position - starts_at[sorted_experts]
    slot_token = jnp.zeros((EXPERTS * capacity,), jnp.int32).at[slot_index].set(order_idx // TOP)
    slot_used = jnp.zeros((EXPERTS * capacity,), jnp.int32).at[slot_index].set(1)
    pick_slot = jnp.zeros((picks_total,), jnp.int32).at[order_idx].set(slot_index)
    return (slot_token, slot_used, order_idx, slot_index, pick_slot.reshape(-1, TOP))


def gelu_tanh(inner_value):
    return jax.nn.gelu(inner_value, approximate=True)


def spread_cols(values):
    return lax.all_gather(values, "col", axis=0, tiled=True)


def spread_rows(values):
    return lax.all_gather(values, "row", axis=0, tiled=True)


def sum_rows(term_fn, row_total):
    return lax.psum_scatter(
        term_fn(jnp.int32(0), row_total * lax.axis_size("row")),
        "row",
        scatter_dimension=0,
        tiled=True,
    )


def sum_cols(term_fn, row_total):
    return lax.psum_scatter(
        term_fn(jnp.int32(0), row_total * lax.axis_size("col")),
        "col",
        scatter_dimension=0,
        tiled=True,
    )


def to_heads(values):
    return lax.all_to_all(values, "col", split_axis=0, concat_axis=1, tiled=True)


def from_heads(values):
    return lax.all_to_all(values, "col", split_axis=1, concat_axis=0, tiled=True)


def token_sums(first_part, second_part):
    return lax.psum((first_part, second_part), "row")


def norm_forward(stream, gain_row, shift_row):
    full_width = stream.shape[1] * lax.axis_size("row")
    sum_plain, squares = token_sums(jnp.sum(stream, axis=1), jnp.sum(stream * stream, axis=1))
    center = sum_plain / full_width
    offset = stream - center[:, None]
    spread = squares / full_width - center * center
    inverse = lax.rsqrt(spread + norm_eps)
    scaled = offset * inverse[:, None]
    return (scaled * gain_row + shift_row, scaled, inverse)


def norm_backward(upstream, scaled, inverse, gain_row):
    full_width = scaled.shape[1] * lax.axis_size("row")
    dscaled = upstream * gain_row
    sum_plain, sum_cross = token_sums(jnp.sum(dscaled, axis=1), jnp.sum(dscaled * scaled, axis=1))
    inner_grad = (
        dscaled - (sum_plain / full_width)[:, None] - scaled * (sum_cross / full_width)[:, None]
    )
    return (
        inner_grad * inverse[:, None],
        jnp.sum(upstream * scaled, axis=0),
        jnp.sum(upstream, axis=0),
    )


def attend_local(packed):
    images = packed.shape[0] // IMG_LEN
    split_heads = packed.reshape(images, IMG_LEN, 3, HEADS, HEAD_DIM)
    scores = jnp.einsum(
        "gqhd,gkhd->ghqk",
        split_heads[:, :, 0],
        split_heads[:, :, 1],
        preferred_element_type=jnp.float32,
    ) * HEAD_DIM ** (-0.5)
    top_score = jnp.max(scores, axis=-1, keepdims=True)
    shifted = jnp.exp(scores - top_score)
    totals = jnp.sum(shifted, axis=-1, keepdims=True)
    weights = (shifted / totals).astype(jnp.bfloat16)
    log_norm = top_score + jnp.log(totals)
    mixed_heads = jnp.einsum(
        "ghqk,gkhd->gqhd", weights, split_heads[:, :, 2], preferred_element_type=jnp.float32
    )
    return (mixed_heads.reshape(images * IMG_LEN, HEADS * HEAD_DIM), log_norm)


def attend_back(packed, log_norm, upstream):
    images = packed.shape[0] // IMG_LEN
    split_heads = packed.reshape(images, IMG_LEN, 3, HEADS, HEAD_DIM)
    queries = split_heads[:, :, 0]
    key_part = split_heads[:, :, 1]
    value_part = split_heads[:, :, 2]
    grad_mixed = upstream.reshape(images, IMG_LEN, HEADS, HEAD_DIM)
    score_scale = HEAD_DIM ** (-0.5)
    scores = (
        jnp.einsum("gqhd,gkhd->ghqk", queries, key_part, preferred_element_type=jnp.float32)
        * score_scale
    )
    prob_rows = jnp.exp(scores - log_norm)
    grad_value = jnp.einsum(
        "ghqk,gqhd->gkhd",
        prob_rows.astype(jnp.bfloat16),
        grad_mixed,
        preferred_element_type=jnp.float32,
    )
    grad_probs = jnp.einsum(
        "gqhd,gkhd->ghqk", grad_mixed, value_part, preferred_element_type=jnp.float32
    )
    grad_scores = (
        prob_rows * (grad_probs - jnp.sum(prob_rows * grad_probs, axis=-1, keepdims=True))
    ).astype(jnp.bfloat16)
    grad_query = (
        jnp.einsum("ghqk,gkhd->gqhd", grad_scores, key_part, preferred_element_type=jnp.float32)
        * score_scale
    )
    grad_key = (
        jnp.einsum("ghqk,gqhd->gkhd", grad_scores, queries, preferred_element_type=jnp.float32)
        * score_scale
    )
    stacked = jnp.stack([grad_query, grad_key, grad_value], axis=2)
    return stacked.reshape(images * IMG_LEN, 3 * HEADS * HEAD_DIM)


def adam_update(weight, first_moment, second_moment, gradient, step_rate, decay_factor):
    first_new = beta_one * first_moment + (1.0 - beta_one) * gradient
    second_new = beta_two * second_moment + (1.0 - beta_two) * gradient * gradient
    first_hat = first_new / (1.0 - beta_one**STEP)
    second_hat = second_new / (1.0 - beta_two**STEP)
    weight_new = weight - step_rate * (
        first_hat / (jnp.sqrt(second_hat) + adam_eps) + decay_factor * weight
    )
    return (first_new, second_new, weight_new)


def general_body(
    x_in,
    cotangent,
    teacher,
    valid_mask,
    routes,
    gate_weights,
    norm_params,
    qkv_weight,
    out_weight,
    up_weight,
    down_weight,
    norm_first,
    norm_second,
    qkv_first,
    qkv_second,
    out_first,
    out_second,
    up_first,
    up_second,
    down_first,
    down_second,
):
    token_total = routes.shape[1]
    row_devices = lax.axis_size("row")
    col_devices = lax.axis_size("col")
    capacity = row_devices * (5 * token_total * TOP // (4 * EXPERTS) // row_devices)
    experts_here = EXPERTS // col_devices
    first_mine = lax.axis_index("col") * experts_here
    slot_share = capacity * experts_here // row_devices
    route_rows = jnp.stack([routes[k] for k in range(TOP)], axis=1)
    gate_rows = jnp.stack([gate_weights[k] for k in range(TOP)], axis=1)
    slot_token, slot_used, order_idx, slot_index, pick_slot = dispatch_tables(route_rows, capacity)
    slot_gate = (
        jnp.zeros((EXPERTS * capacity,), jnp.float32)
        .at[slot_index]
        .set(gate_rows.reshape(-1)[order_idx])
    )
    mine_token = jnp.transpose(
        lax.dynamic_slice_in_dim(slot_token.reshape(EXPERTS, capacity), first_mine, experts_here, 0)
    )
    mine_used = jnp.transpose(
        lax.dynamic_slice_in_dim(slot_used.reshape(EXPERTS, capacity), first_mine, experts_here, 0)
    ).astype(jnp.bfloat16)[:, :, None]
    mine_gate = jnp.transpose(
        lax.dynamic_slice_in_dim(slot_gate.reshape(EXPERTS, capacity), first_mine, experts_here, 0)
    )[:, :, None]
    pick_expert = pick_slot // capacity
    pick_owned = ((pick_expert >= first_mine) & (pick_expert < first_mine + experts_here)).astype(
        jnp.float32
    )
    pick_local = pick_slot % capacity * experts_here + jnp.clip(
        pick_expert - first_mine, 0, experts_here - 1
    )
    x_block, cot_block, teacher_block = (
        lax.all_to_all(x_in, "row", split_axis=1, concat_axis=0, tiled=True),
        lax.all_to_all(cotangent, "row", split_axis=1, concat_axis=0, tiled=True),
        lax.all_to_all(teacher, "row", split_axis=1, concat_axis=0, tiled=True),
    )
    stream = x_block.astype(jnp.float32)
    normed, normed_scaled, normed_inverse = norm_forward(stream, norm_params[0], norm_params[1])
    normed_low = normed.astype(jnp.bfloat16)
    normed_all = spread_cols(normed_low)
    qkv_low = qkv_weight.astype(jnp.bfloat16)

    def qkv_term(row_start, row_count):
        return jnp.dot(normed_all, qkv_low, preferred_element_type=jnp.float32)

    projected = sum_rows(qkv_term, token_total // row_devices)
    packed = to_heads(projected.astype(jnp.bfloat16))
    attended, log_norm = attend_local(packed)
    attended_rows = from_heads(attended.astype(jnp.bfloat16))
    attended_all = spread_rows(attended_rows)
    out_low = out_weight.astype(jnp.bfloat16)

    def out_term(row_start, row_count):
        return jnp.dot(attended_all, out_low, preferred_element_type=jnp.float32)

    middle = stream + sum_cols(out_term, token_total // col_devices)
    second, second_scaled, second_inverse = norm_forward(middle, norm_params[2], norm_params[3])
    second_low = second.astype(jnp.bfloat16)
    second_all = spread_cols(second_low)
    slot_rows = second_all[mine_token] * mine_used
    up_low = up_weight.astype(jnp.bfloat16)
    down_low = down_weight.astype(jnp.bfloat16)

    def up_term(row_start, row_count):
        return jnp.einsum(
            "ced,edf->cef", slot_rows, up_low, preferred_element_type=jnp.float32
        ).reshape(row_count, -1)

    hidden_pre = sum_rows(up_term, slot_share)
    hidden_low = gelu_tanh(hidden_pre).astype(jnp.bfloat16)
    hidden_all = spread_rows(hidden_low).reshape(capacity, experts_here, -1)
    expert_out = jnp.einsum(
        "cef,edf->ced", hidden_all, down_low, preferred_element_type=jnp.float32
    ).reshape(capacity * experts_here, -1)

    def combine_term(row_start, row_count):
        return jnp.sum(expert_out[pick_local] * (gate_rows * pick_owned)[:, :, None], axis=1)

    result = middle + sum_cols(combine_term, token_total // col_devices)
    valid_rows = valid_mask.astype(jnp.float32)[:, None]
    mismatch = result - teacher_block.astype(jnp.float32)
    square_sum, valid_sum = lax.psum(
        (jnp.sum(valid_rows * mismatch * mismatch), jnp.sum(valid_mask.astype(jnp.float32))),
        ("row", "col"),
    )
    valid_total = valid_sum / row_devices
    loss_value = square_sum / valid_total
    grad_out = cot_block.astype(jnp.float32) + 2.0 / valid_total * valid_rows * mismatch
    grad_all = spread_cols(grad_out.astype(jnp.bfloat16))
    grad_slots = (grad_all[mine_token] * mine_gate).astype(jnp.bfloat16)

    def hidden_term(row_start, row_count):
        return jnp.einsum(
            "ced,edf->cef", grad_slots, down_low, preferred_element_type=jnp.float32
        ).reshape(row_count, -1)

    grad_hidden = sum_rows(hidden_term, slot_share)
    gelu_value, gelu_pull = jax.vjp(gelu_tanh, hidden_pre)
    grad_pre = gelu_pull(grad_hidden)[0].astype(jnp.bfloat16)
    grad_pre_all = spread_rows(grad_pre).reshape(capacity, experts_here, -1)
    up_grad = jnp.einsum(
        "ced,cef->edf", slot_rows, grad_pre_all, preferred_element_type=jnp.float32
    )
    down_grad = jnp.einsum(
        "ced,cef->edf", grad_slots, hidden_all, preferred_element_type=jnp.float32
    )
    slot_input_grad = jnp.einsum(
        "cef,edf->ced", grad_pre_all, up_low, preferred_element_type=jnp.float32
    ).reshape(capacity * experts_here, -1)

    def back_combine(row_start, row_count):
        return jnp.sum(slot_input_grad[pick_local] * pick_owned[:, :, None], axis=1)

    grad_second = sum_cols(back_combine, token_total // col_devices)
    grad_middle_norm, second_gain_grad, second_shift_grad = norm_backward(
        grad_second, second_scaled, second_inverse, norm_params[2]
    )
    grad_middle = grad_out + grad_middle_norm
    grad_branch_all = spread_cols(grad_middle.astype(jnp.bfloat16))
    out_grad = jnp.einsum(
        "ti,to->io", attended_all, grad_branch_all, preferred_element_type=jnp.float32
    )

    def attended_term(row_start, row_count):
        return jnp.einsum("to,io->ti", grad_branch_all, out_low, preferred_element_type=jnp.float32)

    grad_attended = sum_rows(attended_term, token_total // row_devices)
    grad_packed = attend_back(packed, log_norm, to_heads(grad_attended.astype(jnp.bfloat16)))
    grad_proj_rows = from_heads(grad_packed.astype(jnp.bfloat16))
    grad_proj_all = spread_rows(grad_proj_rows)
    qkv_grad = jnp.einsum(
        "ti,to->io", normed_all, grad_proj_all, preferred_element_type=jnp.float32
    )

    def input_term(row_start, row_count):
        return jnp.einsum("to,io->ti", grad_proj_all, qkv_low, preferred_element_type=jnp.float32)

    grad_normed = sum_cols(input_term, token_total // col_devices)
    grad_stream_norm, first_gain_grad, first_shift_grad = norm_backward(
        grad_normed, normed_scaled, normed_inverse, norm_params[0]
    )
    input_block = grad_middle + grad_stream_norm
    norm_grad = lax.psum(
        jnp.stack([first_gain_grad, first_shift_grad, second_gain_grad, second_shift_grad], axis=0),
        "col",
    )
    mixed_block = result.astype(jnp.bfloat16).astype(jnp.float32)
    mixed_rows, input_grad = (
        lax.all_to_all(
            mixed_block.astype(jnp.bfloat16), "row", split_axis=0, concat_axis=1, tiled=True
        ).astype(mixed_block.dtype),
        lax.all_to_all(
            input_block.astype(jnp.bfloat16), "row", split_axis=0, concat_axis=1, tiled=True
        ).astype(input_block.dtype),
    )
    mixed_out = mixed_rows.astype(jnp.bfloat16)
    norm_one, norm_two, norm_new = adam_update(
        norm_params, norm_first, norm_second, norm_grad, rate_norm, 0.0
    )
    qkv_one, qkv_two, qkv_new = adam_update(
        qkv_weight, qkv_first, qkv_second, qkv_grad, rate_qkv, decay_matrix
    )
    out_one, out_two, out_new = adam_update(
        out_weight, out_first, out_second, out_grad, rate_out, decay_matrix
    )
    up_one, up_two, up_new = adam_update(
        up_weight, up_first, up_second, up_grad, rate_up, decay_matrix
    )
    down_one, down_two, down_new = adam_update(
        down_weight, down_first, down_second, down_grad, rate_down, decay_matrix
    )
    return (
        mixed_out,
        input_grad,
        loss_value,
        norm_one,
        norm_two,
        norm_new,
        qkv_one,
        qkv_two,
        qkv_new,
        out_one,
        out_two,
        out_new,
        up_one,
        up_two,
        up_new,
        down_one,
        down_two,
        down_new,
    )


def round_up(value, unit):
    return -(-value // unit) * unit


def mxu(lhs, rhs):
    return jnp.dot(lhs, rhs, preferred_element_type=jnp.float32)


def mxu_nt(lhs, rhs):
    return lax.dot_general(lhs, rhs, (((1,), (1,)), ((), ())), preferred_element_type=jnp.float32)


def mxu_tn(lhs, rhs):
    return lax.dot_general(lhs, rhs, (((0,), (0,)), ((), ())), preferred_element_type=jnp.float32)


def low(values):
    return values.astype(jnp.bfloat16)


def kernel_params(**more):
    return pltpu.CompilerParams(vmem_limit_bytes=VMEM_BYTES, **more)


def cost(micros):
    return pl.CostEstimate(
        flops=int(1.1e9 * micros), bytes_accessed=int(3.5e6 * micros), transcendentals=0
    )


def iota(shape, dim):
    return lax.broadcasted_iota(jnp.int32, shape, dim)


def strict(size, lower):
    row = iota((size, size), 0)
    col = iota((size, size), 1)
    return low(((col < row) if lower else (row < col)).astype(jnp.float32))


def column_sums(matrix, column):
    return mxu(matrix, low(jnp.broadcast_to(column, (column.shape[0], 128))))[:, 0:1]


def route_kernel(
    cap, block, tokens, chunk, mine_ref, all_ref, own_ref, extra_ref, order_ref,
    rows_ref, cols_ref, pick_ref, excess_ref,
):
    spare = block - 1
    padded = own_ref.shape[1]
    expert_ids = iota((EXPERTS, padded), 0)
    before = strict(padded, False)
    first = own_ref[0:1, :]
    second = own_ref[1:2, :]
    first_hot = (expert_ids == first).astype(jnp.float32)
    second_hot = (expert_ids == second).astype(jnp.float32)
    first_rank = jnp.sum(first_hot * mxu(low(first_hot), before), axis=0, keepdims=True)
    first_load = jnp.sum(first_hot, axis=1, keepdims=True)
    second_rank = jnp.sum(
        second_hot * (mxu(low(second_hot), before) + first_load), axis=0, keepdims=True
    )
    own_over = jnp.maximum(first_load + jnp.sum(second_hot, axis=1, keepdims=True) - cap, 0.0)
    own_base = column_sums(strict(EXPERTS, True), own_over)

    def slot_of(expert, rank, hot):
        extra = jnp.sum(hot * own_base, axis=0, keepdims=True) + rank - cap
        last = jnp.where(extra < spare, EXPERTS * cap + extra, -1.0)
        slot = jnp.where(rank < cap, expert.astype(jnp.float32) * cap + rank, last)
        return jnp.where(expert >= 0, slot, -1.0)

    row = iota((8, padded), 0)
    table = jnp.where(
        row == 0,
        slot_of(first, first_rank, first_hot),
        jnp.where(row == 1, slot_of(second, second_rank, second_hot), extra_ref[...]),
    )
    rows_ref[...] = table
    cols_ref[...] = jnp.transpose(table)

    devices = order_ref.shape[1]
    length = all_ref.shape[1]
    owner = iota((devices, chunk), 0) * tokens
    place = iota((devices, chunk), 1)
    chunk_ids = iota((EXPERTS, chunk), 0)

    def add_chunk(step, total):
        start = step * chunk
        part = all_ref[:, pl.ds(pl.multiple_of(start, chunk), chunk)]
        hot = (chunk_ids == part[0:1, :]).astype(jnp.float32) + (chunk_ids == part[1:2, :]).astype(
            jnp.float32
        )
        position = place + start
        member = ((position >= owner) & (position < owner + tokens)).astype(jnp.float32)
        return total + mxu_nt(low(member), low(hot))

    loads = lax.fori_loop(
        0, length // chunk, add_chunk, jnp.zeros((devices, EXPERTS), jnp.float32)
    )
    over = jnp.maximum(loads - cap, 0.0)
    room = pick_ref.shape[0]
    by_device = jnp.max(jnp.sum(over, axis=1, keepdims=True), axis=0, keepdims=True) - spare
    by_expert = jnp.max(jnp.sum(over, axis=0, keepdims=True), axis=1, keepdims=True) - room
    excess_ref[...] = jnp.broadcast_to(jnp.maximum(by_device, by_expert), excess_ref.shape)
    turned = low((iota((devices, devices), 0) == order_ref[...]).astype(jnp.float32))
    over = mxu(turned, low(jnp.minimum(over, 256.0)))
    base = mxu(low(over), strict(EXPERTS, False))
    mine = iota((devices, EXPERTS), 1) == mine_ref[0]
    over_mine = jnp.sum(jnp.where(mine, over, 0.0), axis=1, keepdims=True)
    base_mine = jnp.sum(jnp.where(mine, base, 0.0), axis=1, keepdims=True)
    start_mine = column_sums(strict(devices, True), over_mine)
    width = min(1024, devices * block)
    for part in range(devices * block // width):
        inner = iota((devices, width), 1) + part * width - iota((devices, width), 0) * block
        inside = (inner >= 0) & (inner < spare)

        def spread(column):
            return jnp.sum(jnp.where(inside, column, 0.0), axis=0, keepdims=True)

        offset = spread(inner.astype(jnp.float32) - base_mine)
        used = (offset >= 0.0) & (offset < spread(over_mine))
        target = jnp.where(used, offset + spread(start_mine), -1.0)
        pick_ref[:, part * width : (part + 1) * width] = low(
            (iota((room, width), 0).astype(jnp.float32) == target).astype(jnp.float32)
        )


def route_call(cap, spare, room, tokens, mine, all_routes, own_routes, extra, order):
    padded = own_routes.shape[1]
    devices = order.shape[1]
    spec = pl.BlockSpec(memory_space=pltpu.VMEM)
    return pl.pallas_call(
        functools.partial(route_kernel, cap, spare, tokens, 2048),
        in_specs=[pl.BlockSpec(memory_space=pltpu.SMEM)] + [spec] * 4,
        out_shape=(
            jax.ShapeDtypeStruct((8, padded), jnp.float32),
            jax.ShapeDtypeStruct((padded, 8), jnp.float32),
            jax.ShapeDtypeStruct((room, devices * spare), jnp.bfloat16),
            jax.ShapeDtypeStruct((8, 128), jnp.float32),
        ),
        compiler_params=kernel_params(),
        cost_estimate=cost(4),
        name="route",
    )(mine, all_routes, own_routes, extra, order)


def norm_stats(stream):
    center = jnp.mean(stream, axis=1, keepdims=True)
    offset = stream - center
    spread = jnp.mean(offset * offset, axis=1, keepdims=True)
    inverse = lax.rsqrt(spread + norm_eps)
    return offset * inverse, inverse


def norm_pull(upstream, scaled, inverse, gain_row):
    dscaled = upstream * gain_row
    plain = jnp.mean(dscaled, axis=1, keepdims=True)
    cross = jnp.mean(dscaled * scaled, axis=1, keepdims=True)
    return (dscaled - plain - scaled * cross) * inverse


def half_mask(shape, half):
    lane = iota(shape, 1)
    return (lane < HEAD_DIM) if half == 0 else (lane >= HEAD_DIM)


def pick_half(tile, half):
    return jnp.where(half_mask(tile.shape, half), tile, jnp.zeros_like(tile))


def unpack_block(block, col, row, cols, rows, qkv_ref, out_ref, norm_ref):
    width = norm_ref.shape[1]
    deep = width // rows
    qkv_rows = 3 * width // cols
    out_rows = width // cols
    lanes = pl.ds(row * deep, deep)
    qkv_ref[pl.ds(col * qkv_rows, qkv_rows), lanes] = block[0:qkv_rows, :]
    out_ref[pl.ds(col * out_rows, out_rows), lanes] = block[qkv_rows : qkv_rows + out_rows, :]
    tail = block[qkv_rows + out_rows : qkv_rows + out_rows + 16, :].astype(jnp.float32)
    if col == 0:
        norm_ref[0:4, lanes] = tail[0:4] + tail[4:8] + tail[8:12]
    return tail[12:13, 0:1] * 256.0 + tail[13:14, 0:1] if row == 0 else None


def one_hot(slot_cols, slots, start=0):
    place = (iota((slot_cols[0].shape[0], slots), 1) + start).astype(jnp.float32)
    hot = place == slot_cols[0]
    for column in slot_cols[1:]:
        hot = hot | (place == column)
    return low(hot.astype(jnp.float32))


def collect(slot_cols, recv_ref, extra_ref):
    slots = recv_ref.shape[0]
    return mxu(one_hot(slot_cols, slots), recv_ref[...]) + mxu(
        one_hot(slot_cols, extra_ref.shape[0], slots), extra_ref[...]
    )


def front_kernel(
    cols,
    rows,
    order_ref,
    x_ref,
    pack_ref,
    table_ref,
    send_ref,
    extra_ref,
    middle_ref,
    proj_ref,
    att_ref,
    lse_ref,
    qkv_ref,
    out_ref,
    norm_ref,
):
    width = x_ref.shape[1]
    images = x_ref.shape[0] // IMG_PAD
    norm_ref[...] = jnp.zeros_like(norm_ref)
    valid = jnp.zeros((1, 1), jnp.float32)
    for col in range(cols):
        for row in range(rows):
            block = pack_ref[order_ref[col * rows + row]]
            found = unpack_block(block, col, row, cols, rows, qkv_ref, out_ref, norm_ref)
            if found is not None:
                valid = valid + found
    norm_ref[4:5, :] = jnp.broadcast_to(valid, (1, width))
    stream = x_ref[...].astype(jnp.float32)
    scaled, _ = norm_stats(stream)
    normed = low(scaled * norm_ref[0:1, :] + norm_ref[1:2, :])
    proj_ref[...] = low(mxu_nt(normed, qkv_ref[...]))
    key_ok = iota((IMG_PAD, IMG_PAD), 0) < IMG_LEN
    for image in range(images):
        span = slice(image * IMG_PAD, (image + 1) * IMG_PAD)
        for pair in range(HEADS // 2):
            lanes = slice(pair * 128, (pair + 1) * 128)
            queries = proj_ref[span, lanes]
            keys = proj_ref[span, width + pair * 128 : width + (pair + 1) * 128]
            values_t = jnp.transpose(
                proj_ref[span, 2 * width + pair * 128 : 2 * width + (pair + 1) * 128]
            )
            mixed = []
            for half in range(2):
                scores = mxu_nt(pick_half(keys, half), queries) * HEAD_DIM**-0.5
                scores = jnp.where(key_ok, scores, -1e30)
                top = jnp.max(scores, axis=0, keepdims=True)
                shifted = jnp.exp(scores - top)
                total = jnp.sum(shifted, axis=0, keepdims=True)
                probs = low(shifted * (1.0 / total))
                head = image * HEADS + pair * 2 + half
                lse_ref[head : head + 1, :] = top + jnp.log(total)
                mixed.append(mxu(values_t[half * HEAD_DIM : (half + 1) * HEAD_DIM, :], probs))
            att_ref[span, lanes] = low(jnp.transpose(jnp.concatenate(mixed, axis=0)))
    middle = stream + mxu(att_ref[...], out_ref[...])
    middle_ref[...] = middle
    scaled_two, _ = norm_stats(middle)
    second = low(scaled_two * norm_ref[2:3, :] + norm_ref[3:4, :])
    for start, size, result in slot_parts(send_ref, extra_ref):
        place = (iota((size, table_ref.shape[1]), 0) + start).astype(jnp.float32)
        hot = (place == table_ref[0:1, :]) | (place == table_ref[1:2, :])
        result[...] = low(mxu(low(hot.astype(jnp.float32)), second))


def slot_parts(send_ref, extra_ref):
    slots = send_ref.shape[0]
    size = min(512, slots)
    parts = [(start, size, send_ref.at[start : start + size]) for start in range(0, slots, size)]
    return parts + [(slots, extra_ref.shape[0], extra_ref)]


def front_call(cols, rows, slots, spare, order, x_pad, pack, table):
    tokens, width = x_pad.shape
    images = tokens // IMG_PAD
    spec = pl.BlockSpec(memory_space=pltpu.VMEM)
    return pl.pallas_call(
        functools.partial(front_kernel, cols, rows),
        in_specs=[pl.BlockSpec(memory_space=pltpu.SMEM), spec, spec, spec],
        out_shape=(
            jax.ShapeDtypeStruct((slots, width), jnp.bfloat16),
            jax.ShapeDtypeStruct((spare, width), jnp.bfloat16),
            jax.ShapeDtypeStruct((tokens, width), jnp.float32),
            jax.ShapeDtypeStruct((tokens, 3 * width), jnp.bfloat16),
            jax.ShapeDtypeStruct((tokens, width), jnp.bfloat16),
            jax.ShapeDtypeStruct((images * HEADS, IMG_PAD), jnp.float32),
            jax.ShapeDtypeStruct((3 * width, width), jnp.bfloat16),
            jax.ShapeDtypeStruct((width, width), jnp.bfloat16),
            jax.ShapeDtypeStruct((8, width), jnp.float32),
        ),
        compiler_params=kernel_params(),
        cost_estimate=cost(12),
        name="front",
    )(order, x_pad, pack, table)


def weight_copies(row_ref, piece_refs, buffer, sems):
    deep = piece_refs[0].shape[0]
    return [
        pltpu.make_async_copy(
            piece,
            buffer.at[pl.ds(pl.multiple_of(row_ref[index] * deep, deep), deep), :],
            sems.at[index],
        )
        for index, piece in enumerate(piece_refs)
    ]


GELU_A = 0.7978845608028654
GELU_B = 0.044715


def gelu_low(pre):
    inner = pre * (GELU_A + GELU_A * GELU_B * (pre * pre))
    half = 0.5 * pre
    return low(half + half * jnp.tanh(inner))


def gelu_both(pre):
    square = pre * pre
    curve = jnp.tanh(pre * (GELU_A + GELU_A * GELU_B * square))
    half = 0.5 * pre
    value = half + half * curve
    slope = 0.5 + 0.5 * curve + half * (1.0 - curve * curve) * (
        GELU_A + 3.0 * GELU_A * GELU_B * square
    )
    return low(value), low(slope)


def ff_chunks(width):
    size = min(width, 512)
    return [slice(start, start + size) for start in range(0, width, size)]


def row_blocks(rows):
    size = 384 if rows % 384 == 0 else 128
    return [slice(start, start + size) for start in range(0, rows, size)]


def spare_chunks(rows):
    size = min(rows, 1024)
    return [slice(start, start + size) for start in range(0, rows, size)]


def start_weights(row_ref, ups, downs, up_buf, down_buf, up_sems, down_sems):
    copies = weight_copies(row_ref, ups, up_buf, up_sems)
    copies += weight_copies(row_ref, downs, down_buf, down_sems)
    for copy in copies:
        copy.start()
    return copies


def pick_rows(pick_ref, extra_ref):
    total = None
    for part in spare_chunks(extra_ref.shape[0]):
        term = mxu(pick_ref[:, part], extra_ref[part, :])
        total = term if total is None else total + term
    return low(total)


def place_rows(pick_ref, rows, back_ref):
    for part in spare_chunks(back_ref.shape[0]):
        back_ref[part, :] = low(mxu_tn(pick_ref[:, part], rows))


def take_rows(rows_ref, main_ref, extra_ref, pick_ref):
    main = main_ref.shape[0]
    rows_ref[0:main, :] = main_ref[...]
    rows_ref[main:, :] = pick_rows(pick_ref, extra_ref)


def give_rows(total_buf, send_ref, back_ref, pick_ref):
    main = send_ref.shape[0]
    send_ref[...] = total_buf[0:main, :]
    place_rows(pick_ref, total_buf[main:, :], back_ref)


def expert_kernel(pieces, row_ref, main_ref, extra_ref, pick_ref, *rest):
    send_ref, back_ref, rows_ref, total_buf, *buffers = rest[2 * pieces :]
    copies = start_weights(row_ref, rest[:pieces], rest[pieces : 2 * pieces], *buffers)
    take_rows(rows_ref, main_ref, extra_ref, pick_ref)
    for copy in copies:
        copy.wait()
    up_buf, down_buf = buffers[0:2]
    for rows in row_blocks(rows_ref.shape[0]):
        rows_in = rows_ref[rows, :]
        total = None
        for part in ff_chunks(up_buf.shape[1]):
            hidden = gelu_low(mxu(rows_in, up_buf[:, part]))
            term = mxu_nt(hidden, down_buf[:, part])
            total = term if total is None else total + term
        total_buf[rows, :] = low(total)
    give_rows(total_buf, send_ref, back_ref, pick_ref)


def pull_rows(grads_in, slope_ref, rows, up_buf, down_buf, pre_ref):
    total = None
    for part in ff_chunks(up_buf.shape[1]):
        slope = slope_ref[rows, part].astype(jnp.float32)
        grad_pre = low(mxu(grads_in, down_buf[:, part]) * slope)
        pre_ref[rows, part] = grad_pre
        term = mxu_nt(grad_pre, up_buf[:, part])
        total = term if total is None else total + term
    return low(total)


def pull_kernel(pieces, row_ref, main_ref, extra_ref, pick_ref, slope_ref, *rest):
    send_ref, back_ref, rows_ref, pre_ref, total_buf, *buffers = rest[2 * pieces :]
    copies = start_weights(row_ref, rest[:pieces], rest[pieces : 2 * pieces], *buffers)
    take_rows(rows_ref, main_ref, extra_ref, pick_ref)
    for copy in copies:
        copy.wait()
    for rows in row_blocks(rows_ref.shape[0]):
        total_buf[rows, :] = pull_rows(
            rows_ref[rows, :], slope_ref, rows, buffers[0], buffers[1], pre_ref
        )
    give_rows(total_buf, send_ref, back_ref, pick_ref)


def expert_call(kernel_fn, name, rowpos, main, extra, pick, more, ups, downs):
    slots, width = main.shape
    ff = ups[0].shape[1]
    rows = slots + pick.shape[0]
    vmem = pl.BlockSpec(memory_space=pltpu.VMEM)
    inputs = [main, extra, pick, *more]
    outs = [(slots, width), extra.shape, (rows, width)] + [(rows, ff)] * len(more)
    return pl.pallas_call(
        functools.partial(kernel_fn, len(ups)),
        in_specs=[pl.BlockSpec(memory_space=pltpu.SMEM)]
        + [vmem] * len(inputs)
        + [pl.BlockSpec(memory_space=pl.ANY)] * (2 * len(ups)),
        out_shape=[jax.ShapeDtypeStruct(shape, jnp.bfloat16) for shape in outs],
        scratch_shapes=[pltpu.VMEM((rows, width), jnp.bfloat16)]
        + [pltpu.VMEM((width, ff), jnp.bfloat16)] * 2
        + [pltpu.SemaphoreType.DMA((len(ups),))] * 2,
        compiler_params=kernel_params(),
        cost_estimate=cost(12),
        name=name,
    )(rowpos, *inputs, *ups, *downs)


def hidden_kernel(pieces, row_ref, rows_ref, *rest):
    ups = rest[:pieces]
    hidden_ref, slope_ref, up_buf, sems = rest[pieces:]

    @pl.when(pl.program_id(0) == 0)
    def _():
        copies = weight_copies(row_ref, ups, up_buf, sems)
        for copy in copies:
            copy.start()
        for copy in copies:
            copy.wait()

    rows_in = rows_ref[...]
    for part in ff_chunks(up_buf.shape[1]):
        hidden, slope = gelu_both(mxu(rows_in, up_buf[:, part]))
        hidden_ref[:, part] = hidden
        slope_ref[:, part] = slope


def hidden_call(rowpos, slot_rows, ups):
    rows, width = slot_rows.shape
    ff = ups[0].shape[1]
    block = 384 if rows % 384 == 0 else 128
    wide = pl.BlockSpec((block, ff), lambda i: (i, 0))
    return pl.pallas_call(
        functools.partial(hidden_kernel, len(ups)),
        grid=(rows // block,),
        in_specs=[
            pl.BlockSpec(memory_space=pltpu.SMEM),
            pl.BlockSpec((block, width), lambda i: (i, 0)),
        ]
        + [pl.BlockSpec(memory_space=pl.ANY)] * len(ups),
        out_specs=[wide, wide],
        out_shape=[jax.ShapeDtypeStruct((rows, ff), jnp.bfloat16)] * 2,
        scratch_shapes=[
            pltpu.VMEM((width, ff), jnp.bfloat16),
            pltpu.SemaphoreType.DMA((len(ups),)),
        ],
        compiler_params=kernel_params(dimension_semantics=("arbitrary",)),
        cost_estimate=cost(11),
        name="hidden",
    )(rowpos, slot_rows, *ups)


def weight_grad_kernel(pieces, row_ref, x_ref, pre_ref, g_ref, hidden_ref, *rest):
    ups, downs = rest[:pieces], rest[pieces : 2 * pieces]
    x_buf, g_buf, total_buf = rest[2 * pieces :]
    deep = ups[0].shape[0]

    @pl.when(pl.program_id(0) == 0)
    def _():
        x_buf[...] = jnp.transpose(x_ref[...])
        g_buf[...] = jnp.transpose(g_ref[...])

    for left, right, results in ((x_buf, pre_ref, ups), (g_buf, hidden_ref, downs)):
        total_buf[...] = low(mxu(left[...], right[...]))
        for index, result in enumerate(results):
            start = pl.multiple_of(row_ref[index] * deep, deep)
            result[...] = total_buf[pl.ds(start, deep), :]


def weight_grad_call(rowpos, slots_in, grad_pre, grad_slots, hidden, deep):
    rows, width = slots_in.shape
    ff = hidden.shape[1]
    pieces = width // deep
    part = min(ff, 512)
    narrow = pl.BlockSpec((rows, width), lambda i: (0, 0))
    wide = pl.BlockSpec((rows, part), lambda i: (0, i))
    result = pl.BlockSpec((deep, part), lambda i: (0, i))
    outs = pl.pallas_call(
        functools.partial(weight_grad_kernel, pieces),
        grid=(ff // part,),
        in_specs=[pl.BlockSpec(memory_space=pltpu.SMEM), narrow, wide, narrow, wide],
        out_specs=[result] * (2 * pieces),
        out_shape=[jax.ShapeDtypeStruct((deep, ff), jnp.bfloat16)] * (2 * pieces),
        scratch_shapes=[pltpu.VMEM((width, rows), jnp.bfloat16)] * 2
        + [pltpu.VMEM((width, part), jnp.bfloat16)],
        compiler_params=kernel_params(dimension_semantics=("arbitrary",)),
        cost_estimate=cost(10),
        name="weight_grad",
    )(rowpos, slots_in, grad_pre, grad_slots, hidden)
    return list(outs[:pieces]), list(outs[pieces:])


def turn_kernel(
    recv_ref, back_ref, cols_ref, table_ref, middle_ref, teacher_ref, cot_ref, norm_ref,
    send_ref, extra_ref, mixed_ref, grad_ref,
):
    first = collect([cols_ref[:, 0:1]], recv_ref, back_ref)
    second = collect([cols_ref[:, 1:2]], recv_ref, back_ref)
    result = middle_ref[...] + cols_ref[:, 2:3] * first + cols_ref[:, 3:4] * second
    mixed_ref[...] = low(result)
    mismatch = result - teacher_ref[...].astype(jnp.float32)
    masked = cols_ref[:, 4:5] * mismatch
    valid_total = norm_ref[4:5, :]
    squares = jnp.sum(masked * mismatch, axis=0, keepdims=True)
    square_sum = jnp.sum(squares, axis=1, keepdims=True)
    grad_out = cot_ref[...].astype(jnp.float32) + (2.0 / valid_total) * masked
    grad_ref[...] = grad_out
    rounded = low(grad_out).astype(jnp.float32)
    both = jnp.concatenate(
        [low(cols_ref[:, 2:3] * rounded), low(cols_ref[:, 3:4] * rounded)], axis=0
    )
    for start, size, part in slot_parts(send_ref, extra_ref):
        place = (iota((size, table_ref.shape[1]), 0) + start).astype(jnp.float32)
        hot = jnp.concatenate(
            [
                low((place == table_ref[0:1, :]).astype(jnp.float32)),
                low((place == table_ref[1:2, :]).astype(jnp.float32)),
            ],
            axis=1,
        )
        rows = mxu(hot, both)
        if part is extra_ref:
            top = low(square_sum).astype(jnp.float32)
            rest = square_sum - top
            middle = low(rest).astype(jnp.float32)
            lane = iota(rows.shape, 1)
            split = jnp.where(lane == 0, top, jnp.where(lane == 1, middle, rest - middle))
            split = jnp.where(lane < 3, split, 0.0)
            rows = jnp.where(iota(rows.shape, 0) == size - 1, split, rows)
        part[...] = low(rows)


def turn_call(recv, back, cols, table, middle, teacher, cot, norms):
    slots, width = recv.shape
    tokens = middle.shape[0]
    return pl.pallas_call(
        turn_kernel,
        out_shape=(
            jax.ShapeDtypeStruct((slots, width), jnp.bfloat16),
            jax.ShapeDtypeStruct(back.shape, jnp.bfloat16),
            jax.ShapeDtypeStruct((tokens, width), jnp.bfloat16),
            jax.ShapeDtypeStruct((tokens, width), jnp.float32),
        ),
        compiler_params=kernel_params(),
        cost_estimate=cost(6),
        name="turn",
    )(recv, back, cols, table, middle, teacher, cot, norms)


def back_kernel(
    cols_n,
    rows_n,
    order_ref,
    recv_ref,
    back_ref,
    cols_ref,
    x_ref,
    middle_ref,
    grad_ref,
    proj_ref,
    att_ref,
    lse_ref,
    qkv_ref,
    out_ref,
    norm_ref,
    input_ref,
    kept_ref,
    sent_ref,
    gproj_buf,
    gatt_buf,
    gqkv_buf,
    gout_buf,
    gnorm_buf,
):
    width = recv_ref.shape[1]
    images = x_ref.shape[0] // IMG_PAD
    grad_second = collect([cols_ref[:, 0:1], cols_ref[:, 1:2]], recv_ref, back_ref)
    scaled_two, inverse_two = norm_stats(middle_ref[...])
    gnorm_buf[...] = jnp.zeros_like(gnorm_buf)
    gnorm_buf[2:3, :] = jnp.sum(grad_second * scaled_two, axis=0, keepdims=True)
    gnorm_buf[3:4, :] = jnp.sum(grad_second, axis=0, keepdims=True)
    grad_middle = grad_ref[...] + norm_pull(grad_second, scaled_two, inverse_two, norm_ref[2:3, :])
    middle_low = low(grad_middle)
    gout_buf[...] = low(mxu(jnp.transpose(att_ref[...]), middle_low))
    gatt_buf[...] = low(mxu_nt(middle_low, out_ref[...]))
    scale = HEAD_DIM**-0.5
    key_ok = iota((IMG_PAD, IMG_PAD), 0) < IMG_LEN
    for image in range(images):
        span = slice(image * IMG_PAD, (image + 1) * IMG_PAD)
        for pair in range(HEADS // 2):
            q_lanes = slice(pair * 128, (pair + 1) * 128)
            k_lanes = slice(width + pair * 128, width + (pair + 1) * 128)
            v_lanes = slice(2 * width + pair * 128, 2 * width + (pair + 1) * 128)
            queries = proj_ref[span, q_lanes]
            keys = proj_ref[span, k_lanes]
            values = proj_ref[span, v_lanes]
            upstream = gatt_buf[span, q_lanes]
            keys_t = jnp.transpose(keys)
            query_parts = []
            key_parts = []
            value_parts = []
            for half in range(2):
                head = image * HEADS + pair * 2 + half
                scores = mxu_nt(pick_half(keys, half), queries) * scale
                probs = jnp.exp(jnp.where(key_ok, scores, -1e30) - lse_ref[head : head + 1, :])
                grad_probs = mxu_nt(pick_half(values, half), upstream)
                inner = jnp.sum(probs * grad_probs, axis=0, keepdims=True)
                grad_scores = low(probs * (grad_probs - inner))
                value_parts.append(mxu(low(probs), upstream))
                key_parts.append(mxu(grad_scores, queries))
                query_parts.append(
                    mxu(keys_t[half * HEAD_DIM : (half + 1) * HEAD_DIM, :], grad_scores)
                )
            left = half_mask(key_parts[0].shape, 0)
            gproj_buf[span, q_lanes] = low(
                jnp.transpose(jnp.concatenate(query_parts, axis=0)) * scale
            )
            gproj_buf[span, k_lanes] = low(jnp.where(left, key_parts[0], key_parts[1]) * scale)
            gproj_buf[span, v_lanes] = low(jnp.where(left, value_parts[0], value_parts[1]))
    stream = x_ref[...].astype(jnp.float32)
    scaled, inverse = norm_stats(stream)
    normed = low(scaled * norm_ref[0:1, :] + norm_ref[1:2, :])
    grad_normed = mxu(gproj_buf[...], qkv_ref[...])
    gqkv_buf[...] = low(mxu(jnp.transpose(gproj_buf[...]), normed))
    gnorm_buf[0:1, :] = jnp.sum(grad_normed * scaled, axis=0, keepdims=True)
    gnorm_buf[1:2, :] = jnp.sum(grad_normed, axis=0, keepdims=True)
    input_ref[...] = grad_middle + norm_pull(grad_normed, scaled, inverse, norm_ref[0:1, :])
    deep = width // rows_n
    qkv_rows = 3 * width // cols_n
    out_rows = width // cols_n
    for col in range(cols_n):
        for row in range(rows_n):
            index = order_ref[col * rows_n + row]
            lanes = slice(row * deep, (row + 1) * deep)
            qkv_part = gqkv_buf[col * qkv_rows : (col + 1) * qkv_rows, lanes]
            out_part = gout_buf[col * out_rows : (col + 1) * out_rows, lanes]
            norm_part = low(gnorm_buf[:, lanes])
            half = kept_ref.shape[0]

            def write(result, place):
                result[place, 0:qkv_rows, :] = qkv_part
                result[place, qkv_rows : qkv_rows + out_rows, :] = out_part
                result[place, qkv_rows + out_rows : qkv_rows + out_rows + 16, :] = norm_part

            @pl.when(index < half)
            def _():
                write(kept_ref, index)

            @pl.when(index >= half)
            def _():
                write(sent_ref, index - half)


def back_call(
    cols_n, rows_n, order, recv, back, cols, x_pad, middle, grad_out, proj, att, lse, qkv, out, norms
):
    tokens, width = x_pad.shape
    blocks = cols_n * rows_n
    block_rows = 4 * width // cols_n + 16
    spec = pl.BlockSpec(memory_space=pltpu.VMEM)
    return pl.pallas_call(
        functools.partial(back_kernel, cols_n, rows_n),
        in_specs=[pl.BlockSpec(memory_space=pltpu.SMEM)] + [spec] * 12,
        out_shape=(
            jax.ShapeDtypeStruct((tokens, width), jnp.float32),
        )
        + (jax.ShapeDtypeStruct((blocks // 2, block_rows, width // rows_n), jnp.bfloat16),) * 2,
        scratch_shapes=[
            pltpu.VMEM((tokens, 3 * width), jnp.bfloat16),
            pltpu.VMEM((tokens, width), jnp.bfloat16),
            pltpu.VMEM((3 * width, width), jnp.bfloat16),
            pltpu.VMEM((width, width), jnp.bfloat16),
            pltpu.VMEM((16, width), jnp.float32),
        ],
        compiler_params=kernel_params(),
        cost_estimate=cost(14),
        name="back",
    )(order, recv, back, cols, x_pad, middle, grad_out, proj, att, lse, qkv, out, norms)


def adam_kernel(slabs, where_ref, *refs):
    up_grads, down_grads = refs[:slabs], refs[slabs : 2 * slabs]
    ins, outs = refs[2 * slabs : 2 * slabs + 6], refs[-6:]
    for index in range(slabs):

        @pl.when(pl.program_id(0) == index)
        def _():
            for rate, gradient, inputs, results in (
                (rate_up, up_grads[index], ins[0:3], outs[0:3]),
                (rate_down, down_grads[index], ins[3:6], outs[3:6]),
            ):
                first_new, second_new, weight_new = adam_update(
                    inputs[0][0],
                    inputs[1][0],
                    inputs[2][0],
                    gradient[...].astype(jnp.float32),
                    rate,
                    decay_matrix,
                )
                results[0][0] = first_new
                results[1][0] = second_new
                results[2][0] = weight_new


def adam_call(places, gradients, arrays, earlier):
    slabs = len(gradients)
    deep, ff = gradients[0][0].shape
    tile = min(deep, 64)
    tiles = deep // tile

    def gradient_spec(index):
        def where_is(slab, part, where):
            return (jnp.where(slab == index, part, jnp.where(slab < index, 0, tiles - 1)), 0)

        return pl.BlockSpec((tile, ff), where_is)

    block = pl.BlockSpec(
        (1, tile, ff), lambda slab, part, where: (where[2 * slab], part, where[2 * slab + 1])
    )
    in_specs = [gradient_spec(index) for index in range(slabs)] * 2 + [block] * 6
    aliases = {}
    if earlier is not None:
        aliases = {1 + len(in_specs) + index: index for index in range(6)}
        in_specs += [pl.BlockSpec(memory_space=pl.ANY)] * 6
    return pl.pallas_call(
        functools.partial(adam_kernel, slabs),
        grid_spec=pltpu.PrefetchScalarGridSpec(
            num_scalar_prefetch=1, grid=(slabs, tiles), in_specs=in_specs, out_specs=[block] * 6
        ),
        out_shape=[jax.ShapeDtypeStruct(arrays[0].shape, jnp.float32)] * 6,
        input_output_aliases=aliases,
        compiler_params=kernel_params(dimension_semantics=("arbitrary", "arbitrary")),
        cost_estimate=cost(6 * slabs),
        name="adam",
    )(places, *[g[0] for g in gradients], *[g[1] for g in gradients], *arrays, *(earlier or ()))


def swap(values, mask):
    rows = lax.axis_size("row")
    cols = lax.axis_size("col")

    def flat(place):
        return place % rows * cols + place // rows

    return lax.ppermute(
        values, ("row", "col"), [(flat(i), flat(i ^ mask)) for i in range(rows * cols)]
    )


def gather_steps():
    bits = []
    bit = lax.axis_size("col") * lax.axis_size("row") // 2
    while bit:
        bits.append(bit)
        bit //= 2
    return [bits[start : start + 2] for start in range(0, len(bits), 2)]


def masks_of(bits):
    return [
        sum(bit for place, bit in enumerate(bits) if index >> place & 1)
        for index in range(1, 1 << len(bits))
    ]


def late_steps():
    rows = lax.axis_size("row")
    far = [bit for bits in gather_steps() for bit in bits if 1 < bit < rows]
    wide = [bit for bits in gather_steps() for bit in bits if bit > rows]
    steps = [far, wide, [rows], [1]]
    return [bits for bits in steps if bits]


def block_order(steps):
    rows = lax.axis_size("row")
    devices = lax.axis_size("col") * rows
    differs = jnp.arange(devices, dtype=jnp.int32) ^ (
        lax.axis_index("col") * rows + lax.axis_index("row")
    )
    order = jnp.zeros((devices,), jnp.int32)
    place = 0
    for bits in steps:
        for bit in bits:
            order = order | jnp.where((differs & bit) != 0, 1 << place, 0)
            place += 1
    return order


def gather_step(gathered, bits):
    return jnp.concatenate([gathered] + [swap(gathered, mask) for mask in masks_of(bits)], axis=0)


def halves_step(kept, sent):
    return low(kept.astype(jnp.float32) + swap(sent, 1).astype(jnp.float32))


def scatter_step(blocks, bits):
    count = 1 << len(bits)
    size = blocks.shape[0] // count
    total = blocks[:size].astype(jnp.float32)
    for index, mask in enumerate(masks_of(bits)):
        sent = blocks[(index + 1) * size : (index + 2) * size]
        total = total + swap(sent, mask).astype(jnp.float32)
    return low(total)


def pad_images(values):
    tokens, width = values.shape
    images = tokens // IMG_LEN
    padded = jnp.pad(
        values.reshape(images, IMG_LEN, width), ((0, 0), (0, IMG_PAD - IMG_LEN), (0, 0))
    )
    return padded.reshape(images * IMG_PAD, width)


def crop_images(values):
    width = values.shape[1]
    return values.reshape(-1, IMG_PAD, width)[:, :IMG_LEN].reshape(-1, width)


def pad_rows(values, fill):
    images = values.shape[1] // IMG_LEN
    padded = jnp.pad(
        values.reshape(values.shape[0], images, IMG_LEN),
        ((0, 0), (0, 0), (0, IMG_PAD - IMG_LEN)),
        constant_values=fill,
    )
    return padded.reshape(values.shape[0], images * IMG_PAD)


def to_experts(main, extra, share, beside=()):
    if share > 1:
        width = main.shape[1]
        main = jnp.broadcast_to(
            main.reshape(EXPERTS, 1, -1, width),
            (EXPERTS, share, main.shape[0] // EXPERTS, width),
        ).reshape(-1, width)
    first, *others = gather_steps()
    blocks = gather_step(extra[None], first)
    main, blocks = lax.optimization_barrier((main, blocks))
    main = lax.all_to_all(main, BOTH, split_axis=0, concat_axis=0, tiled=True)
    for place, bits in enumerate(others):
        if place == len(others) - 1:
            blocks, beside = lax.optimization_barrier((blocks, beside))
        blocks = gather_step(blocks, bits)
    return main, blocks.reshape(-1, extra.shape[1]), beside


def from_experts(main, share):
    main = lax.all_to_all(main, BOTH, split_axis=0, concat_axis=0, tiled=True)
    width = main.shape[1]
    if share > 1:
        main = low(
            jnp.sum(main.reshape(EXPERTS, share, -1, width).astype(jnp.float32), axis=1)
        ).reshape(-1, width)
    return main


def spare_blocks(extra):
    devices = lax.axis_size("row") * lax.axis_size("col")
    return extra.reshape(devices, -1, extra.shape[1])


def body(*args):
    (
        x_in,
        cotangent,
        teacher,
        valid_mask,
        routes,
        gate_weights,
        norm_params,
        qkv_weight,
        out_weight,
        up_weight,
        down_weight,
        norm_first,
        norm_second,
        qkv_first,
        qkv_second,
        out_first,
        out_second,
        up_first,
        up_second,
        down_first,
        down_second,
    ) = args
    rows_n = lax.axis_size("row")
    cols_n = lax.axis_size("col")
    devices = rows_n * cols_n
    my_row = lax.axis_index("row")
    me = lax.axis_index("col") * rows_n + my_row
    tokens, width = x_in.shape
    token_total = routes.shape[1]
    experts_here, deep, ff = up_weight.shape
    share = rows_n // experts_here
    ff_here = ff // share
    mean_load = TOP * tokens / EXPERTS
    cap = max(16, 16 * round(1.3 * mean_load / 16))
    slots = EXPERTS * cap
    spare = 32
    room = 4 * devices

    def three_parts(values):
        top = lax.reduce_precision(values, 8, 7)
        rest = values - top
        middle_part = lax.reduce_precision(rest, 8, 7)
        return [low(top), low(middle_part), low(rest - middle_part)]

    count = jnp.sum(valid_mask)
    count_rows = low(
        jnp.broadcast_to(
            jnp.stack([count // 256, count % 256, count * 0, count * 0]).astype(jnp.float32)[:, None],
            (4, deep),
        )
    )
    small = jnp.concatenate(
        [low(jnp.transpose(qkv_weight)), low(out_weight), *three_parts(norm_params), count_rows],
        axis=0,
    )
    order = block_order(gather_steps())

    partners = [my_row ^ index for index in range(rows_n)]
    rowpos = jnp.stack(partners).astype(jnp.int32)

    def slab(values, partner):
        return low(
            lax.dynamic_slice(
                values, (partner // share, 0, partner % share * ff_here), (1, deep, ff_here)
            )[0]
        )

    far = rows_n // 2
    first_step, second_step, *last_steps = gather_steps()
    pack = gather_step(small[None], first_step)
    far_ones = [index for index in range(2, rows_n)] or [1]
    first_far = far_ones[0]
    early = swap(slab(up_weight, partners[first_far]), first_far)
    arrived = [swap(pack, mask) for mask in masks_of(second_step)]
    held = (routes, gate_weights, valid_mask, x_in, up_weight, down_weight)
    arrived[0], held = lax.optimization_barrier((arrived[0], held))
    pack = jnp.concatenate([pack] + arrived, axis=0)
    pack, early = lax.optimization_barrier((pack, early))

    start = me * tokens
    own_routes = pad_rows(lax.dynamic_slice_in_dim(held[0], start, tokens, 1), -1)
    own_gates = pad_rows(lax.dynamic_slice_in_dim(held[1], start, tokens, 1), 0)
    own_mask = pad_rows(
        lax.dynamic_slice_in_dim(held[2], my_row * tokens, tokens, 0)[None], 0
    ).astype(jnp.float32)
    padded = own_routes.shape[1]
    extra = jnp.concatenate(
        [jnp.zeros((2, padded), jnp.float32), own_gates, own_mask, jnp.zeros((3, padded), jnp.float32)],
        axis=0,
    )
    all_routes = jnp.pad(
        held[0], ((0, 0), (0, round_up(token_total, 2048) - token_total)), constant_values=-1
    )
    mine = (me // share).astype(jnp.int32).reshape(1)
    x_pad = pad_images(held[3])
    up_slabs = [slab(held[4], partners[index]) for index in far_ones[1:]]
    down_slabs = [slab(held[5], partners[index]) for index in far_ones]
    ups = {0: slab(held[4], partners[0]), first_far: early}
    downs = {0: slab(held[5], partners[0])}
    up_pieces = [swap(piece, index) for index, piece in zip(far_ones[1:], up_slabs)]
    for bits in last_steps:
        pack = gather_step(pack, bits)
    pack, all_routes, own_routes, extra, x_pad, down_slabs = lax.optimization_barrier(
        (pack, all_routes, own_routes, extra, x_pad, down_slabs)
    )
    table, table_cols, pick, excess = route_call(
        cap, spare, room, tokens, mine, all_routes, own_routes, extra, order[None]
    )
    overflow = excess[0, 0] > 0

    pack, up_pieces, table, down_slabs = lax.optimization_barrier(
        (pack, up_pieces, table, down_slabs)
    )
    ups.update(zip(far_ones[1:], up_pieces))
    near_up, near_down = slab(held[4], partners[1]), slab(held[5], partners[1])
    half = (len(far_ones) + 1) // 2
    for index, piece in zip(far_ones[:half], down_slabs):
        downs[index] = swap(piece, index)
    send, spare_rows, middle, proj, att, lse, qkv_all, out_all, norms = front_call(
        cols_n, rows_n, slots, spare, order, x_pad, pack, table
    )
    send, spare_rows, ups, downs, down_slabs = lax.optimization_barrier(
        (send, spare_rows, ups, downs, down_slabs)
    )
    last_downs = [
        swap(piece, index) for index, piece in zip(far_ones[half:], down_slabs[half:])
    ]
    main, extras, last_downs = to_experts(send, spare_rows, share, last_downs)
    downs.update(zip(far_ones[half:], last_downs))
    if far_ones[0] != 1:
        ups[1], downs[1] = swap(near_up, 1), swap(near_down, 1)
    ups = [ups[index] for index in range(rows_n)]
    downs = [downs[index] for index in range(rows_n)]

    main, extras, slot_rows = expert_call(
        expert_kernel, "expert", rowpos, main, extras, pick, (), ups, downs
    )
    combined = from_experts(main, share)
    hidden, slope = hidden_call(rowpos, slot_rows, ups)
    extras = spare_blocks(extras)
    *early_steps, final_step = reversed(gather_steps())
    for bits in early_steps:
        extras = scatter_step(extras, bits)
    extras, hidden, slope = lax.optimization_barrier((extras, hidden, slope))
    grad_send, grad_spare, mixed, grad_out = turn_call(
        combined,
        scatter_step(extras, final_step)[0],
        table_cols,
        table,
        middle,
        pad_images(teacher),
        pad_images(cotangent),
        norms,
    )
    main, extras, _ = to_experts(grad_send, grad_spare, share)
    errors = extras.reshape(devices, spare, width)[:, spare - 1, :3].astype(jnp.float32)
    loss_value = jnp.sum(errors[order]) / norms[4, 0]
    main, extras, grad_slots, grad_pre = expert_call(
        pull_kernel, "pull", rowpos, main, extras, pick, (slope,), ups, downs
    )
    grad_back = from_experts(main, share)
    extras = spare_blocks(extras)
    for bits in early_steps:
        extras = scatter_step(extras, bits)
    up_grads, down_grads = weight_grad_call(rowpos, slot_rows, grad_pre, grad_slots, hidden, deep)
    mixed_rows = crop_images(mixed)
    extras, up_grads, down_grads, mixed_rows, loss_value = lax.optimization_barrier(
        (extras, up_grads, down_grads, mixed_rows, loss_value)
    )
    grad_back_spare = scatter_step(extras, final_step)[0]

    arrays = (up_weight, up_first, up_second, down_weight, down_first, down_second)

    def places_of(chosen):
        return jnp.stack(
            [value for p in chosen for value in (partners[p] // share, partners[p] % share)]
        ).astype(jnp.int32)

    near = list(range(min(2, rows_n)))
    apart = list(range(2, rows_n))
    groups = [apart[: len(apart) // 2], apart[len(apart) // 2 :]]
    groups = [group for group in groups if group]
    gradients = {}
    for index in near:
        pair = (up_grads[index], down_grads[index])
        gradients[index] = tuple(swap(p, index) for p in pair) if index else pair
    if groups:
        up_far = [swap(up_grads[index], index) for index in groups[0]]
        grad_back, grad_back_spare, up_far, down_grads = lax.optimization_barrier(
            (grad_back, grad_back_spare, up_far, down_grads)
        )
        for index, piece in zip(groups[0], up_far):
            gradients[index] = (piece, swap(down_grads[index], index))

    late_order = block_order(late_steps())
    input_pad, blocks, sent_blocks = back_call(
        cols_n,
        rows_n,
        late_order,
        grad_back,
        grad_back_spare,
        table_cols,
        x_pad,
        middle,
        grad_out,
        proj,
        att,
        lse,
        qkv_all,
        out_all,
        norms,
    )
    input_rows = input_pad
    experts_new = None
    later = []
    for place, bits in enumerate(reversed(late_steps())):
        if place == 0:
            blocks = halves_step(blocks, sent_blocks)
        else:
            blocks = scatter_step(blocks, bits)
        if place == 0:
            sent = [gradients[index] for index in near + (groups[0] if groups else [])]
            blocks, sent, up_grads, down_grads, input_rows = lax.optimization_barrier(
                (blocks, sent, up_grads, down_grads, input_rows)
            )
            input_rows = crop_images(input_rows)
            experts_new = adam_call(places_of(near), sent[: len(near)], arrays, None)
            if len(groups) > 1:
                later = [
                    (swap(up_grads[index], index), swap(down_grads[index], index))
                    for index in groups[1]
                ]
        if place == 1:
            blocks, experts_new, input_rows = lax.optimization_barrier(
                (blocks, experts_new, input_rows)
            )
            if groups:
                experts_new = adam_call(places_of(groups[0]), sent[len(near) :], arrays, experts_new)
        if place == 2:
            blocks, experts_new, later = lax.optimization_barrier((blocks, experts_new, later))
    if later:
        experts_new = adam_call(places_of(groups[1]), later, arrays, experts_new)
    up_one, up_two, up_new, down_one, down_two, down_new = experts_new
    summed = blocks[0].astype(jnp.float32)
    qkv_rows = qkv_weight.shape[1]
    out_rows = out_weight.shape[0]
    qkv_one, qkv_two, qkv_new = adam_update(
        qkv_weight, qkv_first, qkv_second, jnp.transpose(summed[:qkv_rows]), rate_qkv, decay_matrix
    )
    out_one, out_two, out_new = adam_update(
        out_weight,
        out_first,
        out_second,
        summed[qkv_rows : qkv_rows + out_rows],
        rate_out,
        decay_matrix,
    )
    norm_one, norm_two, norm_new = adam_update(
        norm_params,
        norm_first,
        norm_second,
        summed[qkv_rows + out_rows : qkv_rows + out_rows + 4],
        rate_norm,
        0.0,
    )
    quick = (
        mixed_rows,
        input_rows,
        loss_value,
        norm_one,
        norm_two,
        norm_new,
        qkv_one,
        qkv_two,
        qkv_new,
        out_one,
        out_two,
        out_new,
        up_one,
        up_two,
        up_new,
        down_one,
        down_two,
        down_new,
    )

    def again(state):
        return (jnp.bool_(False), general_body(*args))

    return lax.while_loop(lambda state: state[0], again, (overflow, quick))[1]


def solution(mesh):
    in_specs = (
        P(("col", "row"), None),
        P(("col", "row"), None),
        P(("col", "row"), None),
        P("col"),
        P(),
        P(),
        P(None, "row"),
        P("row", "col"),
        P("col", "row"),
        P("col", "row", None),
        P("col", "row", None),
        P(None, "row"),
        P(None, "row"),
        P("row", "col"),
        P("row", "col"),
        P("col", "row"),
        P("col", "row"),
        P("col", "row", None),
        P("col", "row", None),
        P("col", "row", None),
        P("col", "row", None),
    )
    out_specs = (
        P(("col", "row"), None),
        P(("col", "row"), None),
        P(),
        P(None, "row"),
        P(None, "row"),
        P(None, "row"),
        P("row", "col"),
        P("row", "col"),
        P("row", "col"),
        P("col", "row"),
        P("col", "row"),
        P("col", "row"),
        P("col", "row", None),
        P("col", "row", None),
        P("col", "row", None),
        P("col", "row", None),
        P("col", "row", None),
        P("col", "row", None),
    )
    return jax.shard_map(body, mesh=mesh, in_specs=in_specs, out_specs=out_specs, check_vma=False)
```

```python
import functools

import jax
import jax.numpy as jnp
from jax import lax
from jax.experimental import pallas as pl
from jax.experimental.pallas import tpu as pltpu
from jax.sharding import PartitionSpec as P

HEADS = 8
HEAD_DIM = 64
EXPERTS = 32
TOP = 2
IMG_LEN = 197
STEP = 5
IMG_PAD = 256
BOTH = ("col", "row")
VMEM_BYTES = 56 * 1024 * 1024

norm_eps = 1e-06
beta_one = 0.9
beta_two = 0.999
adam_eps = 1e-08
decay_matrix = 0.1
rate_norm = 0.4
rate_qkv = 0.02
rate_out = 0.06
rate_up = 0.02
rate_down = 0.01


def dispatch_tables(routes, capacity):
    flat_routes = routes.reshape(-1)
    picks_total = flat_routes.shape[0]
    order_idx = jnp.argsort(flat_routes, stable=True)
    sorted_experts = flat_routes[order_idx]
    expert_ids = jnp.arange(EXPERTS, dtype=jnp.int32)
    expert_load = jnp.sum((flat_routes[:, None] == expert_ids[None, :]).astype(jnp.int32), axis=0)
    starts_at = jnp.cumsum(expert_load) - expert_load
    position = jnp.arange(picks_total, dtype=jnp.int32)
    slot_index = sorted_experts * capacity + position - starts_at[sorted_experts]
    slot_token = jnp.zeros((EXPERTS * capacity,), jnp.int32).at[slot_index].set(order_idx // TOP)
    slot_used = jnp.zeros((EXPERTS * capacity,), jnp.int32).at[slot_index].set(1)
    pick_slot = jnp.zeros((picks_total,), jnp.int32).at[order_idx].set(slot_index)
    return (slot_token, slot_used, order_idx, slot_index, pick_slot.reshape(-1, TOP))


def gelu_tanh(inner_value):
    return jax.nn.gelu(inner_value, approximate=True)


def spread_cols(values):
    return lax.all_gather(values, "col", axis=0, tiled=True)


def spread_rows(values):
    return lax.all_gather(values, "row", axis=0, tiled=True)


def sum_rows(term_fn, row_total):
    return lax.psum_scatter(
        term_fn(jnp.int32(0), row_total * lax.axis_size("row")),
        "row",
        scatter_dimension=0,
        tiled=True,
    )


def sum_cols(term_fn, row_total):
    return lax.psum_scatter(
        term_fn(jnp.int32(0), row_total * lax.axis_size("col")),
        "col",
        scatter_dimension=0,
        tiled=True,
    )


def to_heads(values):
    return lax.all_to_all(values, "col", split_axis=0, concat_axis=1, tiled=True)


def from_heads(values):
    return lax.all_to_all(values, "col", split_axis=1, concat_axis=0, tiled=True)


def token_sums(first_part, second_part):
    return lax.psum((first_part, second_part), "row")


def norm_forward(stream, gain_row, shift_row):
    full_width = stream.shape[1] * lax.axis_size("row")
    sum_plain, squares = token_sums(jnp.sum(stream, axis=1), jnp.sum(stream * stream, axis=1))
    center = sum_plain / full_width
    offset = stream - center[:, None]
    spread = squares / full_width - center * center
    inverse = lax.rsqrt(spread + norm_eps)
    scaled = offset * inverse[:, None]
    return (scaled * gain_row + shift_row, scaled, inverse)


def norm_backward(upstream, scaled, inverse, gain_row):
    full_width = scaled.shape[1] * lax.axis_size("row")
    dscaled = upstream * gain_row
    sum_plain, sum_cross = token_sums(jnp.sum(dscaled, axis=1), jnp.sum(dscaled * scaled, axis=1))
    inner_grad = (
        dscaled - (sum_plain / full_width)[:, None] - scaled * (sum_cross / full_width)[:, None]
    )
    return (
        inner_grad * inverse[:, None],
        jnp.sum(upstream * scaled, axis=0),
        jnp.sum(upstream, axis=0),
    )


def attend_local(packed):
    images = packed.shape[0] // IMG_LEN
    split_heads = packed.reshape(images, IMG_LEN, 3, HEADS, HEAD_DIM)
    scores = jnp.einsum(
        "gqhd,gkhd->ghqk",
        split_heads[:, :, 0],
        split_heads[:, :, 1],
        preferred_element_type=jnp.float32,
    ) * HEAD_DIM ** (-0.5)
    top_score = jnp.max(scores, axis=-1, keepdims=True)
    shifted = jnp.exp(scores - top_score)
    totals = jnp.sum(shifted, axis=-1, keepdims=True)
    weights = (shifted / totals).astype(jnp.bfloat16)
    log_norm = top_score + jnp.log(totals)
    mixed_heads = jnp.einsum(
        "ghqk,gkhd->gqhd", weights, split_heads[:, :, 2], preferred_element_type=jnp.float32
    )
    return (mixed_heads.reshape(images * IMG_LEN, HEADS * HEAD_DIM), log_norm)


def attend_back(packed, log_norm, upstream):
    images = packed.shape[0] // IMG_LEN
    split_heads = packed.reshape(images, IMG_LEN, 3, HEADS, HEAD_DIM)
    queries = split_heads[:, :, 0]
    key_part = split_heads[:, :, 1]
    value_part = split_heads[:, :, 2]
    grad_mixed = upstream.reshape(images, IMG_LEN, HEADS, HEAD_DIM)
    score_scale = HEAD_DIM ** (-0.5)
    scores = (
        jnp.einsum("gqhd,gkhd->ghqk", queries, key_part, preferred_element_type=jnp.float32)
        * score_scale
    )
    prob_rows = jnp.exp(scores - log_norm)
    grad_value = jnp.einsum(
        "ghqk,gqhd->gkhd",
        prob_rows.astype(jnp.bfloat16),
        grad_mixed,
        preferred_element_type=jnp.float32,
    )
    grad_probs = jnp.einsum(
        "gqhd,gkhd->ghqk", grad_mixed, value_part, preferred_element_type=jnp.float32
    )
    grad_scores = (
        prob_rows * (grad_probs - jnp.sum(prob_rows * grad_probs, axis=-1, keepdims=True))
    ).astype(jnp.bfloat16)
    grad_query = (
        jnp.einsum("ghqk,gkhd->gqhd", grad_scores, key_part, preferred_element_type=jnp.float32)
        * score_scale
    )
    grad_key = (
        jnp.einsum("ghqk,gqhd->gkhd", grad_scores, queries, preferred_element_type=jnp.float32)
        * score_scale
    )
    stacked = jnp.stack([grad_query, grad_key, grad_value], axis=2)
    return stacked.reshape(images * IMG_LEN, 3 * HEADS * HEAD_DIM)


def adam_update(weight, first_moment, second_moment, gradient, step_rate, decay_factor):
    first_new = beta_one * first_moment + (1.0 - beta_one) * gradient
    second_new = beta_two * second_moment + (1.0 - beta_two) * gradient * gradient
    first_hat = first_new / (1.0 - beta_one**STEP)
    second_hat = second_new / (1.0 - beta_two**STEP)
    weight_new = weight - step_rate * (
        first_hat / (jnp.sqrt(second_hat) + adam_eps) + decay_factor * weight
    )
    return (first_new, second_new, weight_new)


def general_body(
    x_in,
    cotangent,
    teacher,
    valid_mask,
    routes,
    gate_weights,
    norm_params,
    qkv_weight,
    out_weight,
    up_weight,
    down_weight,
    norm_first,
    norm_second,
    qkv_first,
    qkv_second,
    out_first,
    out_second,
    up_first,
    up_second,
    down_first,
    down_second,
):
    token_total = routes.shape[1]
    row_devices = lax.axis_size("row")
    col_devices = lax.axis_size("col")
    capacity = row_devices * (5 * token_total * TOP // (4 * EXPERTS) // row_devices)
    experts_here = EXPERTS // col_devices
    first_mine = lax.axis_index("col") * experts_here
    slot_share = capacity * experts_here // row_devices
    route_rows = jnp.stack([routes[k] for k in range(TOP)], axis=1)
    gate_rows = jnp.stack([gate_weights[k] for k in range(TOP)], axis=1)
    slot_token, slot_used, order_idx, slot_index, pick_slot = dispatch_tables(route_rows, capacity)
    slot_gate = (
        jnp.zeros((EXPERTS * capacity,), jnp.float32)
        .at[slot_index]
        .set(gate_rows.reshape(-1)[order_idx])
    )
    mine_token = jnp.transpose(
        lax.dynamic_slice_in_dim(slot_token.reshape(EXPERTS, capacity), first_mine, experts_here, 0)
    )
    mine_used = jnp.transpose(
        lax.dynamic_slice_in_dim(slot_used.reshape(EXPERTS, capacity), first_mine, experts_here, 0)
    ).astype(jnp.bfloat16)[:, :, None]
    mine_gate = jnp.transpose(
        lax.dynamic_slice_in_dim(slot_gate.reshape(EXPERTS, capacity), first_mine, experts_here, 0)
    )[:, :, None]
    pick_expert = pick_slot // capacity
    pick_owned = ((pick_expert >= first_mine) & (pick_expert < first_mine + experts_here)).astype(
        jnp.float32
    )
    pick_local = pick_slot % capacity * experts_here + jnp.clip(
        pick_expert - first_mine, 0, experts_here - 1
    )
    x_block, cot_block, teacher_block = (
        lax.all_to_all(x_in, "row", split_axis=1, concat_axis=0, tiled=True),
        lax.all_to_all(cotangent, "row", split_axis=1, concat_axis=0, tiled=True),
        lax.all_to_all(teacher, "row", split_axis=1, concat_axis=0, tiled=True),
    )
    stream = x_block.astype(jnp.float32)
    normed, normed_scaled, normed_inverse = norm_forward(stream, norm_params[0], norm_params[1])
    normed_low = normed.astype(jnp.bfloat16)
    normed_all = spread_cols(normed_low)
    qkv_low = qkv_weight.astype(jnp.bfloat16)

    def qkv_term(row_start, row_count):
        return jnp.dot(normed_all, qkv_low, preferred_element_type=jnp.float32)

    projected = sum_rows(qkv_term, token_total // row_devices)
    packed = to_heads(projected.astype(jnp.bfloat16))
    attended, log_norm = attend_local(packed)
    attended_rows = from_heads(attended.astype(jnp.bfloat16))
    attended_all = spread_rows(attended_rows)
    out_low = out_weight.astype(jnp.bfloat16)

    def out_term(row_start, row_count):
        return jnp.dot(attended_all, out_low, preferred_element_type=jnp.float32)

    middle = stream + sum_cols(out_term, token_total // col_devices)
    second, second_scaled, second_inverse = norm_forward(middle, norm_params[2], norm_params[3])
    second_low = second.astype(jnp.bfloat16)
    second_all = spread_cols(second_low)
    slot_rows = second_all[mine_token] * mine_used
    up_low = up_weight.astype(jnp.bfloat16)
    down_low = down_weight.astype(jnp.bfloat16)

    def up_term(row_start, row_count):
        return jnp.einsum(
            "ced,edf->cef", slot_rows, up_low, preferred_element_type=jnp.float32
        ).reshape(row_count, -1)

    hidden_pre = sum_rows(up_term, slot_share)
    hidden_low = gelu_tanh(hidden_pre).astype(jnp.bfloat16)
    hidden_all = spread_rows(hidden_low).reshape(capacity, experts_here, -1)
    expert_out = jnp.einsum(
        "cef,edf->ced", hidden_all, down_low, preferred_element_type=jnp.float32
    ).reshape(capacity * experts_here, -1)

    def combine_term(row_start, row_count):
        return jnp.sum(expert_out[pick_local] * (gate_rows * pick_owned)[:, :, None], axis=1)

    result = middle + sum_cols(combine_term, token_total // col_devices)
    valid_rows = valid_mask.astype(jnp.float32)[:, None]
    mismatch = result - teacher_block.astype(jnp.float32)
    square_sum, valid_sum = lax.psum(
        (jnp.sum(valid_rows * mismatch * mismatch), jnp.sum(valid_mask.astype(jnp.float32))),
        ("row", "col"),
    )
    valid_total = valid_sum / row_devices
    loss_value = square_sum / valid_total
    grad_out = cot_block.astype(jnp.float32) + 2.0 / valid_total * valid_rows * mismatch
    grad_all = spread_cols(grad_out.astype(jnp.bfloat16))
    grad_slots = (grad_all[mine_token] * mine_gate).astype(jnp.bfloat16)

    def hidden_term(row_start, row_count):
        return jnp.einsum(
            "ced,edf->cef", grad_slots, down_low, preferred_element_type=jnp.float32
        ).reshape(row_count, -1)

    grad_hidden = sum_rows(hidden_term, slot_share)
    gelu_value, gelu_pull = jax.vjp(gelu_tanh, hidden_pre)
    grad_pre = gelu_pull(grad_hidden)[0].astype(jnp.bfloat16)
    grad_pre_all = spread_rows(grad_pre).reshape(capacity, experts_here, -1)
    up_grad = jnp.einsum(
        "ced,cef->edf", slot_rows, grad_pre_all, preferred_element_type=jnp.float32
    )
    down_grad = jnp.einsum(
        "ced,cef->edf", grad_slots, hidden_all, preferred_element_type=jnp.float32
    )
    slot_input_grad = jnp.einsum(
        "cef,edf->ced", grad_pre_all, up_low, preferred_element_type=jnp.float32
    ).reshape(capacity * experts_here, -1)

    def back_combine(row_start, row_count):
        return jnp.sum(slot_input_grad[pick_local] * pick_owned[:, :, None], axis=1)

    grad_second = sum_cols(back_combine, token_total // col_devices)
    grad_middle_norm, second_gain_grad, second_shift_grad = norm_backward(
        grad_second, second_scaled, second_inverse, norm_params[2]
    )
    grad_middle = grad_out + grad_middle_norm
    grad_branch_all = spread_cols(grad_middle.astype(jnp.bfloat16))
    out_grad = jnp.einsum(
        "ti,to->io", attended_all, grad_branch_all, preferred_element_type=jnp.float32
    )

    def attended_term(row_start, row_count):
        return jnp.einsum("to,io->ti", grad_branch_all, out_low, preferred_element_type=jnp.float32)

    grad_attended = sum_rows(attended_term, token_total // row_devices)
    grad_packed = attend_back(packed, log_norm, to_heads(grad_attended.astype(jnp.bfloat16)))
    grad_proj_rows = from_heads(grad_packed.astype(jnp.bfloat16))
    grad_proj_all = spread_rows(grad_proj_rows)
    qkv_grad = jnp.einsum(
        "ti,to->io", normed_all, grad_proj_all, preferred_element_type=jnp.float32
    )

    def input_term(row_start, row_count):
        return jnp.einsum("to,io->ti", grad_proj_all, qkv_low, preferred_element_type=jnp.float32)

    grad_normed = sum_cols(input_term, token_total // col_devices)
    grad_stream_norm, first_gain_grad, first_shift_grad = norm_backward(
        grad_normed, normed_scaled, normed_inverse, norm_params[0]
    )
    input_block = grad_middle + grad_stream_norm
    norm_grad = lax.psum(
        jnp.stack([first_gain_grad, first_shift_grad, second_gain_grad, second_shift_grad], axis=0),
        "col",
    )
    mixed_block = result.astype(jnp.bfloat16).astype(jnp.float32)
    mixed_rows, input_grad = (
        lax.all_to_all(
            mixed_block.astype(jnp.bfloat16), "row", split_axis=0, concat_axis=1, tiled=True
        ).astype(mixed_block.dtype),
        lax.all_to_all(
            input_block.astype(jnp.bfloat16), "row", split_axis=0, concat_axis=1, tiled=True
        ).astype(input_block.dtype),
    )
    mixed_out = mixed_rows.astype(jnp.bfloat16)
    norm_one, norm_two, norm_new = adam_update(
        norm_params, norm_first, norm_second, norm_grad, rate_norm, 0.0
    )
    qkv_one, qkv_two, qkv_new = adam_update(
        qkv_weight, qkv_first, qkv_second, qkv_grad, rate_qkv, decay_matrix
    )
    out_one, out_two, out_new = adam_update(
        out_weight, out_first, out_second, out_grad, rate_out, decay_matrix
    )
    up_one, up_two, up_new = adam_update(
        up_weight, up_first, up_second, up_grad, rate_up, decay_matrix
    )
    down_one, down_two, down_new = adam_update(
        down_weight, down_first, down_second, down_grad, rate_down, decay_matrix
    )
    return (
        mixed_out,
        input_grad,
        loss_value,
        norm_one,
        norm_two,
        norm_new,
        qkv_one,
        qkv_two,
        qkv_new,
        out_one,
        out_two,
        out_new,
        up_one,
        up_two,
        up_new,
        down_one,
        down_two,
        down_new,
    )


def round_up(value, unit):
    return -(-value // unit) * unit


def mxu(lhs, rhs):
    return jnp.dot(lhs, rhs, preferred_element_type=jnp.float32)


def mxu_nt(lhs, rhs):
    return lax.dot_general(lhs, rhs, (((1,), (1,)), ((), ())), preferred_element_type=jnp.float32)


def mxu_tn(lhs, rhs):
    return lax.dot_general(lhs, rhs, (((0,), (0,)), ((), ())), preferred_element_type=jnp.float32)


def low(values):
    return values.astype(jnp.bfloat16)


def kernel_params(**more):
    return pltpu.CompilerParams(vmem_limit_bytes=VMEM_BYTES, **more)


def cost(micros):
    return pl.CostEstimate(
        flops=int(1.1e9 * micros), bytes_accessed=int(3.5e6 * micros), transcendentals=0
    )


def iota(shape, dim):
    return lax.broadcasted_iota(jnp.int32, shape, dim)


def strict(size, lower):
    row = iota((size, size), 0)
    col = iota((size, size), 1)
    return low(((col < row) if lower else (row < col)).astype(jnp.float32))


def column_sums(matrix, column):
    return mxu(matrix, low(jnp.broadcast_to(column, (column.shape[0], 128))))[:, 0:1]


def route_kernel(
    cap, block, tokens, chunk, mine_ref, all_ref, own_ref, extra_ref, order_ref,
    rows_ref, cols_ref, pick_ref, excess_ref,
):
    spare = block - 1
    padded = own_ref.shape[1]
    expert_ids = iota((EXPERTS, padded), 0)
    before = strict(padded, False)
    first = own_ref[0:1, :]
    second = own_ref[1:2, :]
    first_hot = (expert_ids == first).astype(jnp.float32)
    second_hot = (expert_ids == second).astype(jnp.float32)
    first_rank = jnp.sum(first_hot * mxu(low(first_hot), before), axis=0, keepdims=True)
    first_load = jnp.sum(first_hot, axis=1, keepdims=True)
    second_rank = jnp.sum(
        second_hot * (mxu(low(second_hot), before) + first_load), axis=0, keepdims=True
    )
    own_over = jnp.maximum(first_load + jnp.sum(second_hot, axis=1, keepdims=True) - cap, 0.0)
    own_base = column_sums(strict(EXPERTS, True), own_over)

    def slot_of(expert, rank, hot):
        extra = jnp.sum(hot * own_base, axis=0, keepdims=True) + rank - cap
        last = jnp.where(extra < spare, EXPERTS * cap + extra, -1.0)
        slot = jnp.where(rank < cap, expert.astype(jnp.float32) * cap + rank, last)
        return jnp.where(expert >= 0, slot, -1.0)

    row = iota((8, padded), 0)
    table = jnp.where(
        row == 0,
        slot_of(first, first_rank, first_hot),
        jnp.where(row == 1, slot_of(second, second_rank, second_hot), extra_ref[...]),
    )
    rows_ref[...] = table
    cols_ref[...] = jnp.transpose(table)

    devices = order_ref.shape[1]
    length = all_ref.shape[1]
    owner = iota((devices, chunk), 0) * tokens
    place = iota((devices, chunk), 1)
    chunk_ids = iota((EXPERTS, chunk), 0)

    def add_chunk(step, total):
        start = step * chunk
        part = all_ref[:, pl.ds(pl.multiple_of(start, chunk), chunk)]
        hot = (chunk_ids == part[0:1, :]).astype(jnp.float32) + (chunk_ids == part[1:2, :]).astype(
            jnp.float32
        )
        position = place + start
        member = ((position >= owner) & (position < owner + tokens)).astype(jnp.float32)
        return total + mxu_nt(low(member), low(hot))

    loads = lax.fori_loop(
        0, length // chunk, add_chunk, jnp.zeros((devices, EXPERTS), jnp.float32)
    )
    over = jnp.maximum(loads - cap, 0.0)
    room = pick_ref.shape[0]
    by_device = jnp.max(jnp.sum(over, axis=1, keepdims=True), axis=0, keepdims=True) - spare
    by_expert = jnp.max(jnp.sum(over, axis=0, keepdims=True), axis=1, keepdims=True) - room
    excess_ref[...] = jnp.broadcast_to(jnp.maximum(by_device, by_expert), excess_ref.shape)
    turned = low((iota((devices, devices), 0) == order_ref[...]).astype(jnp.float32))
    over = mxu(turned, low(jnp.minimum(over, 256.0)))
    base = mxu(low(over), strict(EXPERTS, False))
    mine = iota((devices, EXPERTS), 1) == mine_ref[0]
    over_mine = jnp.sum(jnp.where(mine, over, 0.0), axis=1, keepdims=True)
    base_mine = jnp.sum(jnp.where(mine, base, 0.0), axis=1, keepdims=True)
    start_mine = column_sums(strict(devices, True), over_mine)
    width = min(1024, devices * block)
    for part in range(devices * block // width):
        inner = iota((devices, width), 1) + part * width - iota((devices, width), 0) * block
        inside = (inner >= 0) & (inner < spare)

        def spread(column):
            return jnp.sum(jnp.where(inside, column, 0.0), axis=0, keepdims=True)

        offset = spread(inner.astype(jnp.float32) - base_mine)
        used = (offset >= 0.0) & (offset < spread(over_mine))
        target = jnp.where(used, offset + spread(start_mine), -1.0)
        pick_ref[:, part * width : (part + 1) * width] = low(
            (iota((room, width), 0).astype(jnp.float32) == target).astype(jnp.float32)
        )


def route_call(cap, spare, room, tokens, mine, all_routes, own_routes, extra, order):
    padded = own_routes.shape[1]
    devices = order.shape[1]
    spec = pl.BlockSpec(memory_space=pltpu.VMEM)
    return pl.pallas_call(
        functools.partial(route_kernel, cap, spare, tokens, 2048),
        in_specs=[pl.BlockSpec(memory_space=pltpu.SMEM)] + [spec] * 4,
        out_shape=(
            jax.ShapeDtypeStruct((8, padded), jnp.float32),
            jax.ShapeDtypeStruct((padded, 8), jnp.float32),
            jax.ShapeDtypeStruct((room, devices * spare), jnp.bfloat16),
            jax.ShapeDtypeStruct((8, 128), jnp.float32),
        ),
        compiler_params=kernel_params(),
        cost_estimate=cost(4),
        name="route",
    )(mine, all_routes, own_routes, extra, order)


def norm_stats(stream):
    center = jnp.mean(stream, axis=1, keepdims=True)
    offset = stream - center
    spread = jnp.mean(offset * offset, axis=1, keepdims=True)
    inverse = lax.rsqrt(spread + norm_eps)
    return offset * inverse, inverse


def norm_pull(upstream, scaled, inverse, gain_row):
    dscaled = upstream * gain_row
    plain = jnp.mean(dscaled, axis=1, keepdims=True)
    cross = jnp.mean(dscaled * scaled, axis=1, keepdims=True)
    return (dscaled - plain - scaled * cross) * inverse


def crop_to(result, padded):
    for image in range(padded.shape[0] // IMG_PAD):
        result[image * IMG_LEN : (image + 1) * IMG_LEN, :] = padded[
            image * IMG_PAD : image * IMG_PAD + IMG_LEN, :
        ]


def half_mask(shape, half):
    lane = iota(shape, 1)
    return (lane < HEAD_DIM) if half == 0 else (lane >= HEAD_DIM)


def pick_half(tile, half):
    return jnp.where(half_mask(tile.shape, half), tile, jnp.zeros_like(tile))


class Staged:
    def __init__(self, ins, in_bufs, in_sems, outs, out_bufs, out_sems):
        self.copies = [
            pltpu.make_async_copy(source, buffer, in_sems.at[index])
            for index, (source, buffer) in enumerate(zip(ins, in_bufs))
        ]
        self.in_bufs = in_bufs
        self.out_bufs = out_bufs
        self.outs = outs
        self.out_sems = out_sems
        self.open = set()
        self.sent = []

    def begin(self):
        for index, copy in enumerate(self.copies):
            copy.start()
            self.open.add(index)

    def need(self, index):
        if index in self.open:
            self.copies[index].wait()
            self.open.remove(index)
        return self.in_bufs[index]

    def ship(self, index):
        copy = pltpu.make_async_copy(
            self.out_bufs[index], self.outs[index], self.out_sems.at[index]
        )
        copy.start()
        self.sent.append(copy)

    def end(self):
        for index in sorted(self.open):
            self.copies[index].wait()
        for copy in self.sent:
            copy.wait()


def staged_call(kernel_fn, name, micros, scalars, inputs, outs, scratch):
    outs = [jax.ShapeDtypeStruct(shape, kind) for shape, kind in outs]
    counts = (len(scalars), len(inputs), len(outs))

    def kernel(*refs):
        scalar_refs, refs = refs[: counts[0]], refs[counts[0] :]
        ins, refs = refs[: counts[1]], refs[counts[1] :]
        results, refs = refs[: counts[2]], refs[counts[2] :]
        in_bufs, refs = refs[: counts[1]], refs[counts[1] :]
        out_bufs, refs = refs[: counts[2]], refs[counts[2] :]
        in_sems, out_sems, *others = refs
        stage = Staged(ins, in_bufs, in_sems, results, out_bufs, out_sems)
        stage.begin()
        kernel_fn(stage, scalar_refs, others)
        stage.end()

    anywhere = pl.BlockSpec(memory_space=pltpu.HBM)
    return pl.pallas_call(
        kernel,
        in_specs=[pl.BlockSpec(memory_space=pltpu.SMEM)] * counts[0] + [anywhere] * counts[1],
        out_specs=[anywhere] * counts[2],
        out_shape=outs,
        scratch_shapes=[pltpu.VMEM(a.shape, a.dtype) for a in inputs]
        + [pltpu.VMEM(a.shape, a.dtype) for a in outs]
        + [pltpu.SemaphoreType.DMA((counts[1],)), pltpu.SemaphoreType.DMA((counts[2],))]
        + scratch,
        compiler_params=kernel_params(),
        cost_estimate=cost(micros),
        name=name,
    )(*scalars, *inputs)


def unpack_block(block, col, row, cols, rows, qkv_ref, out_ref, norm_ref):
    width = norm_ref.shape[1]
    deep = width // rows
    qkv_rows = 3 * width // cols
    out_rows = width // cols
    lanes = pl.ds(row * deep, deep)
    qkv_ref[pl.ds(col * qkv_rows, qkv_rows), lanes] = block[0:qkv_rows, :]
    out_ref[pl.ds(col * out_rows, out_rows), lanes] = block[qkv_rows : qkv_rows + out_rows, :]
    tail = block[qkv_rows + out_rows : qkv_rows + out_rows + 16, :].astype(jnp.float32)
    if col == 0:
        norm_ref[0:4, lanes] = tail[0:4] + tail[4:8] + tail[8:12]


def one_hot(slot_cols, slots, start=0):
    place = (iota((slot_cols[0].shape[0], slots), 1) + start).astype(jnp.float32)
    hot = place == slot_cols[0]
    for column in slot_cols[1:]:
        hot = hot | (place == column)
    return low(hot.astype(jnp.float32))


def collect(slot_cols, recv_ref, extra_ref):
    slots = recv_ref.shape[0]
    return mxu(one_hot(slot_cols, slots), recv_ref[...]) + mxu(
        one_hot(slot_cols, extra_ref.shape[0], slots), extra_ref[...]
    )


def front_kernel(cols, rows, stage, scalar_refs, scratch):
    (order_ref,) = scalar_refs
    pack_ref = stage.need(0)
    qkv_ref, out_ref, norm_ref, proj_ref, att_ref, lse_ref, middle_ref, send_ref, extra_ref = (
        stage.out_bufs
    )
    width = norm_ref.shape[1]
    norm_ref[...] = jnp.zeros_like(norm_ref)
    for col in range(cols):
        for row in range(rows):
            block = pack_ref[order_ref[col * rows + row]]
            unpack_block(block, col, row, cols, rows, qkv_ref, out_ref, norm_ref)
    for index in range(3):
        stage.ship(index)
    x_ref = stage.need(1)
    images = x_ref.shape[0] // IMG_PAD
    stream = x_ref[...].astype(jnp.float32)
    scaled, _ = norm_stats(stream)
    normed = low(scaled * norm_ref[0:1, :] + norm_ref[1:2, :])
    proj_ref[...] = low(mxu_nt(normed, qkv_ref[...]))
    stage.ship(3)
    key_ok = iota((IMG_PAD, IMG_PAD), 0) < IMG_LEN
    for image in range(images):
        span = slice(image * IMG_PAD, (image + 1) * IMG_PAD)
        for pair in range(HEADS // 2):
            lanes = slice(pair * 128, (pair + 1) * 128)
            queries = proj_ref[span, lanes]
            keys = proj_ref[span, width + pair * 128 : width + (pair + 1) * 128]
            values_t = jnp.transpose(
                proj_ref[span, 2 * width + pair * 128 : 2 * width + (pair + 1) * 128]
            )
            mixed = []
            for half in range(2):
                scores = mxu_nt(pick_half(keys, half), queries) * HEAD_DIM**-0.5
                scores = jnp.where(key_ok, scores, -1e30)
                top = jnp.max(scores, axis=0, keepdims=True)
                shifted = jnp.exp(scores - top)
                total = jnp.sum(shifted, axis=0, keepdims=True)
                probs = low(shifted * (1.0 / total))
                head = image * HEADS + pair * 2 + half
                lse_ref[head : head + 1, :] = top + jnp.log(total)
                mixed.append(mxu(values_t[half * HEAD_DIM : (half + 1) * HEAD_DIM, :], probs))
            att_ref[span, lanes] = low(jnp.transpose(jnp.concatenate(mixed, axis=0)))
    stage.ship(4)
    stage.ship(5)
    middle = stream + mxu(att_ref[...], out_ref[...])
    middle_ref[...] = middle
    stage.ship(6)
    table_ref = stage.need(2)
    scaled_two, _ = norm_stats(middle)
    second = low(scaled_two * norm_ref[2:3, :] + norm_ref[3:4, :])
    for start, size, result in slot_parts(send_ref, extra_ref):
        place = (iota((size, table_ref.shape[1]), 0) + start).astype(jnp.float32)
        hot = (place == table_ref[0:1, :]) | (place == table_ref[1:2, :])
        rows_out = mxu(low(hot.astype(jnp.float32)), second)
        if result is extra_ref:
            count = jnp.sum(table_ref[4:5, :], axis=1, keepdims=True)
            first_part = jnp.minimum(count, 256.0)
            rows_out = last_row(rows_out, (first_part, count - first_part))
        result[...] = low(rows_out)
    stage.ship(7)
    stage.ship(8)


def last_row(rows, values):
    lane = iota(rows.shape, 1)
    split = jnp.zeros_like(rows)
    for index, value in enumerate(values):
        split = jnp.where(lane == index, value, split)
    return jnp.where(iota(rows.shape, 0) == rows.shape[0] - 1, split, rows)


def slot_parts(send_ref, extra_ref):
    slots = send_ref.shape[0]
    size = min(512, slots)
    parts = [(start, size, send_ref.at[start : start + size]) for start in range(0, slots, size)]
    return parts + [(slots, extra_ref.shape[0], extra_ref)]


def front_call(cols, rows, slots, spare, order, x_pad, pack, table):
    tokens, width = x_pad.shape
    images = tokens // IMG_PAD
    half, full = jnp.bfloat16, jnp.float32
    outs = staged_call(
        functools.partial(front_kernel, cols, rows),
        "front",
        11,
        [order],
        [pack, x_pad, table],
        [
            ((3 * width, width), half),
            ((width, width), half),
            ((8, width), full),
            ((tokens, 3 * width), half),
            ((tokens, width), half),
            ((images * HEADS, IMG_PAD), full),
            ((tokens, width), full),
            ((slots, width), half),
            ((spare, width), half),
        ],
        [],
    )
    qkv, out, norms, proj, att, lse, middle, send, extra = outs
    return send, extra, middle, proj, att, lse, qkv, out, norms


def weight_copies(row_ref, piece_refs, buffer, sems):
    deep = piece_refs[0].shape[0]
    return [
        pltpu.make_async_copy(
            piece,
            buffer.at[pl.ds(pl.multiple_of(row_ref[index] * deep, deep), deep), :],
            sems.at[index],
        )
        for index, piece in enumerate(piece_refs)
    ]


GELU_A = 0.7978845608028654
GELU_B = 0.044715


def gelu_low(pre):
    inner = pre * (GELU_A + GELU_A * GELU_B * (pre * pre))
    half = 0.5 * pre
    return low(half + half * jnp.tanh(inner))


def gelu_both(pre):
    square = pre * pre
    curve = jnp.tanh(pre * (GELU_A + GELU_A * GELU_B * square))
    half = 0.5 * pre
    value = half + half * curve
    slope = 0.5 + 0.5 * curve + half * (1.0 - curve * curve) * (
        GELU_A + 3.0 * GELU_A * GELU_B * square
    )
    return low(value), low(slope)


def ff_chunks(width):
    size = min(width, 512)
    return [slice(start, start + size) for start in range(0, width, size)]


def row_blocks(rows, spare_rows):
    size = min(512, rows)
    blocks = [slice(start, start + size) for start in range(0, rows, size)]
    blocks[-1] = slice(blocks[-1].start, rows + spare_rows)
    return blocks


def spare_chunks(rows):
    size = min(rows, 1024)
    return [slice(start, start + size) for start in range(0, rows, size)]


def pick_rows(pick_ref, extra_ref):
    total = None
    for part in spare_chunks(extra_ref.shape[0]):
        term = mxu(pick_ref[:, part], extra_ref[part, :])
        total = term if total is None else total + term
    return low(total)


def place_rows(pick_ref, rows, kept_ref, sent_ref):
    half = kept_ref.shape[0]
    for start, result in ((0, kept_ref), (half, sent_ref)):
        for part in spare_chunks(half):
            source = slice(start + part.start, start + part.stop)
            result[part, :] = low(mxu_tn(pick_ref[:, source], rows))


def expert_rows(rows_in, up_buf, wait_down, down_buf):
    hiddens = [gelu_low(mxu(rows_in, up_buf[:, part])) for part in ff_chunks(up_buf.shape[1])]
    wait_down()
    total = None
    for part, hidden in zip(ff_chunks(up_buf.shape[1]), hiddens):
        term = mxu_nt(hidden, down_buf[:, part])
        total = term if total is None else total + term
    return low(total)


def pull_rows(grads_in, slope_ref, rows, up_buf, wait_up, down_buf, pre_ref):
    parts = ff_chunks(up_buf.shape[1])
    for part in parts:
        slope = slope_ref[rows, part].astype(jnp.float32)
        pre_ref[rows, part] = low(mxu(grads_in, down_buf[:, part]) * slope)
    wait_up()
    total = None
    for part in parts:
        term = mxu_nt(pre_ref[rows, part], up_buf[:, part])
        total = term if total is None else total + term
    return low(total)


def expert_kernel(pull, pieces, row_ref, main_ref, extra_ref, pick_ref, *rest):
    if pull:
        slope_ref, *rest = rest
    ups, downs, rest = rest[:pieces], rest[pieces : 2 * pieces], rest[2 * pieces :]
    send_ref, kept_ref, sent_ref, rows_ref, *rest = rest
    if pull:
        pre_ref, slope_buf, pre_buf, *rest = rest
    extra_buf, pick_buf, kept_buf, sent_buf, rows_buf, total_buf, up_buf, down_buf, *sems = rest
    up_sems, down_sems, in_sems, out_sems = sems
    main = main_ref.shape[0]
    blocks = row_blocks(main, rows_buf.shape[0] - main)
    inner = [slice(rows.start, min(rows.stop, main)) for rows in blocks]

    def part_of(ref, rows):
        return ref.at[rows.start : rows.stop, :]

    def copy_in(source, target, index):
        return pltpu.make_async_copy(source, target, in_sems.at[index])

    up_copies = weight_copies(row_ref, ups, up_buf, up_sems)
    down_copies = weight_copies(row_ref, downs, down_buf, down_sems)
    first_weights, last_weights = (
        (down_copies, up_copies) if pull else (up_copies, down_copies)
    )
    main_copies = [
        copy_in(part_of(main_ref, rows), part_of(rows_buf, rows), index)
        for index, rows in enumerate(inner)
    ]
    count = len(blocks)
    late_copies = [
        copy_in(extra_ref, extra_buf, count),
        copy_in(pick_ref, pick_buf, count + 1),
    ]
    slope_copies = [
        copy_in(part_of(slope_ref, rows), part_of(slope_buf, rows), count + 2 + index)
        for index, rows in enumerate(blocks)
    ] if pull else []
    first = [main_copies[0], *first_weights, *slope_copies[:1], *last_weights]
    for copy in [*first, *main_copies[1:], *late_copies, *slope_copies[1:]]:
        copy.start()
    for copy in first_weights:
        copy.wait()
    sent = []

    def send_out(source, target):
        copy = pltpu.make_async_copy(source, target, out_sems.at[len(sent)])
        copy.start()
        sent.append(copy)

    for index, rows in enumerate(blocks):
        main_copies[index].wait()
        if index == count - 1:
            for copy in late_copies:
                copy.wait()
            rows_buf[main:, :] = pick_rows(pick_buf, extra_buf)
            send_out(rows_buf, rows_ref)

        def wait_last():
            if index == 0:
                for copy in last_weights:
                    copy.wait()

        if pull:
            slope_copies[index].wait()
            total = pull_rows(rows_buf[rows, :], slope_buf, rows, up_buf, wait_last, down_buf, pre_buf)
            send_out(part_of(pre_buf, rows), part_of(pre_ref, rows))
        else:
            total = expert_rows(rows_buf[rows, :], up_buf, wait_last, down_buf)
        total_buf[rows, :] = total
        send_out(part_of(total_buf, inner[index]), part_of(send_ref, inner[index]))
    place_rows(pick_buf, total_buf[main:, :], kept_buf, sent_buf)
    send_out(kept_buf, kept_ref)
    send_out(sent_buf, sent_ref)
    for copy in sent:
        copy.wait()


def expert_call(name, rowpos, main, extra, pick, slope, ups, downs):
    slots, width = main.shape
    ff = ups[0].shape[1]
    rows = slots + pick.shape[0]
    blocks = len(row_blocks(slots, pick.shape[0]))
    pull = slope is not None
    half = (extra.shape[0] // 2, width)
    anywhere = pl.BlockSpec(memory_space=pltpu.HBM)
    inputs = [main, extra, pick] + ([slope] if pull else [])
    outs = [(slots, width), half, half, (rows, width)] + ([(rows, ff)] if pull else [])

    def buffer(shape):
        return pltpu.VMEM(shape, jnp.bfloat16)

    return pl.pallas_call(
        functools.partial(expert_kernel, pull, len(ups)),
        in_specs=[pl.BlockSpec(memory_space=pltpu.SMEM)]
        + [anywhere] * (len(inputs) + 2 * len(ups)),
        out_specs=[anywhere] * len(outs),
        out_shape=[jax.ShapeDtypeStruct(shape, jnp.bfloat16) for shape in outs],
        scratch_shapes=([buffer((rows, ff))] * 2 if pull else [])
        + [buffer(extra.shape), buffer(pick.shape), buffer(half), buffer(half)]
        + [buffer((rows, width))] * 2
        + [buffer((width, ff))] * 2
        + [
            pltpu.SemaphoreType.DMA((len(ups),)),
            pltpu.SemaphoreType.DMA((len(ups),)),
            pltpu.SemaphoreType.DMA((2 * blocks + 2,)),
            pltpu.SemaphoreType.DMA((2 * blocks + 3,)),
        ],
        compiler_params=kernel_params(),
        cost_estimate=cost(12),
        name=name,
    )(rowpos, *inputs, *ups, *downs)


def hidden_kernel(pieces, row_ref, rows_ref, *rest):
    ups = rest[:pieces]
    hidden_ref, slope_ref, up_buf, sems = rest[pieces:]

    @pl.when(pl.program_id(0) == 0)
    def _():
        copies = weight_copies(row_ref, ups, up_buf, sems)
        for copy in copies:
            copy.start()
        for copy in copies:
            copy.wait()

    rows_in = rows_ref[...]
    for part in ff_chunks(up_buf.shape[1]):
        hidden, slope = gelu_both(mxu(rows_in, up_buf[:, part]))
        hidden_ref[:, part] = hidden
        slope_ref[:, part] = slope


def hidden_call(rowpos, slot_rows, ups):
    rows, width = slot_rows.shape
    ff = ups[0].shape[1]
    block = 384 if rows % 384 == 0 else 128
    wide = pl.BlockSpec((block, ff), lambda i: (i, 0))
    return pl.pallas_call(
        functools.partial(hidden_kernel, len(ups)),
        grid=(rows // block,),
        in_specs=[
            pl.BlockSpec(memory_space=pltpu.SMEM),
            pl.BlockSpec((block, width), lambda i: (i, 0)),
        ]
        + [pl.BlockSpec(memory_space=pl.ANY)] * len(ups),
        out_specs=[wide, wide],
        out_shape=[jax.ShapeDtypeStruct((rows, ff), jnp.bfloat16)] * 2,
        scratch_shapes=[
            pltpu.VMEM((width, ff), jnp.bfloat16),
            pltpu.SemaphoreType.DMA((len(ups),)),
        ],
        compiler_params=kernel_params(dimension_semantics=("arbitrary",)),
        cost_estimate=cost(11),
        name="hidden",
    )(rowpos, slot_rows, *ups)


WG_PART = 512


def weight_grad_kernel(pieces, row_ref, left_ref, right_ref, *rest):
    results = rest[:pieces]
    left_buf, total_buf = rest[pieces:]
    deep = results[0].shape[0]

    @pl.when(pl.program_id(0) == 0)
    def _():
        left_buf[...] = jnp.transpose(left_ref[...])

    total_buf[...] = low(mxu(left_buf[...], right_ref[...]))
    for index, result in enumerate(results):
        start = pl.multiple_of(row_ref[index] * deep, deep)
        result[...] = total_buf[pl.ds(start, deep), :]


def weight_grad_call(rowpos, left, right, deep):
    rows, width = left.shape
    ff = right.shape[1]
    pieces = width // deep
    part = min(ff, WG_PART)
    return pl.pallas_call(
        functools.partial(weight_grad_kernel, pieces),
        grid=(ff // part,),
        in_specs=[
            pl.BlockSpec(memory_space=pltpu.SMEM),
            pl.BlockSpec((rows, width), lambda i: (0, 0)),
            pl.BlockSpec((rows, part), lambda i: (0, i)),
        ],
        out_specs=[pl.BlockSpec((deep, part), lambda i: (0, i))] * pieces,
        out_shape=[jax.ShapeDtypeStruct((deep, ff), jnp.bfloat16)] * pieces,
        scratch_shapes=[
            pltpu.VMEM((width, rows), jnp.bfloat16),
            pltpu.VMEM((width, part), jnp.bfloat16),
        ],
        compiler_params=kernel_params(dimension_semantics=("arbitrary",)),
        cost_estimate=cost(2),
        name="weight_grad",
    )(rowpos, left, right)


def turn_kernel(stage, scalar_refs, scratch):
    recv_ref, back_ref, cols_ref = (stage.need(index) for index in range(3))
    mixed_ref, grad_ref, send_ref, extra_ref = stage.out_bufs
    first = collect([cols_ref[:, 0:1]], recv_ref, back_ref)
    second = collect([cols_ref[:, 1:2]], recv_ref, back_ref)
    middle_ref, teacher_ref, cot_ref, valid_ref, table_ref = (
        stage.need(index) for index in range(3, 8)
    )
    result = middle_ref[...] + cols_ref[:, 2:3] * first + cols_ref[:, 3:4] * second
    crop_to(scratch[0], result)
    mixed_ref[...] = low(scratch[0][...])
    stage.ship(0)
    mismatch = result - teacher_ref[...].astype(jnp.float32)
    masked = cols_ref[:, 4:5] * mismatch
    valid_total = valid_ref[...]
    squares = jnp.sum(masked * mismatch, axis=0, keepdims=True)
    square_sum = jnp.sum(squares, axis=1, keepdims=True)
    grad_out = cot_ref[...].astype(jnp.float32) + (2.0 / valid_total) * masked
    grad_ref[...] = grad_out
    stage.ship(1)
    rounded = low(grad_out).astype(jnp.float32)
    both = jnp.concatenate(
        [low(cols_ref[:, 2:3] * rounded), low(cols_ref[:, 3:4] * rounded)], axis=0
    )
    for start, size, part in slot_parts(send_ref, extra_ref):
        place = (iota((size, table_ref.shape[1]), 0) + start).astype(jnp.float32)
        hot = jnp.concatenate(
            [
                low((place == table_ref[0:1, :]).astype(jnp.float32)),
                low((place == table_ref[1:2, :]).astype(jnp.float32)),
            ],
            axis=1,
        )
        rows = mxu(hot, both)
        if part is extra_ref:
            top = low(square_sum).astype(jnp.float32)
            rest = square_sum - top
            middle = low(rest).astype(jnp.float32)
            rows = last_row(rows, (top, middle, rest - middle))
        part[...] = low(rows)
    stage.ship(2)
    stage.ship(3)


def turn_call(recv, back, cols, table, middle, teacher, cot, valid):
    half, full = jnp.bfloat16, jnp.float32
    own = (middle.shape[0] // IMG_PAD * IMG_LEN, middle.shape[1])
    mixed, grad_out, send, extra = staged_call(
        turn_kernel,
        "turn",
        6,
        [],
        [recv, back, cols, middle, teacher, cot, valid, table],
        [(own, half), (middle.shape, full), (recv.shape, half), (back.shape, half)],
        [pltpu.VMEM(own, full)],
    )
    return send, extra, mixed, grad_out


def back_kernel(cols_n, rows_n, stage, scalar_refs, scratch):
    (order_ref,) = scalar_refs
    gproj_buf, gatt_buf, gqkv_buf, gout_buf, gnorm_buf = scratch
    input_ref, kept_ref, sent_ref = stage.out_bufs
    recv_ref, back_ref, cols_ref, middle_ref, norm_ref, grad_ref = (
        stage.need(index) for index in range(6)
    )
    width = recv_ref.shape[1]
    images = middle_ref.shape[0] // IMG_PAD
    grad_second = collect([cols_ref[:, 0:1], cols_ref[:, 1:2]], recv_ref, back_ref)
    scaled_two, inverse_two = norm_stats(middle_ref[...])
    gnorm_buf[...] = jnp.zeros_like(gnorm_buf)
    gnorm_buf[2:3, :] = jnp.sum(grad_second * scaled_two, axis=0, keepdims=True)
    gnorm_buf[3:4, :] = jnp.sum(grad_second, axis=0, keepdims=True)
    grad_middle = grad_ref[...] + norm_pull(grad_second, scaled_two, inverse_two, norm_ref[2:3, :])
    middle_low = low(grad_middle)
    att_ref, out_ref = stage.need(6), stage.need(7)
    gout_buf[...] = low(mxu(jnp.transpose(att_ref[...]), middle_low))
    proj_ref, lse_ref = stage.need(8), stage.need(9)
    gatt_buf[...] = low(mxu_nt(middle_low, out_ref[...]))
    scale = HEAD_DIM**-0.5
    key_ok = iota((IMG_PAD, IMG_PAD), 0) < IMG_LEN
    for image in range(images):
        span = slice(image * IMG_PAD, (image + 1) * IMG_PAD)
        for pair in range(HEADS // 2):
            q_lanes = slice(pair * 128, (pair + 1) * 128)
            k_lanes = slice(width + pair * 128, width + (pair + 1) * 128)
            v_lanes = slice(2 * width + pair * 128, 2 * width + (pair + 1) * 128)
            queries = proj_ref[span, q_lanes]
            keys = proj_ref[span, k_lanes]
            values = proj_ref[span, v_lanes]
            upstream = gatt_buf[span, q_lanes]
            keys_t = jnp.transpose(keys)
            query_parts = []
            key_parts = []
            value_parts = []
            for half in range(2):
                head = image * HEADS + pair * 2 + half
                scores = mxu_nt(pick_half(keys, half), queries) * scale
                probs = jnp.exp(jnp.where(key_ok, scores, -1e30) - lse_ref[head : head + 1, :])
                grad_probs = mxu_nt(pick_half(values, half), upstream)
                inner = jnp.sum(probs * grad_probs, axis=0, keepdims=True)
                grad_scores = low(probs * (grad_probs - inner))
                value_parts.append(mxu(low(probs), upstream))
                key_parts.append(mxu(grad_scores, queries))
                query_parts.append(
                    mxu(keys_t[half * HEAD_DIM : (half + 1) * HEAD_DIM, :], grad_scores)
                )
            left = half_mask(key_parts[0].shape, 0)
            gproj_buf[span, q_lanes] = low(
                jnp.transpose(jnp.concatenate(query_parts, axis=0)) * scale
            )
            gproj_buf[span, k_lanes] = low(jnp.where(left, key_parts[0], key_parts[1]) * scale)
            gproj_buf[span, v_lanes] = low(jnp.where(left, value_parts[0], value_parts[1]))
    x_ref, qkv_ref = stage.need(10), stage.need(11)
    stream = x_ref[...].astype(jnp.float32)
    scaled, inverse = norm_stats(stream)
    normed = low(scaled * norm_ref[0:1, :] + norm_ref[1:2, :])
    grad_normed = mxu(gproj_buf[...], qkv_ref[...])
    gqkv_buf[...] = low(mxu(jnp.transpose(gproj_buf[...]), normed))
    gnorm_buf[0:1, :] = jnp.sum(grad_normed * scaled, axis=0, keepdims=True)
    gnorm_buf[1:2, :] = jnp.sum(grad_normed, axis=0, keepdims=True)
    crop_to(input_ref, grad_middle + norm_pull(grad_normed, scaled, inverse, norm_ref[0:1, :]))
    stage.ship(0)
    deep = width // rows_n
    qkv_rows = 3 * width // cols_n
    out_rows = width // cols_n
    for col in range(cols_n):
        for row in range(rows_n):
            index = order_ref[col * rows_n + row]
            lanes = slice(row * deep, (row + 1) * deep)
            qkv_part = gqkv_buf[col * qkv_rows : (col + 1) * qkv_rows, lanes]
            out_part = gout_buf[col * out_rows : (col + 1) * out_rows, lanes]
            norm_part = low(gnorm_buf[:, lanes])
            half = kept_ref.shape[0]

            def write(result, place):
                result[place, 0:qkv_rows, :] = qkv_part
                result[place, qkv_rows : qkv_rows + out_rows, :] = out_part
                result[place, qkv_rows + out_rows : qkv_rows + out_rows + 16, :] = norm_part

            @pl.when(index < half)
            def _():
                write(kept_ref, index)

            @pl.when(index >= half)
            def _():
                write(sent_ref, index - half)

    stage.ship(1)
    stage.ship(2)


def back_call(
    cols_n, rows_n, order, recv, back, cols, x_pad, middle, grad_out, proj, att, lse, qkv, out, norms
):
    tokens, width = x_pad.shape
    blocks = cols_n * rows_n
    block = (blocks // 2, 4 * width // cols_n + 16, width // rows_n)
    half, full = jnp.bfloat16, jnp.float32
    return staged_call(
        functools.partial(back_kernel, cols_n, rows_n),
        "back",
        12,
        [order],
        [recv, back, cols, middle, norms, grad_out, att, out, proj, lse, x_pad, qkv],
        [((tokens // IMG_PAD * IMG_LEN, width), full), (block, half), (block, half)],
        [
            pltpu.VMEM((tokens, 3 * width), half),
            pltpu.VMEM((tokens, width), half),
            pltpu.VMEM((3 * width, width), half),
            pltpu.VMEM((width, width), half),
            pltpu.VMEM((16, width), full),
        ],
    )


def adam_kernel(slabs, where_ref, *refs):
    up_grads, down_grads = refs[:slabs], refs[slabs : 2 * slabs]
    ins, outs = refs[2 * slabs : 2 * slabs + 6], refs[-6:]
    for index in range(slabs):

        @pl.when(pl.program_id(0) == index)
        def _():
            for rate, gradient, inputs, results in (
                (rate_up, up_grads[index], ins[0:3], outs[0:3]),
                (rate_down, down_grads[index], ins[3:6], outs[3:6]),
            ):
                first_new, second_new, weight_new = adam_update(
                    inputs[0][0],
                    inputs[1][0],
                    inputs[2][0],
                    gradient[...].astype(jnp.float32),
                    rate,
                    decay_matrix,
                )
                results[0][0] = first_new
                results[1][0] = second_new
                results[2][0] = weight_new


def adam_call(places, gradients, arrays, earlier):
    slabs = len(gradients)
    deep, ff = gradients[0][0].shape
    tile = min(deep, 64 * slabs)
    tiles = deep // tile

    def gradient_spec(index):
        def where_is(slab, part, where):
            return (jnp.where(slab == index, part, jnp.where(slab < index, 0, tiles - 1)), 0)

        return pl.BlockSpec((tile, ff), where_is)

    block = pl.BlockSpec(
        (1, tile, ff), lambda slab, part, where: (where[2 * slab], part, where[2 * slab + 1])
    )
    in_specs = [gradient_spec(index) for index in range(slabs)] * 2 + [block] * 6
    aliases = {}
    if earlier is not None:
        aliases = {1 + len(in_specs) + index: index for index in range(6)}
        in_specs += [pl.BlockSpec(memory_space=pl.ANY)] * 6
    return pl.pallas_call(
        functools.partial(adam_kernel, slabs),
        grid_spec=pltpu.PrefetchScalarGridSpec(
            num_scalar_prefetch=1, grid=(slabs, tiles), in_specs=in_specs, out_specs=[block] * 6
        ),
        out_shape=[jax.ShapeDtypeStruct(arrays[0].shape, jnp.float32)] * 6,
        input_output_aliases=aliases,
        compiler_params=kernel_params(dimension_semantics=("arbitrary", "arbitrary")),
        cost_estimate=cost(6 * slabs),
        name="adam",
    )(places, *[g[0] for g in gradients], *[g[1] for g in gradients], *arrays, *(earlier or ()))


def swap(values, mask):
    rows = lax.axis_size("row")
    cols = lax.axis_size("col")

    def flat(place):
        return place % rows * cols + place // rows

    return lax.ppermute(
        values, ("row", "col"), [(flat(i), flat(i ^ mask)) for i in range(rows * cols)]
    )


def gather_steps():
    bits = []
    bit = lax.axis_size("col") * lax.axis_size("row") // 2
    while bit:
        bits.append(bit)
        bit //= 2
    return [bits[start : start + 2] for start in range(0, len(bits), 2)]


def masks_of(bits):
    return [
        sum(bit for place, bit in enumerate(bits) if index >> place & 1)
        for index in range(1, 1 << len(bits))
    ]


def weight_steps():
    rows = lax.axis_size("row")
    far = [bit for bits in gather_steps() for bit in bits if 1 < bit < rows]
    wide = [bit for bits in gather_steps() for bit in bits if bit > rows]
    pairs = [wide[start : start + 2] for start in range(0, len(wide), 2)]
    return [bits for bits in [far, *pairs, [rows], [1]] if bits]


def block_order(steps):
    rows = lax.axis_size("row")
    devices = lax.axis_size("col") * rows
    differs = jnp.arange(devices, dtype=jnp.int32) ^ (
        lax.axis_index("col") * rows + lax.axis_index("row")
    )
    order = jnp.zeros((devices,), jnp.int32)
    place = 0
    for bits in steps:
        for bit in bits:
            order = order | jnp.where((differs & bit) != 0, 1 << place, 0)
            place += 1
    return order


def gather_step(gathered, bits):
    return jnp.concatenate([gathered] + [swap(gathered, mask) for mask in masks_of(bits)], axis=0)


def halves_step(kept, sent):
    return low(kept.astype(jnp.float32) + swap(sent, 1).astype(jnp.float32))


def scatter_step(blocks, bits):
    count = 1 << len(bits)
    size = blocks.shape[0] // count
    total = blocks[:size].astype(jnp.float32)
    for index, mask in enumerate(masks_of(bits)):
        sent = blocks[(index + 1) * size : (index + 2) * size]
        total = total + swap(sent, mask).astype(jnp.float32)
    return low(total)


def pad_images(values):
    tokens, width = values.shape
    images = tokens // IMG_LEN
    padded = jnp.pad(
        values.reshape(images, IMG_LEN, width), ((0, 0), (0, IMG_PAD - IMG_LEN), (0, 0))
    )
    return padded.reshape(images * IMG_PAD, width)


def pad_rows(values, fill):
    images = values.shape[1] // IMG_LEN
    padded = jnp.pad(
        values.reshape(values.shape[0], images, IMG_LEN),
        ((0, 0), (0, 0), (0, IMG_PAD - IMG_LEN)),
        constant_values=fill,
    )
    return padded.reshape(values.shape[0], images * IMG_PAD)


def to_experts(main, extra, share, beside, rows=None):
    if share > 1:
        width = main.shape[1]
        main = jnp.broadcast_to(
            main.reshape(EXPERTS, 1, -1, width),
            (EXPERTS, share, main.shape[0] // EXPERTS, width),
        ).reshape(-1, width)
    first, *others = gather_steps()
    blocks = gather_step(extra[None], first)
    if rows is None:
        main, blocks, beside = lax.optimization_barrier((main, blocks, beside))
    else:
        main, blocks, rows = lax.optimization_barrier((main, blocks, rows))
        beside = beside(rows)
    main = lax.all_to_all(main, BOTH, split_axis=0, concat_axis=0, tiled=True)
    for place, bits in enumerate(others):
        if place == len(others) - 1 and rows is not None:
            blocks, beside = lax.optimization_barrier((blocks, beside))
        blocks = gather_step(blocks, bits)
    return main, blocks.reshape(-1, extra.shape[1]), beside


def from_experts(main, share):
    main = lax.all_to_all(main, BOTH, split_axis=0, concat_axis=0, tiled=True)
    width = main.shape[1]
    if share > 1:
        main = low(
            jnp.sum(main.reshape(EXPERTS, share, -1, width).astype(jnp.float32), axis=1)
        ).reshape(-1, width)
    return main


def spare_home(kept, sent):
    blocks = lax.axis_size("row") * lax.axis_size("col") // 2
    blocks = halves_step(
        kept.reshape(blocks, -1, kept.shape[1]), sent.reshape(blocks, -1, sent.shape[1])
    )
    for bits in reversed(gather_steps()[1:]):
        if bits != [1]:
            blocks = scatter_step(blocks, [bit for bit in bits if bit != 1])
    return blocks


def body(*args):
    (
        x_in,
        cotangent,
        teacher,
        valid_mask,
        routes,
        gate_weights,
        norm_params,
        qkv_weight,
        out_weight,
        up_weight,
        down_weight,
        norm_first,
        norm_second,
        qkv_first,
        qkv_second,
        out_first,
        out_second,
        up_first,
        up_second,
        down_first,
        down_second,
    ) = args
    rows_n = lax.axis_size("row")
    cols_n = lax.axis_size("col")
    devices = rows_n * cols_n
    my_row = lax.axis_index("row")
    me = lax.axis_index("col") * rows_n + my_row
    tokens, width = x_in.shape
    token_total = routes.shape[1]
    experts_here, deep, ff = up_weight.shape
    share = rows_n // experts_here
    ff_here = ff // share
    mean_load = TOP * tokens / EXPERTS
    cap = max(16, 16 * round(1.3 * mean_load / 16))
    slots = EXPERTS * cap
    spare = 32
    room = 4 * devices

    def three_parts(values):
        top = lax.reduce_precision(values, 8, 7)
        rest = values - top
        middle_part = lax.reduce_precision(rest, 8, 7)
        return [low(top), low(middle_part), low(rest - middle_part)]

    small = jnp.concatenate(
        [
            low(jnp.transpose(qkv_weight)),
            low(out_weight),
            *three_parts(norm_params),
            jnp.zeros((4, deep), jnp.bfloat16),
        ],
        axis=0,
    )
    order = block_order(gather_steps())
    pack_order = block_order(weight_steps())

    partners = [my_row ^ index for index in range(rows_n)]
    rowpos = jnp.stack(partners).astype(jnp.int32)

    def slab(values, partner):
        return low(
            lax.dynamic_slice(
                values, (partner // share, 0, partner % share * ff_here), (1, deep, ff_here)
            )[0]
        )

    far = rows_n // 2
    first_step, second_step, *last_steps = gather_steps()
    far_ones = [index for index in range(2, rows_n)] or [1]
    first_far, *more_far = far_ones
    steps = weight_steps()
    pack = gather_step(small[None], steps[0])
    held = (routes, gate_weights, valid_mask, x_in, up_weight, down_weight)
    pack, held = lax.optimization_barrier((pack, held))
    early = swap(slab(up_weight, partners[first_far]), first_far)

    start = me * tokens
    own_routes = pad_rows(lax.dynamic_slice_in_dim(held[0], start, tokens, 1), -1)
    own_gates = pad_rows(lax.dynamic_slice_in_dim(held[1], start, tokens, 1), 0)
    own_mask = pad_rows(
        lax.dynamic_slice_in_dim(held[2], my_row * tokens, tokens, 0)[None], 0
    ).astype(jnp.float32)
    padded = own_routes.shape[1]
    extra = jnp.concatenate(
        [jnp.zeros((2, padded), jnp.float32), own_gates, own_mask, jnp.zeros((3, padded), jnp.float32)],
        axis=0,
    )
    all_routes = jnp.pad(
        held[0], ((0, 0), (0, round_up(token_total, 2048) - token_total)), constant_values=-1
    )
    mine = (me // share).astype(jnp.int32).reshape(1)
    x_pad = pad_images(held[3])
    up_slabs = [slab(held[4], partners[index]) for index in more_far]
    down_slabs = [slab(held[5], partners[index]) for index in far_ones]
    near = [1] if first_far != 1 else []
    near_slabs = [(slab(held[4], partners[p]), slab(held[5], partners[p])) for p in near]
    ups = {0: slab(held[4], partners[0])}
    downs = {0: slab(held[5], partners[0])}
    for bits in steps[1:-2]:
        pack = gather_step(pack, bits)
    early, up_slabs = lax.optimization_barrier((early, up_slabs))
    pack, early, down_slabs, near_slabs = lax.optimization_barrier(
        (pack, early, down_slabs, near_slabs)
    )
    ups[first_far] = early
    up_pieces = [swap(piece, index) for index, piece in zip(more_far, up_slabs)]
    pack = gather_step(pack, steps[-2])
    table, table_cols, pick, excess = route_call(
        cap, spare, room, tokens, mine, all_routes, own_routes, extra, order[None]
    )
    overflow = excess[0, 0] > 0

    pack, up_pieces, table, table_cols, pick, x_pad, down_slabs = lax.optimization_barrier(
        (pack, up_pieces, table, table_cols, pick, x_pad, down_slabs)
    )
    ups.update(zip(more_far, up_pieces))
    half = (len(far_ones) + 1) // 2
    for index, piece in zip(far_ones[:half], down_slabs):
        downs[index] = swap(piece, index)
    for p, (up_slab, down_slab) in zip(near, near_slabs):
        ups[p], downs[p] = swap(up_slab, p), swap(down_slab, p)
    pack = gather_step(pack, steps[-1])
    send, spare_rows, middle, proj, att, lse, qkv_all, out_all, norms = front_call(
        cols_n, rows_n, slots, spare, pack_order, x_pad, pack, table
    )
    spare_rows, down_slabs = lax.optimization_barrier((spare_rows, down_slabs))
    for index, piece in zip(far_ones[half:], down_slabs[half:]):
        downs[index] = swap(piece, index)
    main, extras, (ups, downs) = to_experts(send, spare_rows, share, (ups, downs))
    ups = [ups[index] for index in range(rows_n)]
    downs = [downs[index] for index in range(rows_n)]

    counts = extras.reshape(devices, spare, width)[:, spare - 1, :2].astype(jnp.float32)
    valid_total = jnp.sum(counts)
    main, kept, sent, slot_rows = expert_call(
        "expert", rowpos, main, extras, pick, None, ups, downs
    )
    combined = from_experts(main, share)
    extras = spare_home(kept, sent)
    grad_send, grad_spare, mixed_rows, grad_out = turn_call(
        combined,
        scatter_step(extras, gather_steps()[0])[0],
        table_cols,
        table,
        middle,
        pad_images(teacher),
        pad_images(cotangent),
        valid_total[None, None],
    )
    main, extras, (hidden, slope) = to_experts(
        grad_send, grad_spare, share, lambda rows: hidden_call(rowpos, rows, ups), slot_rows
    )
    errors = extras.reshape(devices, spare, width)
    main, kept, sent, grad_slots, grad_pre = expert_call(
        "pull", rowpos, main, extras, pick, slope, ups, downs
    )
    grad_back = from_experts(main, share)
    extras = spare_home(kept, sent)
    up_grads = weight_grad_call(rowpos, slot_rows, grad_pre, deep)
    raw_ups = up_grads
    extras, up_grads, grad_slots = lax.optimization_barrier((extras, up_grads, grad_slots))
    down_grads = weight_grad_call(rowpos, grad_slots, hidden, deep)
    grad_back_spare = scatter_step(extras, gather_steps()[0])[0]

    arrays = (up_weight, up_first, up_second, down_weight, down_first, down_second)

    def places_of(chosen):
        return jnp.stack(
            [value for p in chosen for value in (partners[p] // share, partners[p] % share)]
        ).astype(jnp.int32)

    near = list(range(min(2, rows_n)))
    apart = list(range(2, rows_n))
    groups = [apart[: len(apart) // 2], apart[len(apart) // 2 :]]
    groups = [group for group in groups if group]
    gradients = {}
    for index in near:
        pair = (up_grads[index], down_grads[index])
        gradients[index] = tuple(swap(p, index) for p in pair) if index else pair
    if groups:
        up_far = [swap(raw_ups[index], index) for index in groups[0]]
        grad_back, grad_back_spare, up_far, down_grads = lax.optimization_barrier(
            (grad_back, grad_back_spare, up_far, down_grads)
        )
        down_far = [swap(down_grads[index], index) for index in groups[0]]

    input_rows, blocks, sent_blocks = back_call(
        cols_n,
        rows_n,
        pack_order,
        grad_back,
        grad_back_spare,
        table_cols,
        x_pad,
        middle,
        grad_out,
        proj,
        att,
        lse,
        qkv_all,
        out_all,
        norms,
    )
    if groups:
        blocks, sent_blocks, down_far = lax.optimization_barrier((blocks, sent_blocks, down_far))
        for index, pair in zip(groups[0], zip(up_far, down_far)):
            gradients[index] = pair
    experts_new = None
    later = []
    for place, bits in enumerate(reversed(weight_steps())):
        if place == 0:
            blocks = halves_step(blocks, sent_blocks)
        else:
            blocks = scatter_step(blocks, bits)
        if place == 0:
            sent = [gradients[index] for index in near]
            apart_sent = [gradients[index] for index in groups[0]] if groups else []
            blocks, sent, up_grads, down_grads, errors = lax.optimization_barrier(
                (blocks, sent, up_grads, down_grads, errors)
            )

            experts_new = adam_call(places_of(near), sent, arrays, None)
            if len(groups) > 1:
                later = [
                    (swap(up_grads[index], index), swap(down_grads[index], index))
                    for index in groups[1]
                ]
        if place == 1:
            blocks, experts_new, errors, apart_sent = lax.optimization_barrier(
                (blocks, experts_new, errors, apart_sent)
            )
            loss_value = jnp.sum(errors[:, spare - 1, :3].astype(jnp.float32)[order]) / valid_total
            if groups:
                experts_new = adam_call(places_of(groups[0]), apart_sent, arrays, experts_new)
        if place == 2:
            blocks, experts_new, loss_value = lax.optimization_barrier(
                (blocks, experts_new, loss_value)
            )
    if later:
        experts_new = adam_call(places_of(groups[1]), later, arrays, experts_new)
    up_one, up_two, up_new, down_one, down_two, down_new = experts_new
    summed = blocks[0].astype(jnp.float32)
    qkv_rows = qkv_weight.shape[1]
    out_rows = out_weight.shape[0]
    qkv_one, qkv_two, qkv_new = adam_update(
        qkv_weight, qkv_first, qkv_second, jnp.transpose(summed[:qkv_rows]), rate_qkv, decay_matrix
    )
    out_one, out_two, out_new = adam_update(
        out_weight,
        out_first,
        out_second,
        summed[qkv_rows : qkv_rows + out_rows],
        rate_out,
        decay_matrix,
    )
    norm_one, norm_two, norm_new = adam_update(
        norm_params,
        norm_first,
        norm_second,
        summed[qkv_rows + out_rows : qkv_rows + out_rows + 4],
        rate_norm,
        0.0,
    )
    quick = (
        mixed_rows,
        input_rows,
        loss_value,
        norm_one,
        norm_two,
        norm_new,
        qkv_one,
        qkv_two,
        qkv_new,
        out_one,
        out_two,
        out_new,
        up_one,
        up_two,
        up_new,
        down_one,
        down_two,
        down_new,
    )

    def again(state):
        return (jnp.bool_(False), general_body(*args))

    return lax.while_loop(lambda state: state[0], again, (overflow, quick))[1]


def solution(mesh):
    in_specs = (
        P(("col", "row"), None),
        P(("col", "row"), None),
        P(("col", "row"), None),
        P("col"),
        P(),
        P(),
        P(None, "row"),
        P("row", "col"),
        P("col", "row"),
        P("col", "row", None),
        P("col", "row", None),
        P(None, "row"),
        P(None, "row"),
        P("row", "col"),
        P("row", "col"),
        P("col", "row"),
        P("col", "row"),
        P("col", "row", None),
        P("col", "row", None),
        P("col", "row", None),
        P("col", "row", None),
    )
    out_specs = (
        P(("col", "row"), None),
        P(("col", "row"), None),
        P(),
        P(None, "row"),
        P(None, "row"),
        P(None, "row"),
        P("row", "col"),
        P("row", "col"),
        P("row", "col"),
        P("col", "row"),
        P("col", "row"),
        P("col", "row"),
        P("col", "row", None),
        P("col", "row", None),
        P("col", "row", None),
        P("col", "row", None),
        P("col", "row", None),
        P("col", "row", None),
    )
    return jax.shard_map(body, mesh=mesh, in_specs=in_specs, out_specs=out_specs, check_vma=False)
```

```python
import functools

import jax
import jax.numpy as jnp
from jax import lax
from jax.experimental import pallas as pl
from jax.experimental.pallas import tpu as pltpu
from jax.sharding import PartitionSpec as P

HEADS = 8
HEAD_DIM = 64
EXPERTS = 32
TOP = 2
IMG_LEN = 197
STEP = 5
IMG_PAD = 256
BOTH = ("col", "row")
VMEM_BYTES = 56 * 1024 * 1024

norm_eps = 1e-06
beta_one = 0.9
beta_two = 0.999
adam_eps = 1e-08
decay_matrix = 0.1
rate_norm = 0.4
rate_qkv = 0.02
rate_out = 0.06
rate_up = 0.02
rate_down = 0.01


def dispatch_tables(routes, capacity):
    flat_routes = routes.reshape(-1)
    picks_total = flat_routes.shape[0]
    order_idx = jnp.argsort(flat_routes, stable=True)
    sorted_experts = flat_routes[order_idx]
    expert_ids = jnp.arange(EXPERTS, dtype=jnp.int32)
    expert_load = jnp.sum((flat_routes[:, None] == expert_ids[None, :]).astype(jnp.int32), axis=0)
    starts_at = jnp.cumsum(expert_load) - expert_load
    position = jnp.arange(picks_total, dtype=jnp.int32)
    slot_index = sorted_experts * capacity + position - starts_at[sorted_experts]
    slot_token = jnp.zeros((EXPERTS * capacity,), jnp.int32).at[slot_index].set(order_idx // TOP)
    slot_used = jnp.zeros((EXPERTS * capacity,), jnp.int32).at[slot_index].set(1)
    pick_slot = jnp.zeros((picks_total,), jnp.int32).at[order_idx].set(slot_index)
    return (slot_token, slot_used, order_idx, slot_index, pick_slot.reshape(-1, TOP))


def gelu_tanh(inner_value):
    return jax.nn.gelu(inner_value, approximate=True)


def spread_cols(values):
    return lax.all_gather(values, "col", axis=0, tiled=True)


def spread_rows(values):
    return lax.all_gather(values, "row", axis=0, tiled=True)


def sum_rows(term_fn, row_total):
    return lax.psum_scatter(
        term_fn(jnp.int32(0), row_total * lax.axis_size("row")),
        "row",
        scatter_dimension=0,
        tiled=True,
    )


def sum_cols(term_fn, row_total):
    return lax.psum_scatter(
        term_fn(jnp.int32(0), row_total * lax.axis_size("col")),
        "col",
        scatter_dimension=0,
        tiled=True,
    )


def to_heads(values):
    return lax.all_to_all(values, "col", split_axis=0, concat_axis=1, tiled=True)


def from_heads(values):
    return lax.all_to_all(values, "col", split_axis=1, concat_axis=0, tiled=True)


def token_sums(first_part, second_part):
    return lax.psum((first_part, second_part), "row")


def norm_forward(stream, gain_row, shift_row):
    full_width = stream.shape[1] * lax.axis_size("row")
    sum_plain, squares = token_sums(jnp.sum(stream, axis=1), jnp.sum(stream * stream, axis=1))
    center = sum_plain / full_width
    offset = stream - center[:, None]
    spread = squares / full_width - center * center
    inverse = lax.rsqrt(spread + norm_eps)
    scaled = offset * inverse[:, None]
    return (scaled * gain_row + shift_row, scaled, inverse)


def norm_backward(upstream, scaled, inverse, gain_row):
    full_width = scaled.shape[1] * lax.axis_size("row")
    dscaled = upstream * gain_row
    sum_plain, sum_cross = token_sums(jnp.sum(dscaled, axis=1), jnp.sum(dscaled * scaled, axis=1))
    inner_grad = (
        dscaled - (sum_plain / full_width)[:, None] - scaled * (sum_cross / full_width)[:, None]
    )
    return (
        inner_grad * inverse[:, None],
        jnp.sum(upstream * scaled, axis=0),
        jnp.sum(upstream, axis=0),
    )


def attend_local(packed):
    images = packed.shape[0] // IMG_LEN
    split_heads = packed.reshape(images, IMG_LEN, 3, HEADS, HEAD_DIM)
    scores = jnp.einsum(
        "gqhd,gkhd->ghqk",
        split_heads[:, :, 0],
        split_heads[:, :, 1],
        preferred_element_type=jnp.float32,
    ) * HEAD_DIM ** (-0.5)
    top_score = jnp.max(scores, axis=-1, keepdims=True)
    shifted = jnp.exp(scores - top_score)
    totals = jnp.sum(shifted, axis=-1, keepdims=True)
    weights = (shifted / totals).astype(jnp.bfloat16)
    log_norm = top_score + jnp.log(totals)
    mixed_heads = jnp.einsum(
        "ghqk,gkhd->gqhd", weights, split_heads[:, :, 2], preferred_element_type=jnp.float32
    )
    return (mixed_heads.reshape(images * IMG_LEN, HEADS * HEAD_DIM), log_norm)


def attend_back(packed, log_norm, upstream):
    images = packed.shape[0] // IMG_LEN
    split_heads = packed.reshape(images, IMG_LEN, 3, HEADS, HEAD_DIM)
    queries = split_heads[:, :, 0]
    key_part = split_heads[:, :, 1]
    value_part = split_heads[:, :, 2]
    grad_mixed = upstream.reshape(images, IMG_LEN, HEADS, HEAD_DIM)
    score_scale = HEAD_DIM ** (-0.5)
    scores = (
        jnp.einsum("gqhd,gkhd->ghqk", queries, key_part, preferred_element_type=jnp.float32)
        * score_scale
    )
    prob_rows = jnp.exp(scores - log_norm)
    grad_value = jnp.einsum(
        "ghqk,gqhd->gkhd",
        prob_rows.astype(jnp.bfloat16),
        grad_mixed,
        preferred_element_type=jnp.float32,
    )
    grad_probs = jnp.einsum(
        "gqhd,gkhd->ghqk", grad_mixed, value_part, preferred_element_type=jnp.float32
    )
    grad_scores = (
        prob_rows * (grad_probs - jnp.sum(prob_rows * grad_probs, axis=-1, keepdims=True))
    ).astype(jnp.bfloat16)
    grad_query = (
        jnp.einsum("ghqk,gkhd->gqhd", grad_scores, key_part, preferred_element_type=jnp.float32)
        * score_scale
    )
    grad_key = (
        jnp.einsum("ghqk,gqhd->gkhd", grad_scores, queries, preferred_element_type=jnp.float32)
        * score_scale
    )
    stacked = jnp.stack([grad_query, grad_key, grad_value], axis=2)
    return stacked.reshape(images * IMG_LEN, 3 * HEADS * HEAD_DIM)


def adam_update(weight, first_moment, second_moment, gradient, step_rate, decay_factor):
    first_new = beta_one * first_moment + (1.0 - beta_one) * gradient
    second_new = beta_two * second_moment + (1.0 - beta_two) * gradient * gradient
    first_hat = first_new / (1.0 - beta_one**STEP)
    second_hat = second_new / (1.0 - beta_two**STEP)
    weight_new = weight - step_rate * (
        first_hat / (jnp.sqrt(second_hat) + adam_eps) + decay_factor * weight
    )
    return (first_new, second_new, weight_new)


def general_body(
    x_in,
    cotangent,
    teacher,
    valid_mask,
    routes,
    gate_weights,
    norm_params,
    qkv_weight,
    out_weight,
    up_weight,
    down_weight,
    norm_first,
    norm_second,
    qkv_first,
    qkv_second,
    out_first,
    out_second,
    up_first,
    up_second,
    down_first,
    down_second,
):
    token_total = routes.shape[1]
    row_devices = lax.axis_size("row")
    col_devices = lax.axis_size("col")
    capacity = row_devices * (5 * token_total * TOP // (4 * EXPERTS) // row_devices)
    experts_here = EXPERTS // col_devices
    first_mine = lax.axis_index("col") * experts_here
    slot_share = capacity * experts_here // row_devices
    route_rows = jnp.stack([routes[k] for k in range(TOP)], axis=1)
    gate_rows = jnp.stack([gate_weights[k] for k in range(TOP)], axis=1)
    slot_token, slot_used, order_idx, slot_index, pick_slot = dispatch_tables(route_rows, capacity)
    slot_gate = (
        jnp.zeros((EXPERTS * capacity,), jnp.float32)
        .at[slot_index]
        .set(gate_rows.reshape(-1)[order_idx])
    )
    mine_token = jnp.transpose(
        lax.dynamic_slice_in_dim(slot_token.reshape(EXPERTS, capacity), first_mine, experts_here, 0)
    )
    mine_used = jnp.transpose(
        lax.dynamic_slice_in_dim(slot_used.reshape(EXPERTS, capacity), first_mine, experts_here, 0)
    ).astype(jnp.bfloat16)[:, :, None]
    mine_gate = jnp.transpose(
        lax.dynamic_slice_in_dim(slot_gate.reshape(EXPERTS, capacity), first_mine, experts_here, 0)
    )[:, :, None]
    pick_expert = pick_slot // capacity
    pick_owned = ((pick_expert >= first_mine) & (pick_expert < first_mine + experts_here)).astype(
        jnp.float32
    )
    pick_local = pick_slot % capacity * experts_here + jnp.clip(
        pick_expert - first_mine, 0, experts_here - 1
    )
    x_block, cot_block, teacher_block = (
        lax.all_to_all(x_in, "row", split_axis=1, concat_axis=0, tiled=True),
        lax.all_to_all(cotangent, "row", split_axis=1, concat_axis=0, tiled=True),
        lax.all_to_all(teacher, "row", split_axis=1, concat_axis=0, tiled=True),
    )
    stream = x_block.astype(jnp.float32)
    normed, normed_scaled, normed_inverse = norm_forward(stream, norm_params[0], norm_params[1])
    normed_low = normed.astype(jnp.bfloat16)
    normed_all = spread_cols(normed_low)
    qkv_low = qkv_weight.astype(jnp.bfloat16)

    def qkv_term(row_start, row_count):
        return jnp.dot(normed_all, qkv_low, preferred_element_type=jnp.float32)

    projected = sum_rows(qkv_term, token_total // row_devices)
    packed = to_heads(projected.astype(jnp.bfloat16))
    attended, log_norm = attend_local(packed)
    attended_rows = from_heads(attended.astype(jnp.bfloat16))
    attended_all = spread_rows(attended_rows)
    out_low = out_weight.astype(jnp.bfloat16)

    def out_term(row_start, row_count):
        return jnp.dot(attended_all, out_low, preferred_element_type=jnp.float32)

    middle = stream + sum_cols(out_term, token_total // col_devices)
    second, second_scaled, second_inverse = norm_forward(middle, norm_params[2], norm_params[3])
    second_low = second.astype(jnp.bfloat16)
    second_all = spread_cols(second_low)
    slot_rows = second_all[mine_token] * mine_used
    up_low = up_weight.astype(jnp.bfloat16)
    down_low = down_weight.astype(jnp.bfloat16)

    def up_term(row_start, row_count):
        return jnp.einsum(
            "ced,edf->cef", slot_rows, up_low, preferred_element_type=jnp.float32
        ).reshape(row_count, -1)

    hidden_pre = sum_rows(up_term, slot_share)
    hidden_low = gelu_tanh(hidden_pre).astype(jnp.bfloat16)
    hidden_all = spread_rows(hidden_low).reshape(capacity, experts_here, -1)
    expert_out = jnp.einsum(
        "cef,edf->ced", hidden_all, down_low, preferred_element_type=jnp.float32
    ).reshape(capacity * experts_here, -1)

    def combine_term(row_start, row_count):
        return jnp.sum(expert_out[pick_local] * (gate_rows * pick_owned)[:, :, None], axis=1)

    result = middle + sum_cols(combine_term, token_total // col_devices)
    valid_rows = valid_mask.astype(jnp.float32)[:, None]
    mismatch = result - teacher_block.astype(jnp.float32)
    square_sum, valid_sum = lax.psum(
        (jnp.sum(valid_rows * mismatch * mismatch), jnp.sum(valid_mask.astype(jnp.float32))),
        ("row", "col"),
    )
    valid_total = valid_sum / row_devices
    loss_value = square_sum / valid_total
    grad_out = cot_block.astype(jnp.float32) + 2.0 / valid_total * valid_rows * mismatch
    grad_all = spread_cols(grad_out.astype(jnp.bfloat16))
    grad_slots = (grad_all[mine_token] * mine_gate).astype(jnp.bfloat16)

    def hidden_term(row_start, row_count):
        return jnp.einsum(
            "ced,edf->cef", grad_slots, down_low, preferred_element_type=jnp.float32
        ).reshape(row_count, -1)

    grad_hidden = sum_rows(hidden_term, slot_share)
    gelu_value, gelu_pull = jax.vjp(gelu_tanh, hidden_pre)
    grad_pre = gelu_pull(grad_hidden)[0].astype(jnp.bfloat16)
    grad_pre_all = spread_rows(grad_pre).reshape(capacity, experts_here, -1)
    up_grad = jnp.einsum(
        "ced,cef->edf", slot_rows, grad_pre_all, preferred_element_type=jnp.float32
    )
    down_grad = jnp.einsum(
        "ced,cef->edf", grad_slots, hidden_all, preferred_element_type=jnp.float32
    )
    slot_input_grad = jnp.einsum(
        "cef,edf->ced", grad_pre_all, up_low, preferred_element_type=jnp.float32
    ).reshape(capacity * experts_here, -1)

    def back_combine(row_start, row_count):
        return jnp.sum(slot_input_grad[pick_local] * pick_owned[:, :, None], axis=1)

    grad_second = sum_cols(back_combine, token_total // col_devices)
    grad_middle_norm, second_gain_grad, second_shift_grad = norm_backward(
        grad_second, second_scaled, second_inverse, norm_params[2]
    )
    grad_middle = grad_out + grad_middle_norm
    grad_branch_all = spread_cols(grad_middle.astype(jnp.bfloat16))
    out_grad = jnp.einsum(
        "ti,to->io", attended_all, grad_branch_all, preferred_element_type=jnp.float32
    )

    def attended_term(row_start, row_count):
        return jnp.einsum("to,io->ti", grad_branch_all, out_low, preferred_element_type=jnp.float32)

    grad_attended = sum_rows(attended_term, token_total // row_devices)
    grad_packed = attend_back(packed, log_norm, to_heads(grad_attended.astype(jnp.bfloat16)))
    grad_proj_rows = from_heads(grad_packed.astype(jnp.bfloat16))
    grad_proj_all = spread_rows(grad_proj_rows)
    qkv_grad = jnp.einsum(
        "ti,to->io", normed_all, grad_proj_all, preferred_element_type=jnp.float32
    )

    def input_term(row_start, row_count):
        return jnp.einsum("to,io->ti", grad_proj_all, qkv_low, preferred_element_type=jnp.float32)

    grad_normed = sum_cols(input_term, token_total // col_devices)
    grad_stream_norm, first_gain_grad, first_shift_grad = norm_backward(
        grad_normed, normed_scaled, normed_inverse, norm_params[0]
    )
    input_block = grad_middle + grad_stream_norm
    norm_grad = lax.psum(
        jnp.stack([first_gain_grad, first_shift_grad, second_gain_grad, second_shift_grad], axis=0),
        "col",
    )
    mixed_block = result.astype(jnp.bfloat16).astype(jnp.float32)
    mixed_rows, input_grad = (
        lax.all_to_all(
            mixed_block.astype(jnp.bfloat16), "row", split_axis=0, concat_axis=1, tiled=True
        ).astype(mixed_block.dtype),
        lax.all_to_all(
            input_block.astype(jnp.bfloat16), "row", split_axis=0, concat_axis=1, tiled=True
        ).astype(input_block.dtype),
    )
    mixed_out = mixed_rows.astype(jnp.bfloat16)
    norm_one, norm_two, norm_new = adam_update(
        norm_params, norm_first, norm_second, norm_grad, rate_norm, 0.0
    )
    qkv_one, qkv_two, qkv_new = adam_update(
        qkv_weight, qkv_first, qkv_second, qkv_grad, rate_qkv, decay_matrix
    )
    out_one, out_two, out_new = adam_update(
        out_weight, out_first, out_second, out_grad, rate_out, decay_matrix
    )
    up_one, up_two, up_new = adam_update(
        up_weight, up_first, up_second, up_grad, rate_up, decay_matrix
    )
    down_one, down_two, down_new = adam_update(
        down_weight, down_first, down_second, down_grad, rate_down, decay_matrix
    )
    return (
        mixed_out,
        input_grad,
        loss_value,
        norm_one,
        norm_two,
        norm_new,
        qkv_one,
        qkv_two,
        qkv_new,
        out_one,
        out_two,
        out_new,
        up_one,
        up_two,
        up_new,
        down_one,
        down_two,
        down_new,
    )


def round_up(value, unit):
    return -(-value // unit) * unit


def mxu(lhs, rhs):
    return jnp.dot(lhs, rhs, preferred_element_type=jnp.float32)


def mxu_nt(lhs, rhs):
    return lax.dot_general(lhs, rhs, (((1,), (1,)), ((), ())), preferred_element_type=jnp.float32)


def mxu_tn(lhs, rhs):
    return lax.dot_general(lhs, rhs, (((0,), (0,)), ((), ())), preferred_element_type=jnp.float32)


def low(values):
    return values.astype(jnp.bfloat16)


def kernel_params(**more):
    return pltpu.CompilerParams(vmem_limit_bytes=VMEM_BYTES, **more)


def cost(micros):
    return pl.CostEstimate(
        flops=int(1.1e9 * micros), bytes_accessed=int(3.5e6 * micros), transcendentals=0
    )


def iota(shape, dim):
    return lax.broadcasted_iota(jnp.int32, shape, dim)


def strict(size, lower):
    row = iota((size, size), 0)
    col = iota((size, size), 1)
    return low(((col < row) if lower else (row < col)).astype(jnp.float32))


def column_sums(matrix, column):
    return mxu(matrix, low(jnp.broadcast_to(column, (column.shape[0], 128))))[:, 0:1]


def route_kernel(
    cap, block, tokens, chunk, mine_ref, all_ref, own_ref, extra_ref, order_ref,
    rows_ref, cols_ref, pick_ref, excess_ref,
):
    spare = block - 1
    padded = own_ref.shape[1]
    expert_ids = iota((EXPERTS, padded), 0)
    before = strict(padded, False)
    first = own_ref[0:1, :]
    second = own_ref[1:2, :]
    first_hot = (expert_ids == first).astype(jnp.float32)
    second_hot = (expert_ids == second).astype(jnp.float32)
    first_rank = jnp.sum(first_hot * mxu(low(first_hot), before), axis=0, keepdims=True)
    first_load = jnp.sum(first_hot, axis=1, keepdims=True)
    second_rank = jnp.sum(
        second_hot * (mxu(low(second_hot), before) + first_load), axis=0, keepdims=True
    )
    own_over = jnp.maximum(first_load + jnp.sum(second_hot, axis=1, keepdims=True) - cap, 0.0)
    own_base = column_sums(strict(EXPERTS, True), own_over)

    def slot_of(expert, rank, hot):
        extra = jnp.sum(hot * own_base, axis=0, keepdims=True) + rank - cap
        last = jnp.where(extra < spare, EXPERTS * cap + extra, -1.0)
        slot = jnp.where(rank < cap, expert.astype(jnp.float32) * cap + rank, last)
        return jnp.where(expert >= 0, slot, -1.0)

    row = iota((8, padded), 0)
    table = jnp.where(
        row == 0,
        slot_of(first, first_rank, first_hot),
        jnp.where(row == 1, slot_of(second, second_rank, second_hot), extra_ref[...]),
    )
    rows_ref[...] = table
    cols_ref[...] = jnp.transpose(table)

    devices = order_ref.shape[1]
    length = all_ref.shape[1]
    owner = iota((devices, chunk), 0) * tokens
    place = iota((devices, chunk), 1)
    chunk_ids = iota((EXPERTS, chunk), 0)

    def add_chunk(step, total):
        start = step * chunk
        part = all_ref[:, pl.ds(pl.multiple_of(start, chunk), chunk)]
        hot = (chunk_ids == part[0:1, :]).astype(jnp.float32) + (chunk_ids == part[1:2, :]).astype(
            jnp.float32
        )
        position = place + start
        member = ((position >= owner) & (position < owner + tokens)).astype(jnp.float32)
        return total + mxu_nt(low(member), low(hot))

    loads = lax.fori_loop(
        0, length // chunk, add_chunk, jnp.zeros((devices, EXPERTS), jnp.float32)
    )
    over = jnp.maximum(loads - cap, 0.0)
    room = pick_ref.shape[0]
    by_device = jnp.max(jnp.sum(over, axis=1, keepdims=True), axis=0, keepdims=True) - spare
    by_expert = jnp.max(jnp.sum(over, axis=0, keepdims=True), axis=1, keepdims=True) - room
    excess_ref[...] = jnp.broadcast_to(jnp.maximum(by_device, by_expert), excess_ref.shape)
    turned = low((iota((devices, devices), 0) == order_ref[...]).astype(jnp.float32))
    over = mxu(turned, low(jnp.minimum(over, 256.0)))
    base = mxu(low(over), strict(EXPERTS, False))
    mine = iota((devices, EXPERTS), 1) == mine_ref[0]
    over_mine = jnp.sum(jnp.where(mine, over, 0.0), axis=1, keepdims=True)
    base_mine = jnp.sum(jnp.where(mine, base, 0.0), axis=1, keepdims=True)
    start_mine = column_sums(strict(devices, True), over_mine)
    width = 256
    for part in range(devices * block // width):
        inner = iota((devices, width), 1) + part * width - iota((devices, width), 0) * block
        inside = (inner >= 0) & (inner < spare)

        def spread(column):
            return jnp.sum(jnp.where(inside, column, 0.0), axis=0, keepdims=True)

        offset = spread(inner.astype(jnp.float32) - base_mine)
        used = (offset >= 0.0) & (offset < spread(over_mine))
        target = jnp.where(used, offset + spread(start_mine), -1.0)
        pick_ref[:, part * width : (part + 1) * width] = low(
            (iota((room, width), 0).astype(jnp.float32) == target).astype(jnp.float32)
        )


def route_call(cap, spare, room, tokens, mine, all_routes, own_routes, extra, order):
    padded = own_routes.shape[1]
    devices = order.shape[1]
    spec = pl.BlockSpec(memory_space=pltpu.VMEM)
    return pl.pallas_call(
        functools.partial(route_kernel, cap, spare, tokens, 2048),
        in_specs=[pl.BlockSpec(memory_space=pltpu.SMEM)] + [spec] * 4,
        out_shape=(
            jax.ShapeDtypeStruct((8, padded), jnp.float32),
            jax.ShapeDtypeStruct((padded, 8), jnp.float32),
            jax.ShapeDtypeStruct((room, devices * spare), jnp.bfloat16),
            jax.ShapeDtypeStruct((8, 128), jnp.float32),
        ),
        compiler_params=kernel_params(),
        cost_estimate=cost(4),
        name="route",
    )(mine, all_routes, own_routes, extra, order)


def norm_stats(stream):
    center = jnp.mean(stream, axis=1, keepdims=True)
    offset = stream - center
    spread = jnp.mean(offset * offset, axis=1, keepdims=True)
    inverse = lax.rsqrt(spread + norm_eps)
    return offset * inverse, inverse


def norm_pull(upstream, scaled, inverse, gain_row):
    dscaled = upstream * gain_row
    plain = jnp.mean(dscaled, axis=1, keepdims=True)
    cross = jnp.mean(dscaled * scaled, axis=1, keepdims=True)
    return (dscaled - plain - scaled * cross) * inverse


def crop_to(result, padded):
    for image in range(padded.shape[0] // IMG_PAD):
        result[image * IMG_LEN : (image + 1) * IMG_LEN, :] = padded[
            image * IMG_PAD : image * IMG_PAD + IMG_LEN, :
        ]


def half_mask(shape, half):
    lane = iota(shape, 1)
    return (lane < HEAD_DIM) if half == 0 else (lane >= HEAD_DIM)


def pick_half(tile, half):
    return jnp.where(half_mask(tile.shape, half), tile, jnp.zeros_like(tile))


class Staged:
    def __init__(self, ins, in_bufs, in_sems, outs, out_bufs, out_sems):
        self.copies = [
            pltpu.make_async_copy(source, buffer, in_sems.at[index])
            for index, (source, buffer) in enumerate(zip(ins, in_bufs))
        ]
        self.in_bufs = in_bufs
        self.out_bufs = out_bufs
        self.outs = outs
        self.out_sems = out_sems
        self.open = set()
        self.sent = []

    def begin(self):
        for index, copy in enumerate(self.copies):
            copy.start()
            self.open.add(index)

    def need(self, index):
        if index in self.open:
            self.copies[index].wait()
            self.open.remove(index)
        return self.in_bufs[index]

    def ship(self, index, source=None):
        copy = pltpu.make_async_copy(
            self.out_bufs[index] if source is None else source,
            self.outs[index],
            self.out_sems.at[index],
        )
        copy.start()
        self.sent.append(copy)

    def end(self):
        for index in sorted(self.open):
            self.copies[index].wait()
        for copy in self.sent:
            copy.wait()


def staged_call(kernel_fn, name, micros, scalars, inputs, outs, scratch):
    outs = [jax.ShapeDtypeStruct(shape, kind) for shape, kind in outs]
    counts = (len(scalars), len(inputs), len(outs))

    def kernel(*refs):
        scalar_refs, refs = refs[: counts[0]], refs[counts[0] :]
        ins, refs = refs[: counts[1]], refs[counts[1] :]
        results, refs = refs[: counts[2]], refs[counts[2] :]
        in_bufs, refs = refs[: counts[1]], refs[counts[1] :]
        out_bufs, refs = refs[: counts[2]], refs[counts[2] :]
        in_sems, out_sems, *others = refs
        stage = Staged(ins, in_bufs, in_sems, results, out_bufs, out_sems)
        stage.begin()
        kernel_fn(stage, scalar_refs, others)
        stage.end()

    anywhere = pl.BlockSpec(memory_space=pltpu.HBM)
    return pl.pallas_call(
        kernel,
        in_specs=[pl.BlockSpec(memory_space=pltpu.SMEM)] * counts[0]
        + [anywhere] * counts[1],
        out_specs=[anywhere] * counts[2],
        out_shape=outs,
        scratch_shapes=[pltpu.VMEM(a.shape, a.dtype) for a in inputs]
        + [pltpu.VMEM(a.shape, a.dtype) for a in outs]
        + [pltpu.SemaphoreType.DMA((counts[1],)), pltpu.SemaphoreType.DMA((counts[2],))]
        + scratch,
        compiler_params=kernel_params(),
        cost_estimate=cost(micros),
        name=name,
    )(*scalars, *inputs)


def unpack_block(block, col, row, cols, rows, qkv_ref, out_ref, norm_ref):
    width = norm_ref.shape[1]
    deep = width // rows
    qkv_rows = 3 * width // cols
    out_rows = width // cols
    lanes = pl.ds(row * deep, deep)
    qkv_ref[pl.ds(col * qkv_rows, qkv_rows), lanes] = block[0:qkv_rows, :]
    out_ref[pl.ds(col * out_rows, out_rows), lanes] = block[qkv_rows : qkv_rows + out_rows, :]
    tail = block[qkv_rows + out_rows : qkv_rows + out_rows + 16, :].astype(jnp.float32)
    if col == 0:
        norm_ref[0:4, lanes] = tail[0:4] + tail[4:8] + tail[8:12]


def one_hot(slot_cols, slots, start=0):
    place = (iota((slot_cols[0].shape[0], slots), 1) + start).astype(jnp.float32)
    hot = place == slot_cols[0]
    for column in slot_cols[1:]:
        hot = hot | (place == column)
    return low(hot.astype(jnp.float32))


def collect(slot_cols, recv_ref, extra_ref):
    slots = recv_ref.shape[0]
    return mxu(one_hot(slot_cols, slots), recv_ref[...]) + mxu(
        one_hot(slot_cols, extra_ref.shape[0], slots), extra_ref[...]
    )


def front_kernel(cols, rows, stage, scalar_refs, scratch):
    (order_ref,) = scalar_refs
    pack_refs = stage.need(0), stage.need(1)
    qkv_ref, out_ref, norm_ref, proj_ref, att_ref, probs_ref, middle_ref, send_ref, extra_ref = (
        stage.out_bufs[:9]
    )
    width = norm_ref.shape[1]
    norm_ref[...] = jnp.zeros_like(norm_ref)
    held = pack_refs[0].shape[0]
    pack_buf = scratch[0]
    pack_buf[0:held] = pack_refs[0][...]
    pack_buf[held:] = pack_refs[1][...]
    for col in range(cols):
        for row in range(rows):
            block = pack_buf[order_ref[col * rows + row]]
            unpack_block(block, col, row, cols, rows, qkv_ref, out_ref, norm_ref)
    for index in range(3):
        stage.ship(index)
    x_ref = stage.need(2)
    images = x_ref.shape[0] // IMG_PAD
    stream = x_ref[...].astype(jnp.float32)
    scaled, inverse = norm_stats(stream)
    scaled_ref, scaled_two_ref, inverse_ref, normed_ref = stage.out_bufs[9:]
    scaled_ref[...] = scaled
    stage.ship(9)
    normed = low(scaled * norm_ref[0:1, :] + norm_ref[1:2, :])
    normed_ref[...] = normed
    stage.ship(12)
    proj_ref[...] = low(mxu_nt(normed, qkv_ref[...]))
    stage.ship(3)
    key_ok = iota((IMG_PAD, IMG_PAD), 0) < IMG_LEN
    for image in range(images):
        span = slice(image * IMG_PAD, (image + 1) * IMG_PAD)
        for pair in range(HEADS // 2):
            lanes = slice(pair * 128, (pair + 1) * 128)
            queries = proj_ref[span, lanes]
            keys = proj_ref[span, width + pair * 128 : width + (pair + 1) * 128]
            values_t = jnp.transpose(
                proj_ref[span, 2 * width + pair * 128 : 2 * width + (pair + 1) * 128]
            )
            mixed = []
            for half in range(2):
                scores = mxu_nt(pick_half(keys, half), queries) * HEAD_DIM**-0.5
                scores = jnp.where(key_ok, scores, -1e30)
                top = jnp.max(scores, axis=0, keepdims=True)
                shifted = jnp.exp(scores - top)
                total = jnp.sum(shifted, axis=0, keepdims=True)
                probs = low(shifted * (1.0 / total))
                head = image * HEADS + pair * 2 + half
                probs_ref[head * IMG_PAD : (head + 1) * IMG_PAD, :] = probs
                mixed.append(mxu(values_t[half * HEAD_DIM : (half + 1) * HEAD_DIM, :], probs))
            att_ref[span, lanes] = low(jnp.transpose(jnp.concatenate(mixed, axis=0)))
    stage.ship(4)
    stage.ship(5)
    middle = stream + mxu(att_ref[...], out_ref[...])
    middle_ref[...] = middle
    stage.ship(6)
    table_ref = stage.need(3)
    scaled_two, inverse_two = norm_stats(middle)
    scaled_two_ref[...] = scaled_two
    stage.ship(10)
    lane = iota((inverse.shape[0], 8), 1)
    inverse_ref[...] = jnp.where(lane == 0, inverse, inverse_two)
    stage.ship(11)
    second = low(scaled_two * norm_ref[2:3, :] + norm_ref[3:4, :])
    for start, size, result in slot_parts(send_ref, extra_ref):
        place = (iota((size, table_ref.shape[1]), 0) + start).astype(jnp.float32)
        hot = (place == table_ref[0:1, :]) | (place == table_ref[1:2, :])
        rows_out = mxu(low(hot.astype(jnp.float32)), second)
        if result is extra_ref:
            count = jnp.sum(table_ref[4:5, :], axis=1, keepdims=True)
            first_part = jnp.minimum(count, 256.0)
            rows_out = last_row(rows_out, (first_part, count - first_part))
        result[...] = low(rows_out)
    stage.ship(7)
    stage.ship(8)


def last_row(rows, values):
    lane = iota(rows.shape, 1)
    split = jnp.zeros_like(rows)
    for index, value in enumerate(values):
        split = jnp.where(lane == index, value, split)
    return jnp.where(iota(rows.shape, 0) == rows.shape[0] - 1, split, rows)


def slot_parts(send_ref, extra_ref):
    slots = send_ref.shape[0]
    size = min(512, slots)
    parts = [(start, size, send_ref.at[start : start + size]) for start in range(0, slots, size)]
    return parts + [(slots, extra_ref.shape[0], extra_ref)]


def front_call(cols, rows, slots, spare, order, x_pad, packs, table):
    tokens, width = x_pad.shape
    images = tokens // IMG_PAD
    half, full = jnp.bfloat16, jnp.float32
    outs = staged_call(
        functools.partial(front_kernel, cols, rows),
        "front",
        11,
        [order],
        [*packs, x_pad, table],
        [
            ((3 * width, width), half),
            ((width, width), half),
            ((8, width), full),
            ((tokens, 3 * width), half),
            ((tokens, width), half),
            ((images * HEADS * IMG_PAD, IMG_PAD), half),
            ((tokens, width), full),
            ((slots, width), half),
            ((spare, width), half),
            ((tokens, width), full),
            ((tokens, width), full),
            ((tokens, 8), full),
            ((tokens, width), half),
        ],
        [pltpu.VMEM((cols * rows, *packs[0].shape[1:]), half)],
    )
    qkv, out, norms, proj, att, probs, middle, send, extra, *stats = outs
    return send, extra, middle, proj, att, probs, qkv, out, norms, stats


def weight_copies(row_ref, piece_refs, buffer, sems):
    deep = piece_refs[0].shape[0]
    return [
        pltpu.make_async_copy(
            piece,
            buffer.at[pl.ds(pl.multiple_of(row_ref[index] * deep, deep), deep), :],
            sems.at[index],
        )
        for index, piece in enumerate(piece_refs)
    ]


GELU_A = 0.7978845608028654
GELU_B = 0.044715


def gelu_low(pre):
    inner = pre * (GELU_A + GELU_A * GELU_B * (pre * pre))
    half = 0.5 * pre
    return low(half + half * jnp.tanh(inner))


def gelu_both(pre):
    square = pre * pre
    curve = jnp.tanh(pre * (GELU_A + GELU_A * GELU_B * square))
    half = 0.5 * pre
    value = half + half * curve
    slope = 0.5 + 0.5 * curve + half * (1.0 - curve * curve) * (
        GELU_A + 3.0 * GELU_A * GELU_B * square
    )
    return low(value), low(slope)


def ff_chunks(width):
    size = min(width, 512)
    return [slice(start, start + size) for start in range(0, width, size)]


def row_blocks(rows, spare_rows):
    size = min(512, rows)
    blocks = [slice(start, start + size) for start in range(0, rows, size)]
    blocks[-1] = slice(blocks[-1].start, rows + spare_rows)
    return blocks


def spare_chunks(rows):
    size = min(rows, 1024)
    return [slice(start, start + size) for start in range(0, rows, size)]


def pick_rows(pick_ref, extra_ref):
    total = None
    for part in spare_chunks(extra_ref.shape[0]):
        term = mxu(pick_ref[:, part], extra_ref[part, :])
        total = term if total is None else total + term
    return low(total)


def place_rows(pick_ref, rows, kept_ref, sent_ref):
    half = kept_ref.shape[0]
    for start, result in ((0, kept_ref), (half, sent_ref)):
        for part in spare_chunks(half):
            source = slice(start + part.start, start + part.stop)
            result[part, :] = low(mxu_tn(pick_ref[:, source], rows))


def expert_rows(rows_in, up_buf, wait_down, down_buf):
    hiddens = [gelu_low(mxu(rows_in, up_buf[:, part])) for part in ff_chunks(up_buf.shape[1])]
    wait_down()
    total = None
    for part, hidden in zip(ff_chunks(up_buf.shape[1]), hiddens):
        term = mxu_nt(hidden, down_buf[:, part])
        total = term if total is None else total + term
    return low(total)


def pull_rows(grads_in, slope_ref, rows, up_buf, wait_up, down_buf, pre_ref):
    parts = ff_chunks(up_buf.shape[1])
    for part in parts:
        slope = slope_ref[rows, part].astype(jnp.float32)
        pre_ref[rows, part] = low(mxu(grads_in, down_buf[:, part]) * slope)
    wait_up()
    total = None
    for part in parts:
        term = mxu_nt(pre_ref[rows, part], up_buf[:, part])
        total = term if total is None else total + term
    return low(total)


def expert_kernel(pull, pieces, row_ref, main_ref, extra_ref, pick_ref, *rest):
    if pull:
        slope_ref, *rest = rest
    ups, downs, rest = rest[:pieces], rest[pieces : 2 * pieces], rest[2 * pieces :]
    send_ref, kept_ref, sent_ref, rows_ref, *rest = rest
    if pull:
        pre_ref, slope_buf, pre_buf, *rest = rest
    extra_buf, pick_buf, kept_buf, sent_buf, rows_buf, total_buf, up_buf, down_buf, *sems = rest
    up_sems, down_sems, in_sems, out_sems = sems
    main = main_ref.shape[0]
    blocks = row_blocks(main, rows_buf.shape[0] - main)
    inner = [slice(rows.start, min(rows.stop, main)) for rows in blocks]

    def part_of(ref, rows):
        return ref.at[rows.start : rows.stop, :]

    def copy_in(source, target, index):
        return pltpu.make_async_copy(source, target, in_sems.at[index])

    up_copies = weight_copies(row_ref, ups, up_buf, up_sems)
    down_copies = weight_copies(row_ref, downs, down_buf, down_sems)
    first_weights, last_weights = (
        (down_copies, up_copies) if pull else (up_copies, down_copies)
    )
    count = len(blocks)
    late_copies = [
        copy_in(extra_ref, extra_buf, 0),
        copy_in(pick_ref, pick_buf, 1),
    ]
    slope_copies = [
        copy_in(part_of(slope_ref, rows), part_of(slope_buf, rows), 2 + index)
        for index, rows in enumerate(blocks)
    ] if pull else []
    for copy in [*first_weights, *slope_copies[:1], *last_weights, *late_copies, *slope_copies[1:]]:
        copy.start()
    rows_buf[0:main, :] = main_ref[...]
    for copy in first_weights:
        copy.wait()
    sent = []

    def send_out(source, target):
        copy = pltpu.make_async_copy(source, target, out_sems.at[len(sent)])
        copy.start()
        sent.append(copy)

    for index, rows in enumerate(blocks):
        if index == count - 1:
            for copy in late_copies:
                copy.wait()
            rows_buf[main:, :] = pick_rows(pick_buf, extra_buf)
            send_out(rows_buf, rows_ref)

        def wait_last():
            if index == 0:
                for copy in last_weights:
                    copy.wait()

        if pull:
            slope_copies[index].wait()
            total = pull_rows(rows_buf[rows, :], slope_buf, rows, up_buf, wait_last, down_buf, pre_buf)
            send_out(part_of(pre_buf, rows), part_of(pre_ref, rows))
        else:
            total = expert_rows(rows_buf[rows, :], up_buf, wait_last, down_buf)
        total_buf[rows, :] = total
        send_out(part_of(total_buf, inner[index]), part_of(send_ref, inner[index]))
    place_rows(pick_buf, total_buf[main:, :], kept_buf, sent_buf)
    send_out(kept_buf, kept_ref)
    send_out(sent_buf, sent_ref)
    for copy in sent:
        copy.wait()


def expert_call(name, rowpos, main, extra, pick, slope, ups, downs):
    slots, width = main.shape
    ff = ups[0].shape[1]
    rows = slots + pick.shape[0]
    blocks = len(row_blocks(slots, pick.shape[0]))
    pull = slope is not None
    half = (extra.shape[0] // 2, width)
    anywhere = pl.BlockSpec(memory_space=pltpu.HBM)
    inputs = [main, extra, pick] + ([slope] if pull else [])
    outs = [(slots, width), half, half, (rows, width)] + ([(rows, ff)] if pull else [])

    def buffer(shape):
        return pltpu.VMEM(shape, jnp.bfloat16)

    return pl.pallas_call(
        functools.partial(expert_kernel, pull, len(ups)),
        in_specs=[
            pl.BlockSpec(memory_space=pltpu.SMEM),
            pl.BlockSpec(memory_space=pltpu.VMEM),
        ]
        + [anywhere] * (len(inputs) - 1 + 2 * len(ups)),
        out_specs=[anywhere] * len(outs),
        out_shape=[jax.ShapeDtypeStruct(shape, jnp.bfloat16) for shape in outs],
        scratch_shapes=([buffer((rows, ff))] * 2 if pull else [])
        + [buffer(extra.shape), buffer(pick.shape), buffer(half), buffer(half)]
        + [buffer((rows, width))] * 2
        + [buffer((width, ff))] * 2
        + [
            pltpu.SemaphoreType.DMA((len(ups),)),
            pltpu.SemaphoreType.DMA((len(ups),)),
            pltpu.SemaphoreType.DMA((blocks + 2,)),
            pltpu.SemaphoreType.DMA((2 * blocks + 3,)),
        ],
        compiler_params=kernel_params(),
        cost_estimate=cost(12),
        name=name,
    )(rowpos, *inputs, *ups, *downs)


def hidden_kernel(pieces, row_ref, rows_ref, *rest):
    ups = rest[:pieces]
    hidden_ref, slope_ref, up_buf, sems = rest[pieces:]

    @pl.when(pl.program_id(0) == 0)
    def _():
        copies = weight_copies(row_ref, ups, up_buf, sems)
        for copy in copies:
            copy.start()
        for copy in copies:
            copy.wait()

    rows_in = rows_ref[...]
    for part in ff_chunks(up_buf.shape[1]):
        hidden, slope = gelu_both(mxu(rows_in, up_buf[:, part]))
        hidden_ref[:, part] = hidden
        slope_ref[:, part] = slope


def hidden_call(rowpos, slot_rows, ups):
    rows, width = slot_rows.shape
    ff = ups[0].shape[1]
    block = 384 if rows % 384 == 0 else 128
    wide = pl.BlockSpec((block, ff), lambda i: (i, 0))
    return pl.pallas_call(
        functools.partial(hidden_kernel, len(ups)),
        grid=(rows // block,),
        in_specs=[
            pl.BlockSpec(memory_space=pltpu.SMEM),
            pl.BlockSpec((block, width), lambda i: (i, 0)),
        ]
        + [pl.BlockSpec(memory_space=pl.ANY)] * len(ups),
        out_specs=[wide, wide],
        out_shape=[jax.ShapeDtypeStruct((rows, ff), jnp.bfloat16)] * 2,
        scratch_shapes=[
            pltpu.VMEM((width, ff), jnp.bfloat16),
            pltpu.SemaphoreType.DMA((len(ups),)),
        ],
        compiler_params=kernel_params(dimension_semantics=("arbitrary",)),
        cost_estimate=cost(3),
        name="hidden",
    )(rowpos, slot_rows, *ups)


WG_PART = 1024


def weight_grad_kernel(pieces, row_ref, left_ref, right_ref, *rest):
    results = rest[:pieces]
    left_buf, total_buf = rest[pieces:]
    deep = results[0].shape[0]

    @pl.when(pl.program_id(0) == 0)
    def _():
        left_buf[...] = jnp.transpose(left_ref[...])

    total_buf[...] = low(mxu(left_buf[...], right_ref[...]))
    for index, result in enumerate(results):
        start = pl.multiple_of(row_ref[index] * deep, deep)
        result[...] = total_buf[pl.ds(start, deep), :]


def weight_grad_call(rowpos, left, right, deep):
    rows, width = left.shape
    ff = right.shape[1]
    pieces = width // deep
    part = min(ff, WG_PART)
    return pl.pallas_call(
        functools.partial(weight_grad_kernel, pieces),
        grid=(ff // part,),
        in_specs=[
            pl.BlockSpec(memory_space=pltpu.SMEM),
            pl.BlockSpec((rows, width), lambda i: (0, 0)),
            pl.BlockSpec((rows, part), lambda i: (0, i)),
        ],
        out_specs=[pl.BlockSpec((deep, part), lambda i: (0, i))] * pieces,
        out_shape=[jax.ShapeDtypeStruct((deep, ff), jnp.bfloat16)] * pieces,
        scratch_shapes=[
            pltpu.VMEM((width, rows), jnp.bfloat16),
            pltpu.VMEM((width, part), jnp.bfloat16),
        ],
        compiler_params=kernel_params(dimension_semantics=("arbitrary",)),
        cost_estimate=cost(2),
        name="weight_grad",
    )(rowpos, left, right)


def turn_kernel(stage, scalar_refs, scratch):
    recv_ref, back_ref, cols_ref = (stage.need(index) for index in range(3))
    mixed_ref, grad_ref, send_ref, extra_ref = stage.out_bufs
    first = collect([cols_ref[:, 0:1]], recv_ref, back_ref)
    second = collect([cols_ref[:, 1:2]], recv_ref, back_ref)
    middle_ref, teacher_ref, cot_ref, valid_ref, table_ref = (
        stage.need(index) for index in range(3, 8)
    )
    result = middle_ref[...] + cols_ref[:, 2:3] * first + cols_ref[:, 3:4] * second
    crop_to(scratch[0], result)
    mixed_ref[...] = low(scratch[0][...])
    stage.ship(0)
    mismatch = result - teacher_ref[...].astype(jnp.float32)
    masked = cols_ref[:, 4:5] * mismatch
    valid_total = valid_ref[...]
    squares = jnp.sum(masked * mismatch, axis=0, keepdims=True)
    square_sum = jnp.sum(squares, axis=1, keepdims=True)
    grad_out = cot_ref[...].astype(jnp.float32) + (2.0 / valid_total) * masked
    grad_ref[...] = grad_out
    stage.ship(1)
    rounded = low(grad_out).astype(jnp.float32)
    both = jnp.concatenate(
        [low(cols_ref[:, 2:3] * rounded), low(cols_ref[:, 3:4] * rounded)], axis=0
    )
    for start, size, part in slot_parts(send_ref, extra_ref):
        place = (iota((size, table_ref.shape[1]), 0) + start).astype(jnp.float32)
        hot = jnp.concatenate(
            [
                low((place == table_ref[0:1, :]).astype(jnp.float32)),
                low((place == table_ref[1:2, :]).astype(jnp.float32)),
            ],
            axis=1,
        )
        rows = mxu(hot, both)
        if part is extra_ref:
            top = low(square_sum).astype(jnp.float32)
            rest = square_sum - top
            middle = low(rest).astype(jnp.float32)
            rows = last_row(rows, (top, middle, rest - middle))
        part[...] = low(rows)
    stage.ship(2)
    stage.ship(3)


def turn_call(recv, back, cols, table, middle, teacher, cot, valid):
    half, full = jnp.bfloat16, jnp.float32
    own = (middle.shape[0] // IMG_PAD * IMG_LEN, middle.shape[1])
    mixed, grad_out, send, extra = staged_call(
        turn_kernel,
        "turn",
        6,
        [],
        [recv, back, cols, middle, teacher, cot, valid, table],
        [(own, half), (middle.shape, full), (recv.shape, half), (back.shape, half)],
        [pltpu.VMEM(own, full)],
    )
    return send, extra, mixed, grad_out


def back_kernel(cols_n, rows_n, stage, scalar_refs, scratch):
    (order_ref,) = scalar_refs
    gproj_buf, gatt_buf, gqkv_buf, gout_buf, gnorm_buf, pack_buf = scratch
    input_ref = stage.out_bufs[0]
    recv_ref, back_ref, cols_ref = (stage.need(index) for index in range(3))
    width = recv_ref.shape[1]
    grad_second = collect([cols_ref[:, 0:1], cols_ref[:, 1:2]], recv_ref, back_ref)
    scaled_two_ref, norm_ref, grad_ref, inverse_ref = (
        stage.need(index) for index in range(3, 7)
    )
    images = scaled_two_ref.shape[0] // IMG_PAD
    scaled_two, inverse_two = scaled_two_ref[...], inverse_ref[:, 1:2]
    gnorm_buf[...] = jnp.zeros_like(gnorm_buf)
    gnorm_buf[2:3, :] = jnp.sum(grad_second * scaled_two, axis=0, keepdims=True)
    gnorm_buf[3:4, :] = jnp.sum(grad_second, axis=0, keepdims=True)
    grad_middle = grad_ref[...] + norm_pull(grad_second, scaled_two, inverse_two, norm_ref[2:3, :])
    middle_low = low(grad_middle)
    att_ref, out_ref = stage.need(7), stage.need(8)
    gout_buf[...] = low(mxu(jnp.transpose(att_ref[...]), middle_low))
    proj_ref, probs_ref = stage.need(9), stage.need(10)
    gatt_buf[...] = low(mxu_nt(middle_low, out_ref[...]))
    scale = HEAD_DIM**-0.5
    for image in range(images):
        span = slice(image * IMG_PAD, (image + 1) * IMG_PAD)
        for pair in range(HEADS // 2):
            q_lanes = slice(pair * 128, (pair + 1) * 128)
            k_lanes = slice(width + pair * 128, width + (pair + 1) * 128)
            v_lanes = slice(2 * width + pair * 128, 2 * width + (pair + 1) * 128)
            queries = proj_ref[span, q_lanes]
            keys = proj_ref[span, k_lanes]
            values = proj_ref[span, v_lanes]
            upstream = gatt_buf[span, q_lanes]
            keys_t = jnp.transpose(keys)
            query_parts = []
            key_parts = []
            value_parts = []
            for half in range(2):
                head = image * HEADS + pair * 2 + half
                probs_low = probs_ref[head * IMG_PAD : (head + 1) * IMG_PAD, :]
                probs = probs_low.astype(jnp.float32)
                grad_probs = mxu_nt(pick_half(values, half), upstream)
                inner = jnp.sum(probs * grad_probs, axis=0, keepdims=True)
                grad_scores = low(probs * (grad_probs - inner))
                value_parts.append(mxu(probs_low, upstream))
                key_parts.append(mxu(grad_scores, queries))
                query_parts.append(
                    mxu(keys_t[half * HEAD_DIM : (half + 1) * HEAD_DIM, :], grad_scores)
                )
            left = half_mask(key_parts[0].shape, 0)
            gproj_buf[span, q_lanes] = low(
                jnp.transpose(jnp.concatenate(query_parts, axis=0)) * scale
            )
            gproj_buf[span, k_lanes] = low(jnp.where(left, key_parts[0], key_parts[1]) * scale)
            gproj_buf[span, v_lanes] = low(jnp.where(left, value_parts[0], value_parts[1]))
    normed_ref, qkv_ref, scaled_ref = (stage.need(index) for index in range(11, 14))
    scaled, inverse = scaled_ref[...], inverse_ref[:, 0:1]
    gqkv_buf[...] = low(mxu(jnp.transpose(gproj_buf[...]), normed_ref[...]))
    grad_normed = mxu(gproj_buf[...], qkv_ref[...])
    gnorm_buf[0:1, :] = jnp.sum(grad_normed * scaled, axis=0, keepdims=True)
    gnorm_buf[1:2, :] = jnp.sum(grad_normed, axis=0, keepdims=True)
    crop_to(input_ref, grad_middle + norm_pull(grad_normed, scaled, inverse, norm_ref[0:1, :]))
    stage.ship(0)
    deep = width // rows_n
    qkv_rows = 3 * width // cols_n
    out_rows = width // cols_n
    for col in range(cols_n):
        for row in range(rows_n):
            index = order_ref[col * rows_n + row]
            lanes = slice(row * deep, (row + 1) * deep)
            qkv_part = gqkv_buf[col * qkv_rows : (col + 1) * qkv_rows, lanes]
            out_part = gout_buf[col * out_rows : (col + 1) * out_rows, lanes]
            norm_part = low(gnorm_buf[:, lanes])
            pack_buf[index, 0:qkv_rows, :] = qkv_part
            pack_buf[index, qkv_rows : qkv_rows + out_rows, :] = out_part
            pack_buf[index, qkv_rows + out_rows : qkv_rows + out_rows + 16, :] = norm_part
    half = pack_buf.shape[0] // 2
    stage.ship(2, pack_buf.at[half:])
    stage.ship(1, pack_buf.at[:half])


def back_call(
    cols_n, rows_n, order, recv, back, cols, stats, grad_out, proj, att, probs, qkv, out, norms
):
    scaled, scaled_two, inverse, normed = stats
    tokens, width = scaled.shape
    blocks = cols_n * rows_n
    block = (blocks // 2, 4 * width // cols_n + 16, width // rows_n)
    half, full = jnp.bfloat16, jnp.float32
    return staged_call(
        functools.partial(back_kernel, cols_n, rows_n),
        "back",
        12,
        [order],
        [
            recv, back, cols, scaled_two, norms, grad_out, inverse, att, out, proj, probs,
            normed, qkv, scaled,
        ],
        [((tokens // IMG_PAD * IMG_LEN, width), full), (block, half), (block, half)],
        [
            pltpu.VMEM((tokens, 3 * width), half),
            pltpu.VMEM((tokens, width), half),
            pltpu.VMEM((3 * width, width), half),
            pltpu.VMEM((width, width), half),
            pltpu.VMEM((16, width), full),
            pltpu.VMEM((blocks, *block[1:]), half),
        ],
    )


def adam_kernel(slabs, where_ref, *refs):
    up_grads, down_grads = refs[:slabs], refs[slabs : 2 * slabs]
    ins, outs = refs[2 * slabs : 2 * slabs + 6], refs[-6:]
    for index in range(slabs):

        @pl.when(pl.program_id(0) == index)
        def _():
            for rate, gradient, inputs, results in (
                (rate_up, up_grads[index], ins[0:3], outs[0:3]),
                (rate_down, down_grads[index], ins[3:6], outs[3:6]),
            ):
                first_new, second_new, weight_new = adam_update(
                    inputs[0][0],
                    inputs[1][0],
                    inputs[2][0],
                    gradient[...].astype(jnp.float32),
                    rate,
                    decay_matrix,
                )
                results[0][0] = first_new
                results[1][0] = second_new
                results[2][0] = weight_new


def adam_call(places, gradients, arrays, earlier):
    slabs = len(gradients)
    deep, ff = gradients[0][0].shape
    tile = min(deep, 64 * slabs)
    tiles = deep // tile

    def gradient_spec(index):
        def where_is(slab, part, where):
            return (jnp.where(slab == index, part, jnp.where(slab < index, 0, tiles - 1)), 0)

        return pl.BlockSpec((tile, ff), where_is)

    block = pl.BlockSpec(
        (1, tile, ff), lambda slab, part, where: (where[2 * slab], part, where[2 * slab + 1])
    )
    in_specs = [gradient_spec(index) for index in range(slabs)] * 2 + [block] * 6
    aliases = {}
    if earlier is not None:
        aliases = {1 + len(in_specs) + index: index for index in range(6)}
        in_specs += [pl.BlockSpec(memory_space=pl.ANY)] * 6
    return pl.pallas_call(
        functools.partial(adam_kernel, slabs),
        grid_spec=pltpu.PrefetchScalarGridSpec(
            num_scalar_prefetch=1, grid=(slabs, tiles), in_specs=in_specs, out_specs=[block] * 6
        ),
        out_shape=[jax.ShapeDtypeStruct(arrays[0].shape, jnp.float32)] * 6,
        input_output_aliases=aliases,
        compiler_params=kernel_params(dimension_semantics=("arbitrary", "arbitrary")),
        cost_estimate=cost(6 * slabs),
        name="adam",
    )(places, *[g[0] for g in gradients], *[g[1] for g in gradients], *arrays, *(earlier or ()))


def swap(values, mask):
    rows = lax.axis_size("row")
    cols = lax.axis_size("col")

    def flat(place):
        return place % rows * cols + place // rows

    return lax.ppermute(
        values, ("row", "col"), [(flat(i), flat(i ^ mask)) for i in range(rows * cols)]
    )


def gather_steps():
    bits = []
    bit = lax.axis_size("col") * lax.axis_size("row") // 2
    while bit:
        bits.append(bit)
        bit //= 2
    return [bits[start : start + 2] for start in range(0, len(bits), 2)]


def masks_of(bits):
    return [
        sum(bit for place, bit in enumerate(bits) if index >> place & 1)
        for index in range(1, 1 << len(bits))
    ]


def weight_steps():
    rows = lax.axis_size("row")
    far = [bit for bits in gather_steps() for bit in bits if 1 < bit < rows]
    wide = [bit for bits in gather_steps() for bit in bits if bit > rows]
    pairs = [wide[start : start + 2] for start in range(0, len(wide), 2)]
    return [bits for bits in [far, *pairs, [rows], [1]] if bits]


def block_order(steps):
    rows = lax.axis_size("row")
    devices = lax.axis_size("col") * rows
    differs = jnp.arange(devices, dtype=jnp.int32) ^ (
        lax.axis_index("col") * rows + lax.axis_index("row")
    )
    order = jnp.zeros((devices,), jnp.int32)
    place = 0
    for bits in steps:
        for bit in bits:
            order = order | jnp.where((differs & bit) != 0, 1 << place, 0)
            place += 1
    return order


def gather_step(gathered, bits):
    return jnp.concatenate([gathered] + [swap(gathered, mask) for mask in masks_of(bits)], axis=0)


def halves_step(kept, sent):
    return low(kept.astype(jnp.float32) + swap(sent, 1).astype(jnp.float32))


def scatter_step(blocks, bits):
    count = 1 << len(bits)
    size = blocks.shape[0] // count
    total = blocks[:size].astype(jnp.float32)
    for index, mask in enumerate(masks_of(bits)):
        sent = blocks[(index + 1) * size : (index + 2) * size]
        total = total + swap(sent, mask).astype(jnp.float32)
    return low(total)


def pad_images(values):
    tokens, width = values.shape
    images = tokens // IMG_LEN
    padded = jnp.pad(
        values.reshape(images, IMG_LEN, width), ((0, 0), (0, IMG_PAD - IMG_LEN), (0, 0))
    )
    return padded.reshape(images * IMG_PAD, width)


def pad_rows(values, fill):
    images = values.shape[1] // IMG_LEN
    padded = jnp.pad(
        values.reshape(values.shape[0], images, IMG_LEN),
        ((0, 0), (0, 0), (0, IMG_PAD - IMG_LEN)),
        constant_values=fill,
    )
    return padded.reshape(values.shape[0], images * IMG_PAD)


def to_experts(main, extra, share, beside, rows=None):
    if share > 1:
        width = main.shape[1]
        main = jnp.broadcast_to(
            main.reshape(EXPERTS, 1, -1, width),
            (EXPERTS, share, main.shape[0] // EXPERTS, width),
        ).reshape(-1, width)
    first, *others = gather_steps()
    blocks = gather_step(extra[None], first)
    if rows is None:
        main, blocks, beside = lax.optimization_barrier((main, blocks, beside))
    else:
        main, blocks, rows = lax.optimization_barrier((main, blocks, rows))
        beside = beside(rows)
    main = lax.all_to_all(main, BOTH, split_axis=0, concat_axis=0, tiled=True)
    for place, bits in enumerate(others):
        if place == len(others) - 1 and rows is not None:
            blocks, beside = lax.optimization_barrier((blocks, beside))
        blocks = gather_step(blocks, bits)
    return main, blocks.reshape(-1, extra.shape[1]), beside


def from_experts(main, share):
    main = lax.all_to_all(main, BOTH, split_axis=0, concat_axis=0, tiled=True)
    width = main.shape[1]
    if share > 1:
        main = low(
            jnp.sum(main.reshape(EXPERTS, share, -1, width).astype(jnp.float32), axis=1)
        ).reshape(-1, width)
    return main


def spare_home(kept, sent):
    blocks = lax.axis_size("row") * lax.axis_size("col") // 2
    blocks = halves_step(
        kept.reshape(blocks, -1, kept.shape[1]), sent.reshape(blocks, -1, sent.shape[1])
    )
    for bits in reversed(gather_steps()[1:]):
        if bits != [1]:
            blocks = scatter_step(blocks, [bit for bit in bits if bit != 1])
    return blocks


def body(*args):
    (
        x_in,
        cotangent,
        teacher,
        valid_mask,
        routes,
        gate_weights,
        norm_params,
        qkv_weight,
        out_weight,
        up_weight,
        down_weight,
        norm_first,
        norm_second,
        qkv_first,
        qkv_second,
        out_first,
        out_second,
        up_first,
        up_second,
        down_first,
        down_second,
    ) = args
    rows_n = lax.axis_size("row")
    cols_n = lax.axis_size("col")
    devices = rows_n * cols_n
    my_row = lax.axis_index("row")
    me = lax.axis_index("col") * rows_n + my_row
    tokens, width = x_in.shape
    token_total = routes.shape[1]
    experts_here, deep, ff = up_weight.shape
    share = rows_n // experts_here
    ff_here = ff // share
    mean_load = TOP * tokens / EXPERTS
    cap = max(16, 16 * round(1.3 * mean_load / 16))
    slots = EXPERTS * cap
    spare = max(32, 8 * round(mean_load / 5))
    room = 4 * devices

    def three_parts(values):
        top = lax.reduce_precision(values, 8, 7)
        rest = values - top
        middle_part = lax.reduce_precision(rest, 8, 7)
        return [low(top), low(middle_part), low(rest - middle_part)]

    small = jnp.concatenate(
        [
            low(jnp.transpose(qkv_weight)),
            low(out_weight),
            *three_parts(norm_params),
            jnp.zeros((4, deep), jnp.bfloat16),
        ],
        axis=0,
    )
    order = block_order(gather_steps())
    pack_order = block_order(weight_steps())

    partners = [my_row ^ index for index in range(rows_n)]
    rowpos = jnp.stack(partners).astype(jnp.int32)

    def slab(values, partner):
        return low(
            lax.dynamic_slice(
                values, (partner // share, 0, partner % share * ff_here), (1, deep, ff_here)
            )[0]
        )

    far = rows_n // 2
    first_step, second_step, *last_steps = gather_steps()
    far_ones = [index for index in range(2, rows_n)] or [1]
    first_far, *more_far = far_ones
    steps = weight_steps()
    pack = gather_step(small[None], steps[0])
    held = (routes, gate_weights, valid_mask, x_in, up_weight, down_weight)
    pack, held = lax.optimization_barrier((pack, held))
    early = swap(slab(up_weight, partners[first_far]), first_far)

    start = me * tokens
    own_routes = pad_rows(lax.dynamic_slice_in_dim(held[0], start, tokens, 1), -1)
    own_gates = pad_rows(lax.dynamic_slice_in_dim(held[1], start, tokens, 1), 0)
    own_mask = pad_rows(
        lax.dynamic_slice_in_dim(held[2], my_row * tokens, tokens, 0)[None], 0
    ).astype(jnp.float32)
    padded = own_routes.shape[1]
    extra = jnp.concatenate(
        [jnp.zeros((2, padded), jnp.float32), own_gates, own_mask, jnp.zeros((3, padded), jnp.float32)],
        axis=0,
    )
    all_routes = jnp.pad(
        held[0], ((0, 0), (0, round_up(token_total, 2048) - token_total)), constant_values=-1
    )
    mine = (me // share).astype(jnp.int32).reshape(1)
    x_pad = pad_images(held[3])
    up_slabs = [slab(held[4], partners[index]) for index in more_far]
    down_slabs = [slab(held[5], partners[index]) for index in far_ones]
    near = [1] if first_far != 1 else []
    near_slabs = [(slab(held[4], partners[p]), slab(held[5], partners[p])) for p in near]
    ups = {0: slab(held[4], partners[0])}
    downs = {0: slab(held[5], partners[0])}
    for bits in steps[1:-2]:
        pack = gather_step(pack, bits)
    early, up_slabs = lax.optimization_barrier((early, up_slabs))
    pack, early, down_slabs, near_slabs = lax.optimization_barrier(
        (pack, early, down_slabs, near_slabs)
    )
    ups[first_far] = early
    up_pieces = [swap(piece, index) for index, piece in zip(more_far, up_slabs)]
    pack = gather_step(pack, steps[-2])
    table, table_cols, pick, excess = route_call(
        cap, spare, room, tokens, mine, all_routes, own_routes, extra, order[None]
    )
    overflow = excess[0, 0] > 0

    pack, up_pieces, table, table_cols, pick, x_pad, down_slabs = lax.optimization_barrier(
        (pack, up_pieces, table, table_cols, pick, x_pad, down_slabs)
    )
    ups.update(zip(more_far, up_pieces))
    for index, piece in zip(far_ones, down_slabs):
        downs[index] = swap(piece, index)
    for p, (up_slab, down_slab) in zip(near, near_slabs):
        ups[p], downs[p] = swap(up_slab, p), swap(down_slab, p)
    packs = [pack, swap(pack, 1)]
    if near:
        packs, ups, downs[1] = lax.optimization_barrier((packs, ups, downs[1]))
    send, spare_rows, middle, proj, att, probs, qkv_all, out_all, norms, stats = front_call(
        cols_n, rows_n, slots, spare, pack_order, x_pad, packs, table
    )
    main, extras, (ups, downs) = to_experts(send, spare_rows, share, (ups, downs))
    ups = [ups[index] for index in range(rows_n)]
    downs = [downs[index] for index in range(rows_n)]

    counts = extras.reshape(devices, spare, width)[:, spare - 1, :2].astype(jnp.float32)
    valid_total = jnp.sum(counts)
    main, kept, sent, slot_rows = expert_call(
        "expert", rowpos, main, extras, pick, None, ups, downs
    )
    combined = from_experts(main, share)
    extras = spare_home(kept, sent)
    grad_send, grad_spare, mixed_rows, grad_out = turn_call(
        combined,
        scatter_step(extras, gather_steps()[0])[0],
        table_cols,
        table,
        middle,
        pad_images(teacher),
        pad_images(cotangent),
        valid_total[None, None],
    )
    main, extras, (hidden, slope) = to_experts(
        grad_send, grad_spare, share, lambda rows: hidden_call(rowpos, rows, ups), slot_rows
    )
    errors = extras.reshape(devices, spare, width)
    main, kept, sent, grad_slots, grad_pre = expert_call(
        "pull", rowpos, main, extras, pick, slope, ups, downs
    )
    grad_back = from_experts(main, share)
    extras = spare_home(kept, sent)
    up_grads = weight_grad_call(rowpos, slot_rows, grad_pre, deep)
    raw_ups = up_grads
    extras, up_grads, grad_slots = lax.optimization_barrier((extras, up_grads, grad_slots))
    down_grads = weight_grad_call(rowpos, grad_slots, hidden, deep)
    grad_back_spare = scatter_step(extras, gather_steps()[0])[0]

    arrays = (up_weight, up_first, up_second, down_weight, down_first, down_second)

    def places_of(chosen):
        return jnp.stack(
            [value for p in chosen for value in (partners[p] // share, partners[p] % share)]
        ).astype(jnp.int32)

    near = list(range(min(2, rows_n)))
    apart = list(range(2, rows_n))
    groups = [apart[: len(apart) // 2], apart[len(apart) // 2 :]]
    groups = [group for group in groups if group]
    gradients = {}
    for index in near:
        pair = (up_grads[index], down_grads[index])
        gradients[index] = tuple(swap(p, index) for p in pair) if index else pair
    if groups:
        up_far = [swap(raw_ups[index], index) for index in groups[0]]
        grad_back, grad_back_spare, up_far, down_grads = lax.optimization_barrier(
            (grad_back, grad_back_spare, up_far, down_grads)
        )
        down_far = [swap(down_grads[index], index) for index in groups[0]]

    input_rows, blocks, sent_blocks = back_call(
        cols_n,
        rows_n,
        pack_order,
        grad_back,
        grad_back_spare,
        table_cols,
        stats,
        grad_out,
        proj,
        att,
        probs,
        qkv_all,
        out_all,
        norms,
    )
    if groups:
        blocks, sent_blocks, down_far = lax.optimization_barrier((blocks, sent_blocks, down_far))
        for index, pair in zip(groups[0], zip(up_far, down_far)):
            gradients[index] = pair
    experts_new = None
    later = []
    for place, bits in enumerate(reversed(weight_steps())):
        if place == 0:
            blocks = halves_step(blocks, sent_blocks)
        else:
            blocks = scatter_step(blocks, bits)
        if place == 0:
            sent = [gradients[index] for index in near]
            apart_sent = [gradients[index] for index in groups[0]] if groups else []
            blocks, sent, up_grads, down_grads, errors = lax.optimization_barrier(
                (blocks, sent, up_grads, down_grads, errors)
            )

            experts_new = adam_call(places_of(near), sent, arrays, None)
            if len(groups) > 1:
                later = [
                    (swap(up_grads[index], index), swap(down_grads[index], index))
                    for index in groups[1]
                ]
        if place == 1:
            blocks, experts_new, errors, apart_sent = lax.optimization_barrier(
                (blocks, experts_new, errors, apart_sent)
            )
            loss_value = jnp.sum(errors[:, spare - 1, :3].astype(jnp.float32)[order]) / valid_total
            if groups:
                experts_new = adam_call(places_of(groups[0]), apart_sent, arrays, experts_new)
        if place == 2:
            blocks, experts_new, loss_value = lax.optimization_barrier(
                (blocks, experts_new, loss_value)
            )
    if later:
        experts_new = adam_call(places_of(groups[1]), later, arrays, experts_new)
    up_one, up_two, up_new, down_one, down_two, down_new = experts_new
    summed = blocks[0].astype(jnp.float32)
    qkv_rows = qkv_weight.shape[1]
    out_rows = out_weight.shape[0]
    qkv_one, qkv_two, qkv_new = adam_update(
        qkv_weight, qkv_first, qkv_second, jnp.transpose(summed[:qkv_rows]), rate_qkv, decay_matrix
    )
    out_one, out_two, out_new = adam_update(
        out_weight,
        out_first,
        out_second,
        summed[qkv_rows : qkv_rows + out_rows],
        rate_out,
        decay_matrix,
    )
    norm_one, norm_two, norm_new = adam_update(
        norm_params,
        norm_first,
        norm_second,
        summed[qkv_rows + out_rows : qkv_rows + out_rows + 4],
        rate_norm,
        0.0,
    )
    quick = (
        mixed_rows,
        input_rows,
        loss_value,
        norm_one,
        norm_two,
        norm_new,
        qkv_one,
        qkv_two,
        qkv_new,
        out_one,
        out_two,
        out_new,
        up_one,
        up_two,
        up_new,
        down_one,
        down_two,
        down_new,
    )

    def again(state):
        return (jnp.bool_(False), general_body(*args))

    return lax.while_loop(lambda state: state[0], again, (overflow, quick))[1]


def solution(mesh):
    in_specs = (
        P(("col", "row"), None),
        P(("col", "row"), None),
        P(("col", "row"), None),
        P("col"),
        P(),
        P(),
        P(None, "row"),
        P("row", "col"),
        P("col", "row"),
        P("col", "row", None),
        P("col", "row", None),
        P(None, "row"),
        P(None, "row"),
        P("row", "col"),
        P("row", "col"),
        P("col", "row"),
        P("col", "row"),
        P("col", "row", None),
        P("col", "row", None),
        P("col", "row", None),
        P("col", "row", None),
    )
    out_specs = (
        P(("col", "row"), None),
        P(("col", "row"), None),
        P(),
        P(None, "row"),
        P(None, "row"),
        P(None, "row"),
        P("row", "col"),
        P("row", "col"),
        P("row", "col"),
        P("col", "row"),
        P("col", "row"),
        P("col", "row"),
        P("col", "row", None),
        P("col", "row", None),
        P("col", "row", None),
        P("col", "row", None),
        P("col", "row", None),
        P("col", "row", None),
    )
    return jax.shard_map(body, mesh=mesh, in_specs=in_specs, out_specs=out_specs, check_vma=False)
```

```python
import functools

import jax
import jax.numpy as jnp
from jax import lax
from jax.experimental import pallas as pl
from jax.experimental.pallas import tpu as pltpu
from jax.sharding import PartitionSpec as P

HEADS = 8
HEAD_DIM = 64
EXPERTS = 32
TOP = 2
IMG_LEN = 197
STEP = 5
IMG_PAD = 256
BOTH = ("col", "row")
VMEM_BYTES = 60 * 1024 * 1024

norm_eps = 1e-06
beta_one = 0.9
beta_two = 0.999
adam_eps = 1e-08
decay_matrix = 0.1
rate_norm = 0.4
rate_qkv = 0.02
rate_out = 0.06
rate_up = 0.02
rate_down = 0.01


def dispatch_tables(routes, capacity):
    flat_routes = routes.reshape(-1)
    picks_total = flat_routes.shape[0]
    order_idx = jnp.argsort(flat_routes, stable=True)
    sorted_experts = flat_routes[order_idx]
    expert_ids = jnp.arange(EXPERTS, dtype=jnp.int32)
    expert_load = jnp.sum((flat_routes[:, None] == expert_ids[None, :]).astype(jnp.int32), axis=0)
    starts_at = jnp.cumsum(expert_load) - expert_load
    position = jnp.arange(picks_total, dtype=jnp.int32)
    slot_index = sorted_experts * capacity + position - starts_at[sorted_experts]
    slot_token = jnp.zeros((EXPERTS * capacity,), jnp.int32).at[slot_index].set(order_idx // TOP)
    slot_used = jnp.zeros((EXPERTS * capacity,), jnp.int32).at[slot_index].set(1)
    pick_slot = jnp.zeros((picks_total,), jnp.int32).at[order_idx].set(slot_index)
    return (slot_token, slot_used, order_idx, slot_index, pick_slot.reshape(-1, TOP))


def gelu_tanh(inner_value):
    return jax.nn.gelu(inner_value, approximate=True)


def spread_cols(values):
    return lax.all_gather(values, "col", axis=0, tiled=True)


def spread_rows(values):
    return lax.all_gather(values, "row", axis=0, tiled=True)


def sum_rows(term_fn, row_total):
    return lax.psum_scatter(
        term_fn(jnp.int32(0), row_total * lax.axis_size("row")),
        "row",
        scatter_dimension=0,
        tiled=True,
    )


def sum_cols(term_fn, row_total):
    return lax.psum_scatter(
        term_fn(jnp.int32(0), row_total * lax.axis_size("col")),
        "col",
        scatter_dimension=0,
        tiled=True,
    )


def to_heads(values):
    return lax.all_to_all(values, "col", split_axis=0, concat_axis=1, tiled=True)


def from_heads(values):
    return lax.all_to_all(values, "col", split_axis=1, concat_axis=0, tiled=True)


def token_sums(first_part, second_part):
    return lax.psum((first_part, second_part), "row")


def norm_forward(stream, gain_row, shift_row):
    full_width = stream.shape[1] * lax.axis_size("row")
    sum_plain, squares = token_sums(jnp.sum(stream, axis=1), jnp.sum(stream * stream, axis=1))
    center = sum_plain / full_width
    offset = stream - center[:, None]
    spread = squares / full_width - center * center
    inverse = lax.rsqrt(spread + norm_eps)
    scaled = offset * inverse[:, None]
    return (scaled * gain_row + shift_row, scaled, inverse)


def norm_backward(upstream, scaled, inverse, gain_row):
    full_width = scaled.shape[1] * lax.axis_size("row")
    dscaled = upstream * gain_row
    sum_plain, sum_cross = token_sums(jnp.sum(dscaled, axis=1), jnp.sum(dscaled * scaled, axis=1))
    inner_grad = (
        dscaled - (sum_plain / full_width)[:, None] - scaled * (sum_cross / full_width)[:, None]
    )
    return (
        inner_grad * inverse[:, None],
        jnp.sum(upstream * scaled, axis=0),
        jnp.sum(upstream, axis=0),
    )


def attend_local(packed):
    images = packed.shape[0] // IMG_LEN
    split_heads = packed.reshape(images, IMG_LEN, 3, HEADS, HEAD_DIM)
    scores = jnp.einsum(
        "gqhd,gkhd->ghqk",
        split_heads[:, :, 0],
        split_heads[:, :, 1],
        preferred_element_type=jnp.float32,
    ) * HEAD_DIM ** (-0.5)
    top_score = jnp.max(scores, axis=-1, keepdims=True)
    shifted = jnp.exp(scores - top_score)
    totals = jnp.sum(shifted, axis=-1, keepdims=True)
    weights = (shifted / totals).astype(jnp.bfloat16)
    log_norm = top_score + jnp.log(totals)
    mixed_heads = jnp.einsum(
        "ghqk,gkhd->gqhd", weights, split_heads[:, :, 2], preferred_element_type=jnp.float32
    )
    return (mixed_heads.reshape(images * IMG_LEN, HEADS * HEAD_DIM), log_norm)


def attend_back(packed, log_norm, upstream):
    images = packed.shape[0] // IMG_LEN
    split_heads = packed.reshape(images, IMG_LEN, 3, HEADS, HEAD_DIM)
    queries = split_heads[:, :, 0]
    key_part = split_heads[:, :, 1]
    value_part = split_heads[:, :, 2]
    grad_mixed = upstream.reshape(images, IMG_LEN, HEADS, HEAD_DIM)
    score_scale = HEAD_DIM ** (-0.5)
    scores = (
        jnp.einsum("gqhd,gkhd->ghqk", queries, key_part, preferred_element_type=jnp.float32)
        * score_scale
    )
    prob_rows = jnp.exp(scores - log_norm)
    grad_value = jnp.einsum(
        "ghqk,gqhd->gkhd",
        prob_rows.astype(jnp.bfloat16),
        grad_mixed,
        preferred_element_type=jnp.float32,
    )
    grad_probs = jnp.einsum(
        "gqhd,gkhd->ghqk", grad_mixed, value_part, preferred_element_type=jnp.float32
    )
    grad_scores = (
        prob_rows * (grad_probs - jnp.sum(prob_rows * grad_probs, axis=-1, keepdims=True))
    ).astype(jnp.bfloat16)
    grad_query = (
        jnp.einsum("ghqk,gkhd->gqhd", grad_scores, key_part, preferred_element_type=jnp.float32)
        * score_scale
    )
    grad_key = (
        jnp.einsum("ghqk,gqhd->gkhd", grad_scores, queries, preferred_element_type=jnp.float32)
        * score_scale
    )
    stacked = jnp.stack([grad_query, grad_key, grad_value], axis=2)
    return stacked.reshape(images * IMG_LEN, 3 * HEADS * HEAD_DIM)


def adam_update(weight, first_moment, second_moment, gradient, step_rate, decay_factor):
    first_new = beta_one * first_moment + (1.0 - beta_one) * gradient
    second_new = beta_two * second_moment + (1.0 - beta_two) * gradient * gradient
    first_hat = first_new / (1.0 - beta_one**STEP)
    second_hat = second_new / (1.0 - beta_two**STEP)
    weight_new = weight - step_rate * (
        first_hat / (jnp.sqrt(second_hat) + adam_eps) + decay_factor * weight
    )
    return (first_new, second_new, weight_new)


def general_body(
    x_in,
    cotangent,
    teacher,
    valid_mask,
    routes,
    gate_weights,
    norm_params,
    qkv_weight,
    out_weight,
    up_weight,
    down_weight,
    norm_first,
    norm_second,
    qkv_first,
    qkv_second,
    out_first,
    out_second,
    up_first,
    up_second,
    down_first,
    down_second,
):
    token_total = routes.shape[1]
    row_devices = lax.axis_size("row")
    col_devices = lax.axis_size("col")
    capacity = row_devices * (5 * token_total * TOP // (4 * EXPERTS) // row_devices)
    experts_here = EXPERTS // col_devices
    first_mine = lax.axis_index("col") * experts_here
    slot_share = capacity * experts_here // row_devices
    route_rows = jnp.stack([routes[k] for k in range(TOP)], axis=1)
    gate_rows = jnp.stack([gate_weights[k] for k in range(TOP)], axis=1)
    slot_token, slot_used, order_idx, slot_index, pick_slot = dispatch_tables(route_rows, capacity)
    slot_gate = (
        jnp.zeros((EXPERTS * capacity,), jnp.float32)
        .at[slot_index]
        .set(gate_rows.reshape(-1)[order_idx])
    )
    mine_token = jnp.transpose(
        lax.dynamic_slice_in_dim(slot_token.reshape(EXPERTS, capacity), first_mine, experts_here, 0)
    )
    mine_used = jnp.transpose(
        lax.dynamic_slice_in_dim(slot_used.reshape(EXPERTS, capacity), first_mine, experts_here, 0)
    ).astype(jnp.bfloat16)[:, :, None]
    mine_gate = jnp.transpose(
        lax.dynamic_slice_in_dim(slot_gate.reshape(EXPERTS, capacity), first_mine, experts_here, 0)
    )[:, :, None]
    pick_expert = pick_slot // capacity
    pick_owned = ((pick_expert >= first_mine) & (pick_expert < first_mine + experts_here)).astype(
        jnp.float32
    )
    pick_local = pick_slot % capacity * experts_here + jnp.clip(
        pick_expert - first_mine, 0, experts_here - 1
    )
    x_block, cot_block, teacher_block = (
        lax.all_to_all(x_in, "row", split_axis=1, concat_axis=0, tiled=True),
        lax.all_to_all(cotangent, "row", split_axis=1, concat_axis=0, tiled=True),
        lax.all_to_all(teacher, "row", split_axis=1, concat_axis=0, tiled=True),
    )
    stream = x_block.astype(jnp.float32)
    normed, normed_scaled, normed_inverse = norm_forward(stream, norm_params[0], norm_params[1])
    normed_low = normed.astype(jnp.bfloat16)
    normed_all = spread_cols(normed_low)
    qkv_low = qkv_weight.astype(jnp.bfloat16)

    def qkv_term(row_start, row_count):
        return jnp.dot(normed_all, qkv_low, preferred_element_type=jnp.float32)

    projected = sum_rows(qkv_term, token_total // row_devices)
    packed = to_heads(projected.astype(jnp.bfloat16))
    attended, log_norm = attend_local(packed)
    attended_rows = from_heads(attended.astype(jnp.bfloat16))
    attended_all = spread_rows(attended_rows)
    out_low = out_weight.astype(jnp.bfloat16)

    def out_term(row_start, row_count):
        return jnp.dot(attended_all, out_low, preferred_element_type=jnp.float32)

    middle = stream + sum_cols(out_term, token_total // col_devices)
    second, second_scaled, second_inverse = norm_forward(middle, norm_params[2], norm_params[3])
    second_low = second.astype(jnp.bfloat16)
    second_all = spread_cols(second_low)
    slot_rows = second_all[mine_token] * mine_used
    up_low = up_weight.astype(jnp.bfloat16)
    down_low = down_weight.astype(jnp.bfloat16)

    def up_term(row_start, row_count):
        return jnp.einsum(
            "ced,edf->cef", slot_rows, up_low, preferred_element_type=jnp.float32
        ).reshape(row_count, -1)

    hidden_pre = sum_rows(up_term, slot_share)
    hidden_low = gelu_tanh(hidden_pre).astype(jnp.bfloat16)
    hidden_all = spread_rows(hidden_low).reshape(capacity, experts_here, -1)
    expert_out = jnp.einsum(
        "cef,edf->ced", hidden_all, down_low, preferred_element_type=jnp.float32
    ).reshape(capacity * experts_here, -1)

    def combine_term(row_start, row_count):
        return jnp.sum(expert_out[pick_local] * (gate_rows * pick_owned)[:, :, None], axis=1)

    result = middle + sum_cols(combine_term, token_total // col_devices)
    valid_rows = valid_mask.astype(jnp.float32)[:, None]
    mismatch = result - teacher_block.astype(jnp.float32)
    square_sum, valid_sum = lax.psum(
        (jnp.sum(valid_rows * mismatch * mismatch), jnp.sum(valid_mask.astype(jnp.float32))),
        ("row", "col"),
    )
    valid_total = valid_sum / row_devices
    loss_value = square_sum / valid_total
    grad_out = cot_block.astype(jnp.float32) + 2.0 / valid_total * valid_rows * mismatch
    grad_all = spread_cols(grad_out.astype(jnp.bfloat16))
    grad_slots = (grad_all[mine_token] * mine_gate).astype(jnp.bfloat16)

    def hidden_term(row_start, row_count):
        return jnp.einsum(
            "ced,edf->cef", grad_slots, down_low, preferred_element_type=jnp.float32
        ).reshape(row_count, -1)

    grad_hidden = sum_rows(hidden_term, slot_share)
    gelu_value, gelu_pull = jax.vjp(gelu_tanh, hidden_pre)
    grad_pre = gelu_pull(grad_hidden)[0].astype(jnp.bfloat16)
    grad_pre_all = spread_rows(grad_pre).reshape(capacity, experts_here, -1)
    up_grad = jnp.einsum(
        "ced,cef->edf", slot_rows, grad_pre_all, preferred_element_type=jnp.float32
    )
    down_grad = jnp.einsum(
        "ced,cef->edf", grad_slots, hidden_all, preferred_element_type=jnp.float32
    )
    slot_input_grad = jnp.einsum(
        "cef,edf->ced", grad_pre_all, up_low, preferred_element_type=jnp.float32
    ).reshape(capacity * experts_here, -1)

    def back_combine(row_start, row_count):
        return jnp.sum(slot_input_grad[pick_local] * pick_owned[:, :, None], axis=1)

    grad_second = sum_cols(back_combine, token_total // col_devices)
    grad_middle_norm, second_gain_grad, second_shift_grad = norm_backward(
        grad_second, second_scaled, second_inverse, norm_params[2]
    )
    grad_middle = grad_out + grad_middle_norm
    grad_branch_all = spread_cols(grad_middle.astype(jnp.bfloat16))
    out_grad = jnp.einsum(
        "ti,to->io", attended_all, grad_branch_all, preferred_element_type=jnp.float32
    )

    def attended_term(row_start, row_count):
        return jnp.einsum("to,io->ti", grad_branch_all, out_low, preferred_element_type=jnp.float32)

    grad_attended = sum_rows(attended_term, token_total // row_devices)
    grad_packed = attend_back(packed, log_norm, to_heads(grad_attended.astype(jnp.bfloat16)))
    grad_proj_rows = from_heads(grad_packed.astype(jnp.bfloat16))
    grad_proj_all = spread_rows(grad_proj_rows)
    qkv_grad = jnp.einsum(
        "ti,to->io", normed_all, grad_proj_all, preferred_element_type=jnp.float32
    )

    def input_term(row_start, row_count):
        return jnp.einsum("to,io->ti", grad_proj_all, qkv_low, preferred_element_type=jnp.float32)

    grad_normed = sum_cols(input_term, token_total // col_devices)
    grad_stream_norm, first_gain_grad, first_shift_grad = norm_backward(
        grad_normed, normed_scaled, normed_inverse, norm_params[0]
    )
    input_block = grad_middle + grad_stream_norm
    norm_grad = lax.psum(
        jnp.stack([first_gain_grad, first_shift_grad, second_gain_grad, second_shift_grad], axis=0),
        "col",
    )
    mixed_block = result.astype(jnp.bfloat16).astype(jnp.float32)
    mixed_rows, input_grad = (
        lax.all_to_all(
            mixed_block.astype(jnp.bfloat16), "row", split_axis=0, concat_axis=1, tiled=True
        ).astype(mixed_block.dtype),
        lax.all_to_all(
            input_block.astype(jnp.bfloat16), "row", split_axis=0, concat_axis=1, tiled=True
        ).astype(input_block.dtype),
    )
    mixed_out = mixed_rows.astype(jnp.bfloat16)
    norm_one, norm_two, norm_new = adam_update(
        norm_params, norm_first, norm_second, norm_grad, rate_norm, 0.0
    )
    qkv_one, qkv_two, qkv_new = adam_update(
        qkv_weight, qkv_first, qkv_second, qkv_grad, rate_qkv, decay_matrix
    )
    out_one, out_two, out_new = adam_update(
        out_weight, out_first, out_second, out_grad, rate_out, decay_matrix
    )
    up_one, up_two, up_new = adam_update(
        up_weight, up_first, up_second, up_grad, rate_up, decay_matrix
    )
    down_one, down_two, down_new = adam_update(
        down_weight, down_first, down_second, down_grad, rate_down, decay_matrix
    )
    return (
        mixed_out,
        input_grad,
        loss_value,
        norm_one,
        norm_two,
        norm_new,
        qkv_one,
        qkv_two,
        qkv_new,
        out_one,
        out_two,
        out_new,
        up_one,
        up_two,
        up_new,
        down_one,
        down_two,
        down_new,
    )


def round_up(value, unit):
    return -(-value // unit) * unit


def mxu(lhs, rhs):
    return jnp.dot(lhs, rhs, preferred_element_type=jnp.float32)


def mxu_nt(lhs, rhs):
    return lax.dot_general(lhs, rhs, (((1,), (1,)), ((), ())), preferred_element_type=jnp.float32)


def mxu_tn(lhs, rhs):
    return lax.dot_general(lhs, rhs, (((0,), (0,)), ((), ())), preferred_element_type=jnp.float32)


def low(values):
    return values.astype(jnp.bfloat16)


def kernel_params(**more):
    return pltpu.CompilerParams(vmem_limit_bytes=VMEM_BYTES, **more)


def cost(micros):
    return pl.CostEstimate(
        flops=int(1.1e9 * micros), bytes_accessed=int(3.5e6 * micros), transcendentals=0
    )


def iota(shape, dim):
    return lax.broadcasted_iota(jnp.int32, shape, dim)


def strict(size, lower):
    row = iota((size, size), 0)
    col = iota((size, size), 1)
    return low(((col < row) if lower else (row < col)).astype(jnp.float32))


def column_sums(matrix, column):
    return mxu(matrix, low(jnp.broadcast_to(column, (column.shape[0], 128))))[:, 0:1]


def route_kernel(
    cap, block, tokens, chunk, mine_ref, all_ref, own_ref, extra_ref, order_ref,
    rows_ref, cols_ref, pick_ref, excess_ref,
):
    spare = block - 1
    padded = own_ref.shape[1]
    expert_ids = iota((EXPERTS, padded), 0)
    before = strict(padded, False)
    first = own_ref[0:1, :]
    second = own_ref[1:2, :]
    first_hot = (expert_ids == first).astype(jnp.float32)
    second_hot = (expert_ids == second).astype(jnp.float32)
    first_rank = jnp.sum(first_hot * mxu(low(first_hot), before), axis=0, keepdims=True)
    first_load = jnp.sum(first_hot, axis=1, keepdims=True)
    second_rank = jnp.sum(
        second_hot * (mxu(low(second_hot), before) + first_load), axis=0, keepdims=True
    )
    own_over = jnp.maximum(first_load + jnp.sum(second_hot, axis=1, keepdims=True) - cap, 0.0)
    own_base = column_sums(strict(EXPERTS, True), own_over)

    def slot_of(expert, rank, hot):
        extra = jnp.sum(hot * own_base, axis=0, keepdims=True) + rank - cap
        last = jnp.where(extra < spare, EXPERTS * cap + extra, -1.0)
        slot = jnp.where(rank < cap, expert.astype(jnp.float32) * cap + rank, last)
        return jnp.where(expert >= 0, slot, -1.0)

    row = iota((8, padded), 0)
    table = jnp.where(
        row == 0,
        slot_of(first, first_rank, first_hot),
        jnp.where(row == 1, slot_of(second, second_rank, second_hot), extra_ref[...]),
    )
    rows_ref[...] = table
    cols_ref[...] = jnp.transpose(table)

    devices = order_ref.shape[1]
    length = all_ref.shape[1]
    owner = iota((devices, chunk), 0) * tokens
    place = iota((devices, chunk), 1)
    chunk_ids = iota((EXPERTS, chunk), 0)

    def add_chunk(step, total):
        start = step * chunk
        part = all_ref[:, pl.ds(pl.multiple_of(start, chunk), chunk)]
        hot = (chunk_ids == part[0:1, :]).astype(jnp.float32) + (chunk_ids == part[1:2, :]).astype(
            jnp.float32
        )
        position = place + start
        member = ((position >= owner) & (position < owner + tokens)).astype(jnp.float32)
        return total + mxu_nt(low(member), low(hot))

    loads = lax.fori_loop(
        0, length // chunk, add_chunk, jnp.zeros((devices, EXPERTS), jnp.float32)
    )
    over = jnp.maximum(loads - cap, 0.0)
    room = pick_ref.shape[0]
    by_device = jnp.max(jnp.sum(over, axis=1, keepdims=True), axis=0, keepdims=True) - spare
    by_expert = jnp.max(jnp.sum(over, axis=0, keepdims=True), axis=1, keepdims=True) - room
    excess_ref[...] = jnp.broadcast_to(jnp.maximum(by_device, by_expert), excess_ref.shape)
    turned = low((iota((devices, devices), 0) == order_ref[...]).astype(jnp.float32))
    over = mxu(turned, low(jnp.minimum(over, 256.0)))
    base = mxu(low(over), strict(EXPERTS, False))
    mine = iota((devices, EXPERTS), 1) == mine_ref[0]
    over_mine = jnp.sum(jnp.where(mine, over, 0.0), axis=1, keepdims=True)
    base_mine = jnp.sum(jnp.where(mine, base, 0.0), axis=1, keepdims=True)
    start_mine = column_sums(strict(devices, True), over_mine)
    width = 256
    for part in range(devices * block // width):
        inner = iota((devices, width), 1) + part * width - iota((devices, width), 0) * block
        inside = (inner >= 0) & (inner < spare)

        def spread(column):
            return jnp.sum(jnp.where(inside, column, 0.0), axis=0, keepdims=True)

        offset = spread(inner.astype(jnp.float32) - base_mine)
        used = (offset >= 0.0) & (offset < spread(over_mine))
        target = jnp.where(used, offset + spread(start_mine), -1.0)
        pick_ref[:, part * width : (part + 1) * width] = low(
            (iota((room, width), 0).astype(jnp.float32) == target).astype(jnp.float32)
        )


def route_call(cap, spare, room, tokens, mine, all_routes, own_routes, extra, order):
    padded = own_routes.shape[1]
    devices = order.shape[1]
    spec = pl.BlockSpec(memory_space=pltpu.VMEM)
    return pl.pallas_call(
        functools.partial(route_kernel, cap, spare, tokens, 2048),
        in_specs=[pl.BlockSpec(memory_space=pltpu.SMEM)] + [spec] * 4,
        out_shape=(
            jax.ShapeDtypeStruct((8, padded), jnp.float32),
            jax.ShapeDtypeStruct((padded, 8), jnp.float32),
            jax.ShapeDtypeStruct((room, devices * spare), jnp.bfloat16),
            jax.ShapeDtypeStruct((8, 128), jnp.float32),
        ),
        compiler_params=kernel_params(),
        cost_estimate=cost(4),
        name="route",
    )(mine, all_routes, own_routes, extra, order)


def norm_stats(stream):
    center = jnp.mean(stream, axis=1, keepdims=True)
    offset = stream - center
    spread = jnp.mean(offset * offset, axis=1, keepdims=True)
    inverse = lax.rsqrt(spread + norm_eps)
    return offset * inverse, inverse


def norm_pull(upstream, scaled, inverse, gain_row):
    dscaled = upstream * gain_row
    plain = jnp.mean(dscaled, axis=1, keepdims=True)
    cross = jnp.mean(dscaled * scaled, axis=1, keepdims=True)
    return (dscaled - plain - scaled * cross) * inverse


def crop_to(result, padded):
    for image in range(padded.shape[0] // IMG_PAD):
        result[image * IMG_LEN : (image + 1) * IMG_LEN, :] = padded[
            image * IMG_PAD : image * IMG_PAD + IMG_LEN, :
        ]


def half_mask(shape, half):
    lane = iota(shape, 1)
    return (lane < HEAD_DIM) if half == 0 else (lane >= HEAD_DIM)


def pick_half(tile, half):
    return jnp.where(half_mask(tile.shape, half), tile, jnp.zeros_like(tile))


class Staged:
    def __init__(self, ins, in_bufs, in_sems, outs, out_bufs, out_sems):
        self.copies = [
            pltpu.make_async_copy(source, buffer, in_sems.at[index])
            for index, (source, buffer) in enumerate(zip(ins, in_bufs))
        ]
        self.in_bufs = in_bufs
        self.out_bufs = out_bufs
        self.outs = outs
        self.out_sems = out_sems
        self.open = set()
        self.sent = []

    def begin(self):
        for index, copy in enumerate(self.copies):
            copy.start()
            self.open.add(index)

    def need(self, index):
        if index in self.open:
            self.copies[index].wait()
            self.open.remove(index)
        return self.in_bufs[index]

    def ship(self, index, source=None):
        copy = pltpu.make_async_copy(
            self.out_bufs[index] if source is None else source,
            self.outs[index],
            self.out_sems.at[index],
        )
        copy.start()
        self.sent.append(copy)

    def end(self):
        for index in sorted(self.open):
            self.copies[index].wait()
        for copy in self.sent:
            copy.wait()


def staged_call(kernel_fn, name, micros, scalars, inputs, outs, scratch):
    outs = [jax.ShapeDtypeStruct(shape, kind) for shape, kind in outs]
    counts = (len(scalars), len(inputs), len(outs))

    def kernel(*refs):
        scalar_refs, refs = refs[: counts[0]], refs[counts[0] :]
        ins, refs = refs[: counts[1]], refs[counts[1] :]
        results, refs = refs[: counts[2]], refs[counts[2] :]
        in_bufs, refs = refs[: counts[1]], refs[counts[1] :]
        out_bufs, refs = refs[: counts[2]], refs[counts[2] :]
        in_sems, out_sems, *others = refs
        stage = Staged(ins, in_bufs, in_sems, results, out_bufs, out_sems)
        stage.begin()
        kernel_fn(stage, scalar_refs, others)
        stage.end()

    anywhere = pl.BlockSpec(memory_space=pltpu.HBM)
    return pl.pallas_call(
        kernel,
        in_specs=[pl.BlockSpec(memory_space=pltpu.SMEM)] * counts[0]
        + [anywhere] * counts[1],
        out_specs=[anywhere] * counts[2],
        out_shape=outs,
        scratch_shapes=[pltpu.VMEM(a.shape, a.dtype) for a in inputs]
        + [pltpu.VMEM(a.shape, a.dtype) for a in outs]
        + [pltpu.SemaphoreType.DMA((counts[1],)), pltpu.SemaphoreType.DMA((counts[2],))]
        + scratch,
        compiler_params=kernel_params(),
        cost_estimate=cost(micros),
        name=name,
    )(*scalars, *inputs)


def unpack_block(block, col, row, cols, rows, qkv_ref, out_ref, norm_ref):
    width = norm_ref.shape[1]
    deep = width // rows
    qkv_rows = 3 * width // cols
    out_rows = width // cols
    lanes = pl.ds(row * deep, deep)
    qkv_ref[pl.ds(col * qkv_rows, qkv_rows), lanes] = block[0:qkv_rows, :]
    out_ref[pl.ds(col * out_rows, out_rows), lanes] = block[qkv_rows : qkv_rows + out_rows, :]
    tail = block[qkv_rows + out_rows : qkv_rows + out_rows + 16, :].astype(jnp.float32)
    if col == 0:
        norm_ref[0:4, lanes] = tail[0:4] + tail[4:8] + tail[8:12]


def one_hot(slot_cols, slots, start=0):
    place = (iota((slot_cols[0].shape[0], slots), 1) + start).astype(jnp.float32)
    hot = place == slot_cols[0]
    for column in slot_cols[1:]:
        hot = hot | (place == column)
    return low(hot.astype(jnp.float32))


def collect(slot_cols, recv_ref, extra_ref):
    slots = recv_ref.shape[0]
    return mxu(one_hot(slot_cols, slots), recv_ref[...]) + mxu(
        one_hot(slot_cols, extra_ref.shape[0], slots), extra_ref[...]
    )


def front_kernel(cols, rows, stage, scalar_refs, scratch):
    (order_ref,) = scalar_refs
    pack_refs = stage.need(0), stage.need(1)
    qkv_ref, out_ref, norm_ref, proj_ref, att_ref, probs_ref, middle_ref, send_ref, extra_ref = (
        stage.out_bufs[:9]
    )
    width = norm_ref.shape[1]
    norm_ref[...] = jnp.zeros_like(norm_ref)
    held = pack_refs[0].shape[0]
    pack_buf = scratch[0]
    pack_buf[0:held] = pack_refs[0][...]
    pack_buf[held:] = pack_refs[1][...]
    for col in range(cols):
        for row in range(rows):
            block = pack_buf[order_ref[col * rows + row]]
            unpack_block(block, col, row, cols, rows, qkv_ref, out_ref, norm_ref)
    for index in range(3):
        stage.ship(index)
    x_ref = stage.need(2)
    images = x_ref.shape[0] // IMG_PAD
    stream = x_ref[...].astype(jnp.float32)
    scaled, inverse = norm_stats(stream)
    scaled_ref, scaled_two_ref, inverse_ref, normed_ref = stage.out_bufs[9:]
    scaled_ref[...] = scaled
    stage.ship(9)
    normed = low(scaled * norm_ref[0:1, :] + norm_ref[1:2, :])
    normed_ref[...] = normed
    stage.ship(12)
    proj_ref[...] = low(mxu_nt(normed, qkv_ref[...]))
    stage.ship(3)
    key_ok = iota((IMG_PAD, IMG_PAD), 0) < IMG_LEN
    for image in range(images):
        span = slice(image * IMG_PAD, (image + 1) * IMG_PAD)
        for pair in range(HEADS // 2):
            lanes = slice(pair * 128, (pair + 1) * 128)
            queries = proj_ref[span, lanes]
            keys = proj_ref[span, width + pair * 128 : width + (pair + 1) * 128]
            values_t = jnp.transpose(
                proj_ref[span, 2 * width + pair * 128 : 2 * width + (pair + 1) * 128]
            )
            mixed = []
            for half in range(2):
                scores = mxu_nt(pick_half(keys, half), queries) * HEAD_DIM**-0.5
                scores = jnp.where(key_ok, scores, -1e30)
                top = jnp.max(scores, axis=0, keepdims=True)
                shifted = jnp.exp(scores - top)
                total = jnp.sum(shifted, axis=0, keepdims=True)
                probs = low(shifted * (1.0 / total))
                head = image * HEADS + pair * 2 + half
                probs_ref[head * IMG_PAD : (head + 1) * IMG_PAD, :] = probs
                mixed.append(mxu(values_t[half * HEAD_DIM : (half + 1) * HEAD_DIM, :], probs))
            att_ref[span, lanes] = low(jnp.transpose(jnp.concatenate(mixed, axis=0)))
    stage.ship(4)
    stage.ship(5)
    middle = stream + mxu(att_ref[...], out_ref[...])
    middle_ref[...] = middle
    stage.ship(6)
    table_ref = stage.need(3)
    scaled_two, inverse_two = norm_stats(middle)
    scaled_two_ref[...] = scaled_two
    stage.ship(10)
    lane = iota((inverse.shape[0], 8), 1)
    inverse_ref[...] = jnp.where(lane == 0, inverse, inverse_two)
    stage.ship(11)
    second = low(scaled_two * norm_ref[2:3, :] + norm_ref[3:4, :])
    for start, size, result in slot_parts(send_ref, extra_ref):
        place = (iota((size, table_ref.shape[1]), 0) + start).astype(jnp.float32)
        hot = (place == table_ref[0:1, :]) | (place == table_ref[1:2, :])
        rows_out = mxu(low(hot.astype(jnp.float32)), second)
        if result is extra_ref:
            count = jnp.sum(table_ref[4:5, :], axis=1, keepdims=True)
            first_part = jnp.minimum(count, 256.0)
            rows_out = last_row(rows_out, (first_part, count - first_part))
        result[...] = low(rows_out)
    stage.ship(7)
    stage.ship(8)


def last_row(rows, values):
    lane = iota(rows.shape, 1)
    split = jnp.zeros_like(rows)
    for index, value in enumerate(values):
        split = jnp.where(lane == index, value, split)
    return jnp.where(iota(rows.shape, 0) == rows.shape[0] - 1, split, rows)


def slot_parts(send_ref, extra_ref):
    slots = send_ref.shape[0]
    size = min(512, slots)
    parts = [(start, size, send_ref.at[start : start + size]) for start in range(0, slots, size)]
    return parts + [(slots, extra_ref.shape[0], extra_ref)]


def front_call(cols, rows, slots, spare, order, x_pad, packs, table):
    tokens, width = x_pad.shape
    images = tokens // IMG_PAD
    half, full = jnp.bfloat16, jnp.float32
    outs = staged_call(
        functools.partial(front_kernel, cols, rows),
        "front",
        11,
        [order],
        [*packs, x_pad, table],
        [
            ((3 * width, width), half),
            ((width, width), half),
            ((8, width), full),
            ((tokens, 3 * width), half),
            ((tokens, width), half),
            ((images * HEADS * IMG_PAD, IMG_PAD), half),
            ((tokens, width), full),
            ((slots, width), half),
            ((spare, width), half),
            ((tokens, width), full),
            ((tokens, width), full),
            ((tokens, 8), full),
            ((tokens, width), half),
        ],
        [pltpu.VMEM((cols * rows, *packs[0].shape[1:]), half)],
    )
    qkv, out, norms, proj, att, probs, middle, send, extra, *stats = outs
    return send, extra, middle, proj, att, probs, qkv, out, norms, stats


def weight_copies(row_ref, piece_refs, buffer, sems):
    deep = piece_refs[0].shape[0]
    return [
        pltpu.make_async_copy(
            piece,
            buffer.at[pl.ds(pl.multiple_of(row_ref[index] * deep, deep), deep), :],
            sems.at[index],
        )
        for index, piece in enumerate(piece_refs)
    ]


GELU_A = 0.7978845608028654
GELU_B = 0.044715


def gelu_low(pre):
    inner = pre * (GELU_A + GELU_A * GELU_B * (pre * pre))
    half = 0.5 * pre
    return low(half + half * jnp.tanh(inner))


def gelu_both(pre):
    square = pre * pre
    curve = jnp.tanh(pre * (GELU_A + GELU_A * GELU_B * square))
    half = 0.5 * pre
    value = half + half * curve
    slope = 0.5 + 0.5 * curve + half * (1.0 - curve * curve) * (
        GELU_A + 3.0 * GELU_A * GELU_B * square
    )
    return low(value), low(slope)


def ff_chunks(width):
    size = min(width, 512)
    return [slice(start, start + size) for start in range(0, width, size)]


def row_blocks(rows, spare_rows):
    size = min(512, rows)
    blocks = [slice(start, start + size) for start in range(0, rows, size)]
    blocks[-1] = slice(blocks[-1].start, rows + spare_rows)
    return blocks


def spare_chunks(rows):
    size = min(rows, 1024)
    return [slice(start, start + size) for start in range(0, rows, size)]


def pick_rows(pick_ref, extra_ref):
    total = None
    for part in spare_chunks(extra_ref.shape[0]):
        term = mxu(pick_ref[:, part], extra_ref[part, :])
        total = term if total is None else total + term
    return low(total)


def place_rows(pick_ref, rows, kept_ref, sent_ref):
    half = kept_ref.shape[0]
    for start, result in ((0, kept_ref), (half, sent_ref)):
        for part in spare_chunks(half):
            source = slice(start + part.start, start + part.stop)
            result[part, :] = low(mxu_tn(pick_ref[:, source], rows))


def expert_rows(rows_in, up_buf, wait_down, down_buf):
    hiddens = [gelu_low(mxu(rows_in, up_buf[:, part])) for part in ff_chunks(up_buf.shape[1])]
    wait_down()
    total = None
    for part, hidden in zip(ff_chunks(up_buf.shape[1]), hiddens):
        term = mxu_nt(hidden, down_buf[:, part])
        total = term if total is None else total + term
    return low(total)


def pull_rows(grads_in, slope_ref, rows, up_buf, wait_up, down_buf, pre_ref):
    parts = ff_chunks(up_buf.shape[1])
    for part in parts:
        slope = slope_ref[rows, part].astype(jnp.float32)
        pre_ref[rows, part] = low(mxu(grads_in, down_buf[:, part]) * slope)
    wait_up()
    total = None
    for part in parts:
        term = mxu_nt(pre_ref[rows, part], up_buf[:, part])
        total = term if total is None else total + term
    return low(total)


def expert_kernel(pull, pieces, row_ref, main_ref, extra_ref, pick_ref, *rest):
    if pull:
        slope_ref, *rest = rest
    ups, downs, rest = rest[:pieces], rest[pieces : 2 * pieces], rest[2 * pieces :]
    send_ref, kept_ref, sent_ref, rows_ref, *rest = rest
    if pull:
        pre_ref, slope_buf, pre_buf, *rest = rest
    extra_buf, pick_buf, kept_buf, sent_buf, rows_buf, total_buf, up_buf, down_buf, *sems = rest
    up_sems, down_sems, in_sems, out_sems = sems
    main = main_ref.shape[0]
    blocks = row_blocks(main, rows_buf.shape[0] - main)
    inner = [slice(rows.start, min(rows.stop, main)) for rows in blocks]

    def part_of(ref, rows):
        return ref.at[rows.start : rows.stop, :]

    def copy_in(source, target, index):
        return pltpu.make_async_copy(source, target, in_sems.at[index])

    up_copies = weight_copies(row_ref, ups, up_buf, up_sems)
    down_copies = weight_copies(row_ref, downs, down_buf, down_sems)
    first_weights, last_weights = (
        (down_copies, up_copies) if pull else (up_copies, down_copies)
    )
    count = len(blocks)
    late_copies = [
        copy_in(extra_ref, extra_buf, 0),
        copy_in(pick_ref, pick_buf, 1),
    ]
    slope_copies = [
        copy_in(part_of(slope_ref, rows), part_of(slope_buf, rows), 2 + index)
        for index, rows in enumerate(blocks)
    ] if pull else []
    for copy in [*first_weights, *slope_copies[:1], *last_weights, *late_copies, *slope_copies[1:]]:
        copy.start()
    rows_buf[0:main, :] = main_ref[...]
    for copy in first_weights:
        copy.wait()
    sent = []

    def send_out(source, target):
        copy = pltpu.make_async_copy(source, target, out_sems.at[len(sent)])
        copy.start()
        sent.append(copy)

    for index, rows in enumerate(blocks):
        if index == count - 1:
            for copy in late_copies:
                copy.wait()
            rows_buf[main:, :] = pick_rows(pick_buf, extra_buf)
            send_out(rows_buf, rows_ref)

        def wait_last():
            if index == 0:
                for copy in last_weights:
                    copy.wait()

        if pull:
            slope_copies[index].wait()
            total = pull_rows(rows_buf[rows, :], slope_buf, rows, up_buf, wait_last, down_buf, pre_buf)
            send_out(part_of(pre_buf, rows), part_of(pre_ref, rows))
        else:
            total = expert_rows(rows_buf[rows, :], up_buf, wait_last, down_buf)
        total_buf[rows, :] = total
        send_out(part_of(total_buf, inner[index]), part_of(send_ref, inner[index]))
    place_rows(pick_buf, total_buf[main:, :], kept_buf, sent_buf)
    send_out(kept_buf, kept_ref)
    send_out(sent_buf, sent_ref)
    for copy in sent:
        copy.wait()


def expert_call(name, rowpos, main, extra, pick, slope, ups, downs):
    slots, width = main.shape
    ff = ups[0].shape[1]
    rows = slots + pick.shape[0]
    blocks = len(row_blocks(slots, pick.shape[0]))
    pull = slope is not None
    half = (extra.shape[0] // 2, width)
    anywhere = pl.BlockSpec(memory_space=pltpu.HBM)
    inputs = [main, extra, pick] + ([slope] if pull else [])
    outs = [(slots, width), half, half, (rows, width)] + ([(rows, ff)] if pull else [])

    def buffer(shape):
        return pltpu.VMEM(shape, jnp.bfloat16)

    return pl.pallas_call(
        functools.partial(expert_kernel, pull, len(ups)),
        in_specs=[
            pl.BlockSpec(memory_space=pltpu.SMEM),
            pl.BlockSpec(memory_space=pltpu.VMEM),
        ]
        + [anywhere] * (len(inputs) - 1 + 2 * len(ups)),
        out_specs=[anywhere] * len(outs),
        out_shape=[jax.ShapeDtypeStruct(shape, jnp.bfloat16) for shape in outs],
        scratch_shapes=([buffer((rows, ff))] * 2 if pull else [])
        + [buffer(extra.shape), buffer(pick.shape), buffer(half), buffer(half)]
        + [buffer((rows, width))] * 2
        + [buffer((width, ff))] * 2
        + [
            pltpu.SemaphoreType.DMA((len(ups),)),
            pltpu.SemaphoreType.DMA((len(ups),)),
            pltpu.SemaphoreType.DMA((blocks + 2,)),
            pltpu.SemaphoreType.DMA((2 * blocks + 3,)),
        ],
        compiler_params=kernel_params(),
        cost_estimate=cost(12),
        name=name,
    )(rowpos, *inputs, *ups, *downs)


def hidden_kernel(pieces, row_ref, rows_ref, *rest):
    ups = rest[:pieces]
    hidden_ref, slope_ref, up_buf, sems = rest[pieces:]

    @pl.when(pl.program_id(0) == 0)
    def _():
        copies = weight_copies(row_ref, ups, up_buf, sems)
        for copy in copies:
            copy.start()
        for copy in copies:
            copy.wait()

    rows_in = rows_ref[...]
    for part in ff_chunks(up_buf.shape[1]):
        hidden, slope = gelu_both(mxu(rows_in, up_buf[:, part]))
        hidden_ref[:, part] = hidden
        slope_ref[:, part] = slope


def hidden_call(rowpos, slot_rows, ups):
    rows, width = slot_rows.shape
    ff = ups[0].shape[1]
    block = 384 if rows % 384 == 0 else 128
    wide = pl.BlockSpec((block, ff), lambda i: (i, 0))
    return pl.pallas_call(
        functools.partial(hidden_kernel, len(ups)),
        grid=(rows // block,),
        in_specs=[
            pl.BlockSpec(memory_space=pltpu.SMEM),
            pl.BlockSpec((block, width), lambda i: (i, 0)),
        ]
        + [pl.BlockSpec(memory_space=pl.ANY)] * len(ups),
        out_specs=[wide, wide],
        out_shape=[jax.ShapeDtypeStruct((rows, ff), jnp.bfloat16)] * 2,
        scratch_shapes=[
            pltpu.VMEM((width, ff), jnp.bfloat16),
            pltpu.SemaphoreType.DMA((len(ups),)),
        ],
        compiler_params=kernel_params(dimension_semantics=("arbitrary",)),
        cost_estimate=cost(3),
        name="hidden",
    )(rowpos, slot_rows, *ups)


WG_PART = 1024


def weight_grad_kernel(pieces, row_ref, left_ref, right_ref, *rest):
    results = rest[:pieces]
    left_buf, total_buf = rest[pieces:]
    deep = results[0].shape[0]

    @pl.when(pl.program_id(0) == 0)
    def _():
        left_buf[...] = jnp.transpose(left_ref[...])

    total_buf[...] = low(mxu(left_buf[...], right_ref[...]))
    for index, result in enumerate(results):
        start = pl.multiple_of(row_ref[index] * deep, deep)
        result[...] = total_buf[pl.ds(start, deep), :]


def weight_grad_call(rowpos, left, right, deep):
    rows, width = left.shape
    ff = right.shape[1]
    pieces = width // deep
    part = min(ff, WG_PART)
    return pl.pallas_call(
        functools.partial(weight_grad_kernel, pieces),
        grid=(ff // part,),
        in_specs=[
            pl.BlockSpec(memory_space=pltpu.SMEM),
            pl.BlockSpec((rows, width), lambda i: (0, 0)),
            pl.BlockSpec((rows, part), lambda i: (0, i)),
        ],
        out_specs=[pl.BlockSpec((deep, part), lambda i: (0, i))] * pieces,
        out_shape=[jax.ShapeDtypeStruct((deep, ff), jnp.bfloat16)] * pieces,
        scratch_shapes=[
            pltpu.VMEM((width, rows), jnp.bfloat16),
            pltpu.VMEM((width, part), jnp.bfloat16),
        ],
        compiler_params=kernel_params(dimension_semantics=("arbitrary",)),
        cost_estimate=cost(1),
        name="weight_grad",
    )(rowpos, left, right)


def turn_kernel(stage, scalar_refs, scratch):
    recv_ref, back_ref, cols_ref = (stage.need(index) for index in range(3))
    mixed_ref, grad_ref, send_ref, extra_ref = stage.out_bufs
    first = collect([cols_ref[:, 0:1]], recv_ref, back_ref)
    second = collect([cols_ref[:, 1:2]], recv_ref, back_ref)
    middle_ref, teacher_ref, cot_ref, valid_ref, table_ref = (
        stage.need(index) for index in range(3, 8)
    )
    result = middle_ref[...] + cols_ref[:, 2:3] * first + cols_ref[:, 3:4] * second
    crop_to(scratch[0], result)
    mixed_ref[...] = low(scratch[0][...])
    stage.ship(0)
    mismatch = result - teacher_ref[...].astype(jnp.float32)
    masked = cols_ref[:, 4:5] * mismatch
    valid_total = valid_ref[...]
    squares = jnp.sum(masked * mismatch, axis=0, keepdims=True)
    square_sum = jnp.sum(squares, axis=1, keepdims=True)
    grad_out = cot_ref[...].astype(jnp.float32) + (2.0 / valid_total) * masked
    grad_ref[...] = grad_out
    stage.ship(1)
    rounded = low(grad_out).astype(jnp.float32)
    both = jnp.concatenate(
        [low(cols_ref[:, 2:3] * rounded), low(cols_ref[:, 3:4] * rounded)], axis=0
    )
    for start, size, part in slot_parts(send_ref, extra_ref):
        place = (iota((size, table_ref.shape[1]), 0) + start).astype(jnp.float32)
        hot = jnp.concatenate(
            [
                low((place == table_ref[0:1, :]).astype(jnp.float32)),
                low((place == table_ref[1:2, :]).astype(jnp.float32)),
            ],
            axis=1,
        )
        rows = mxu(hot, both)
        if part is extra_ref:
            top = low(square_sum).astype(jnp.float32)
            rest = square_sum - top
            middle = low(rest).astype(jnp.float32)
            rows = last_row(rows, (top, middle, rest - middle))
        part[...] = low(rows)
    stage.ship(2)
    stage.ship(3)


def turn_call(recv, back, cols, table, middle, teacher, cot, valid):
    half, full = jnp.bfloat16, jnp.float32
    own = (middle.shape[0] // IMG_PAD * IMG_LEN, middle.shape[1])
    mixed, grad_out, send, extra = staged_call(
        turn_kernel,
        "turn",
        6,
        [],
        [recv, back, cols, middle, teacher, cot, valid, table],
        [(own, half), (middle.shape, full), (recv.shape, half), (back.shape, half)],
        [pltpu.VMEM(own, full)],
    )
    return send, extra, mixed, grad_out


def back_kernel(cols_n, rows_n, stage, scalar_refs, scratch):
    (order_ref,) = scalar_refs
    gproj_buf, gatt_buf, gqkv_buf, gout_buf, gnorm_buf, pack_buf = scratch
    input_ref = stage.out_bufs[0]
    recv_ref, back_ref, cols_ref = (stage.need(index) for index in range(3))
    width = recv_ref.shape[1]
    grad_second = collect([cols_ref[:, 0:1], cols_ref[:, 1:2]], recv_ref, back_ref)
    scaled_two_ref, norm_ref, grad_ref, inverse_ref = (
        stage.need(index) for index in range(3, 7)
    )
    images = scaled_two_ref.shape[0] // IMG_PAD
    scaled_two, inverse_two = scaled_two_ref[...], inverse_ref[:, 1:2]
    gnorm_buf[...] = jnp.zeros_like(gnorm_buf)
    gnorm_buf[2:3, :] = jnp.sum(grad_second * scaled_two, axis=0, keepdims=True)
    gnorm_buf[3:4, :] = jnp.sum(grad_second, axis=0, keepdims=True)
    grad_middle = grad_ref[...] + norm_pull(grad_second, scaled_two, inverse_two, norm_ref[2:3, :])
    middle_low = low(grad_middle)
    att_ref, out_ref = stage.need(7), stage.need(8)
    gout_buf[...] = low(mxu(jnp.transpose(att_ref[...]), middle_low))
    proj_ref, probs_ref = stage.need(9), stage.need(10)
    gatt_buf[...] = low(mxu_nt(middle_low, out_ref[...]))
    scale = HEAD_DIM**-0.5
    for image in range(images):
        span = slice(image * IMG_PAD, (image + 1) * IMG_PAD)
        for pair in range(HEADS // 2):
            q_lanes = slice(pair * 128, (pair + 1) * 128)
            k_lanes = slice(width + pair * 128, width + (pair + 1) * 128)
            v_lanes = slice(2 * width + pair * 128, 2 * width + (pair + 1) * 128)
            queries = proj_ref[span, q_lanes]
            keys = proj_ref[span, k_lanes]
            values = proj_ref[span, v_lanes]
            upstream = gatt_buf[span, q_lanes]
            keys_t = jnp.transpose(keys)
            query_parts = []
            key_parts = []
            value_parts = []
            for half in range(2):
                head = image * HEADS + pair * 2 + half
                probs_low = probs_ref[head * IMG_PAD : (head + 1) * IMG_PAD, :]
                probs = probs_low.astype(jnp.float32)
                grad_probs = mxu_nt(pick_half(values, half), upstream)
                inner = jnp.sum(probs * grad_probs, axis=0, keepdims=True)
                grad_scores = low(probs * (grad_probs - inner))
                value_parts.append(mxu(probs_low, upstream))
                key_parts.append(mxu(grad_scores, queries))
                query_parts.append(
                    mxu(keys_t[half * HEAD_DIM : (half + 1) * HEAD_DIM, :], grad_scores)
                )
            left = half_mask(key_parts[0].shape, 0)
            gproj_buf[span, q_lanes] = low(
                jnp.transpose(jnp.concatenate(query_parts, axis=0)) * scale
            )
            gproj_buf[span, k_lanes] = low(jnp.where(left, key_parts[0], key_parts[1]) * scale)
            gproj_buf[span, v_lanes] = low(jnp.where(left, value_parts[0], value_parts[1]))
    normed_ref, qkv_ref, scaled_ref = (stage.need(index) for index in range(11, 14))
    scaled, inverse = scaled_ref[...], inverse_ref[:, 0:1]
    gqkv_buf[...] = low(mxu(jnp.transpose(gproj_buf[...]), normed_ref[...]))
    grad_normed = mxu(gproj_buf[...], qkv_ref[...])
    gnorm_buf[0:1, :] = jnp.sum(grad_normed * scaled, axis=0, keepdims=True)
    gnorm_buf[1:2, :] = jnp.sum(grad_normed, axis=0, keepdims=True)
    crop_to(input_ref, grad_middle + norm_pull(grad_normed, scaled, inverse, norm_ref[0:1, :]))
    stage.ship(0)
    deep = width // rows_n
    qkv_rows = 3 * width // cols_n
    out_rows = width // cols_n
    for col in range(cols_n):
        for row in range(rows_n):
            index = order_ref[col * rows_n + row]
            lanes = slice(row * deep, (row + 1) * deep)
            qkv_part = gqkv_buf[col * qkv_rows : (col + 1) * qkv_rows, lanes]
            out_part = gout_buf[col * out_rows : (col + 1) * out_rows, lanes]
            norm_part = low(gnorm_buf[:, lanes])
            pack_buf[index, 0:qkv_rows, :] = qkv_part
            pack_buf[index, qkv_rows : qkv_rows + out_rows, :] = out_part
            pack_buf[index, qkv_rows + out_rows : qkv_rows + out_rows + 16, :] = norm_part
    half = pack_buf.shape[0] // 2
    stage.ship(2, pack_buf.at[half:])
    stage.ship(1, pack_buf.at[:half])


def back_call(
    cols_n, rows_n, order, recv, back, cols, stats, grad_out, proj, att, probs, qkv, out, norms
):
    scaled, scaled_two, inverse, normed = stats
    tokens, width = scaled.shape
    blocks = cols_n * rows_n
    block = (blocks // 2, 4 * width // cols_n + 16, width // rows_n)
    half, full = jnp.bfloat16, jnp.float32
    return staged_call(
        functools.partial(back_kernel, cols_n, rows_n),
        "back",
        12,
        [order],
        [
            recv, back, cols, scaled_two, norms, grad_out, inverse, att, out, proj, probs,
            normed, qkv, scaled,
        ],
        [((tokens // IMG_PAD * IMG_LEN, width), full), (block, half), (block, half)],
        [
            pltpu.VMEM((tokens, 3 * width), half),
            pltpu.VMEM((tokens, width), half),
            pltpu.VMEM((3 * width, width), half),
            pltpu.VMEM((width, width), half),
            pltpu.VMEM((16, width), full),
            pltpu.VMEM((blocks, *block[1:]), half),
        ],
    )


def adam_kernel(slabs, where_ref, *refs):
    up_grads, down_grads = refs[:slabs], refs[slabs : 2 * slabs]
    ins, outs = refs[2 * slabs : 2 * slabs + 6], refs[-6:]
    for index in range(slabs):

        @pl.when(pl.program_id(0) == index)
        def _():
            for rate, gradient, inputs, results in (
                (rate_up, up_grads[index], ins[0:3], outs[0:3]),
                (rate_down, down_grads[index], ins[3:6], outs[3:6]),
            ):
                first_new, second_new, weight_new = adam_update(
                    inputs[0][0],
                    inputs[1][0],
                    inputs[2][0],
                    gradient[...].astype(jnp.float32),
                    rate,
                    decay_matrix,
                )
                results[0][0] = first_new
                results[1][0] = second_new
                results[2][0] = weight_new


def adam_call(places, gradients, arrays, earlier):
    slabs = len(gradients)
    deep, ff = gradients[0][0].shape
    tile = min(deep, 64 * slabs)
    tiles = deep // tile

    def gradient_spec(index):
        def where_is(slab, part, where):
            return (jnp.where(slab == index, part, jnp.where(slab < index, 0, tiles - 1)), 0)

        return pl.BlockSpec((tile, ff), where_is)

    block = pl.BlockSpec(
        (1, tile, ff), lambda slab, part, where: (where[2 * slab], part, where[2 * slab + 1])
    )
    in_specs = [gradient_spec(index) for index in range(slabs)] * 2 + [block] * 6
    aliases = {}
    if earlier is not None:
        aliases = {1 + len(in_specs) + index: index for index in range(6)}
        in_specs += [pl.BlockSpec(memory_space=pl.ANY)] * 6
    return pl.pallas_call(
        functools.partial(adam_kernel, slabs),
        grid_spec=pltpu.PrefetchScalarGridSpec(
            num_scalar_prefetch=1, grid=(slabs, tiles), in_specs=in_specs, out_specs=[block] * 6
        ),
        out_shape=[jax.ShapeDtypeStruct(arrays[0].shape, jnp.float32)] * 6,
        input_output_aliases=aliases,
        compiler_params=kernel_params(dimension_semantics=("arbitrary", "arbitrary")),
        cost_estimate=cost(6 * slabs),
        name="adam",
    )(places, *[g[0] for g in gradients], *[g[1] for g in gradients], *arrays, *(earlier or ()))


def swap(values, mask):
    rows = lax.axis_size("row")
    cols = lax.axis_size("col")

    def flat(place):
        return place % rows * cols + place // rows

    return lax.ppermute(
        values, ("row", "col"), [(flat(i), flat(i ^ mask)) for i in range(rows * cols)]
    )


def gather_steps():
    bits = []
    bit = lax.axis_size("col") * lax.axis_size("row") // 2
    while bit:
        bits.append(bit)
        bit //= 2
    return [bits[start : start + 2] for start in range(0, len(bits), 2)]


def masks_of(bits):
    return [
        sum(bit for place, bit in enumerate(bits) if index >> place & 1)
        for index in range(1, 1 << len(bits))
    ]


def weight_steps():
    rows = lax.axis_size("row")
    far = [bit for bits in gather_steps() for bit in bits if 1 < bit < rows]
    wide = [bit for bits in gather_steps() for bit in bits if bit > rows]
    pairs = [wide[start : start + 2] for start in range(0, len(wide), 2)]
    return [bits for bits in [far, *pairs, [rows], [1]] if bits]


def block_order(steps):
    rows = lax.axis_size("row")
    devices = lax.axis_size("col") * rows
    differs = jnp.arange(devices, dtype=jnp.int32) ^ (
        lax.axis_index("col") * rows + lax.axis_index("row")
    )
    order = jnp.zeros((devices,), jnp.int32)
    place = 0
    for bits in steps:
        for bit in bits:
            order = order | jnp.where((differs & bit) != 0, 1 << place, 0)
            place += 1
    return order


def gather_step(gathered, bits):
    return jnp.concatenate([gathered] + [swap(gathered, mask) for mask in masks_of(bits)], axis=0)


def halves_step(kept, sent):
    return low(kept.astype(jnp.float32) + swap(sent, 1).astype(jnp.float32))


def scatter_step(blocks, bits):
    count = 1 << len(bits)
    size = blocks.shape[0] // count
    total = blocks[:size].astype(jnp.float32)
    for index, mask in enumerate(masks_of(bits)):
        sent = blocks[(index + 1) * size : (index + 2) * size]
        total = total + swap(sent, mask).astype(jnp.float32)
    return low(total)


def pad_images(values):
    tokens, width = values.shape
    images = tokens // IMG_LEN
    padded = jnp.pad(
        values.reshape(images, IMG_LEN, width), ((0, 0), (0, IMG_PAD - IMG_LEN), (0, 0))
    )
    return padded.reshape(images * IMG_PAD, width)


def pad_rows(values, fill):
    images = values.shape[1] // IMG_LEN
    padded = jnp.pad(
        values.reshape(values.shape[0], images, IMG_LEN),
        ((0, 0), (0, 0), (0, IMG_PAD - IMG_LEN)),
        constant_values=fill,
    )
    return padded.reshape(values.shape[0], images * IMG_PAD)


def to_experts(main, extra, share, beside, rows=None):
    if share > 1:
        width = main.shape[1]
        main = jnp.broadcast_to(
            main.reshape(EXPERTS, 1, -1, width),
            (EXPERTS, share, main.shape[0] // EXPERTS, width),
        ).reshape(-1, width)
    first, *others = gather_steps()
    blocks = gather_step(extra[None], first)
    if rows is None:
        main, blocks, beside = lax.optimization_barrier((main, blocks, beside))
    else:
        main, blocks, rows = lax.optimization_barrier((main, blocks, rows))
        beside = beside(rows)
    main = lax.all_to_all(main, BOTH, split_axis=0, concat_axis=0, tiled=True)
    for place, bits in enumerate(others):
        if place == len(others) - 1 and rows is not None:
            blocks, beside = lax.optimization_barrier((blocks, beside))
        blocks = gather_step(blocks, bits)
    return main, blocks.reshape(-1, extra.shape[1]), beside


def from_experts(main, share):
    main = lax.all_to_all(main, BOTH, split_axis=0, concat_axis=0, tiled=True)
    width = main.shape[1]
    if share > 1:
        main = low(
            jnp.sum(main.reshape(EXPERTS, share, -1, width).astype(jnp.float32), axis=1)
        ).reshape(-1, width)
    return main


def spare_home(kept, sent, beside=None):
    blocks = lax.axis_size("row") * lax.axis_size("col") // 2
    blocks = halves_step(
        kept.reshape(blocks, -1, kept.shape[1]), sent.reshape(blocks, -1, sent.shape[1])
    )
    if beside is not None:
        blocks, beside = lax.optimization_barrier((blocks, beside))
    for bits in reversed(gather_steps()[1:]):
        if bits != [1]:
            blocks = scatter_step(blocks, [bit for bit in bits if bit != 1])
    return blocks if beside is None else (blocks, beside)


def body(*args):
    (
        x_in,
        cotangent,
        teacher,
        valid_mask,
        routes,
        gate_weights,
        norm_params,
        qkv_weight,
        out_weight,
        up_weight,
        down_weight,
        norm_first,
        norm_second,
        qkv_first,
        qkv_second,
        out_first,
        out_second,
        up_first,
        up_second,
        down_first,
        down_second,
    ) = args
    rows_n = lax.axis_size("row")
    cols_n = lax.axis_size("col")
    devices = rows_n * cols_n
    my_row = lax.axis_index("row")
    me = lax.axis_index("col") * rows_n + my_row
    tokens, width = x_in.shape
    token_total = routes.shape[1]
    experts_here, deep, ff = up_weight.shape
    share = rows_n // experts_here
    ff_here = ff // share
    mean_load = TOP * tokens / EXPERTS
    cap = max(16, 16 * round(1.3 * mean_load / 16))
    slots = EXPERTS * cap
    spare = max(32, 8 * round(mean_load / 5))
    room = 4 * devices

    def three_parts(values):
        top = lax.reduce_precision(values, 8, 7)
        rest = values - top
        middle_part = lax.reduce_precision(rest, 8, 7)
        return [low(top), low(middle_part), low(rest - middle_part)]

    small = jnp.concatenate(
        [
            low(jnp.transpose(qkv_weight)),
            low(out_weight),
            *three_parts(norm_params),
            jnp.zeros((4, deep), jnp.bfloat16),
        ],
        axis=0,
    )
    order = block_order(gather_steps())
    pack_order = block_order(weight_steps())

    partners = [my_row ^ index for index in range(rows_n)]
    rowpos = jnp.stack(partners).astype(jnp.int32)

    def slab(values, partner):
        return low(
            lax.dynamic_slice(
                values, (partner // share, 0, partner % share * ff_here), (1, deep, ff_here)
            )[0]
        )

    far = rows_n // 2
    first_step, second_step, *last_steps = gather_steps()
    far_ones = [index for index in range(2, rows_n)] or [1]
    first_far, *more_far = far_ones
    steps = weight_steps()
    pack = gather_step(small[None], steps[0])
    held = (routes, gate_weights, valid_mask, x_in, up_weight, down_weight)
    pack, held = lax.optimization_barrier((pack, held))
    early = swap(slab(up_weight, partners[first_far]), first_far)

    start = me * tokens
    own_routes = pad_rows(lax.dynamic_slice_in_dim(held[0], start, tokens, 1), -1)
    own_gates = pad_rows(lax.dynamic_slice_in_dim(held[1], start, tokens, 1), 0)
    own_mask = pad_rows(
        lax.dynamic_slice_in_dim(held[2], my_row * tokens, tokens, 0)[None], 0
    ).astype(jnp.float32)
    padded = own_routes.shape[1]
    extra = jnp.concatenate(
        [jnp.zeros((2, padded), jnp.float32), own_gates, own_mask, jnp.zeros((3, padded), jnp.float32)],
        axis=0,
    )
    all_routes = jnp.pad(
        held[0], ((0, 0), (0, round_up(token_total, 2048) - token_total)), constant_values=-1
    )
    mine = (me // share).astype(jnp.int32).reshape(1)
    x_pad = pad_images(held[3])
    up_slabs = [slab(held[4], partners[index]) for index in more_far]
    down_slabs = [slab(held[5], partners[index]) for index in far_ones]
    near = [1] if first_far != 1 else []
    near_slabs = [(slab(held[4], partners[p]), slab(held[5], partners[p])) for p in near]
    ups = {0: slab(held[4], partners[0])}
    downs = {0: slab(held[5], partners[0])}
    for bits in steps[1:-2]:
        pack = gather_step(pack, bits)
    early, up_slabs = lax.optimization_barrier((early, up_slabs))
    pack, early, down_slabs, near_slabs = lax.optimization_barrier(
        (pack, early, down_slabs, near_slabs)
    )
    ups[first_far] = early
    up_pieces = [swap(piece, index) for index, piece in zip(more_far, up_slabs)]
    pack = gather_step(pack, steps[-2])
    table, table_cols, pick, excess = route_call(
        cap, spare, room, tokens, mine, all_routes, own_routes, extra, order[None]
    )
    overflow = excess[0, 0] > 0

    pack, up_pieces, table, table_cols, pick, x_pad, down_slabs = lax.optimization_barrier(
        (pack, up_pieces, table, table_cols, pick, x_pad, down_slabs)
    )
    ups.update(zip(more_far, up_pieces))
    for index, piece in zip(far_ones, down_slabs):
        downs[index] = swap(piece, index)
    for p, (up_slab, down_slab) in zip(near, near_slabs):
        ups[p], downs[p] = swap(up_slab, p), swap(down_slab, p)
    packs = [pack, swap(pack, 1)]
    if near:
        packs, ups, downs[1] = lax.optimization_barrier((packs, ups, downs[1]))
    send, spare_rows, middle, proj, att, probs, qkv_all, out_all, norms, stats = front_call(
        cols_n, rows_n, slots, spare, pack_order, x_pad, packs, table
    )
    main, extras, (ups, downs) = to_experts(send, spare_rows, share, (ups, downs))
    ups = [ups[index] for index in range(rows_n)]
    downs = [downs[index] for index in range(rows_n)]

    counts = extras.reshape(devices, spare, width)[:, spare - 1, :2].astype(jnp.float32)
    valid_total = jnp.sum(counts)
    main, kept, sent, slot_rows = expert_call(
        "expert", rowpos, main, extras, pick, None, ups, downs
    )
    combined = from_experts(main, share)
    extras = spare_home(kept, sent)
    grad_send, grad_spare, mixed_rows, grad_out = turn_call(
        combined,
        scatter_step(extras, gather_steps()[0])[0],
        table_cols,
        table,
        middle,
        pad_images(teacher),
        pad_images(cotangent),
        valid_total[None, None],
    )
    main, extras, (hidden, slope) = to_experts(
        grad_send, grad_spare, share, lambda rows: hidden_call(rowpos, rows, ups), slot_rows
    )
    errors = extras.reshape(devices, spare, width)
    main, kept, sent, grad_slots, grad_pre = expert_call(
        "pull", rowpos, main, extras, pick, slope, ups, downs
    )
    grad_back = from_experts(main, share)
    extras, (grad_pre, grad_slots) = spare_home(kept, sent, (grad_pre, grad_slots))
    up_grads = weight_grad_call(rowpos, slot_rows, grad_pre, deep)
    raw_ups = up_grads
    down_grads = weight_grad_call(rowpos, grad_slots, hidden, deep)
    extras, up_grads, down_grads = lax.optimization_barrier((extras, up_grads, down_grads))
    grad_back_spare = scatter_step(extras, gather_steps()[0])[0]

    arrays = (up_weight, up_first, up_second, down_weight, down_first, down_second)

    def places_of(chosen):
        return jnp.stack(
            [value for p in chosen for value in (partners[p] // share, partners[p] % share)]
        ).astype(jnp.int32)

    near = list(range(min(2, rows_n)))
    apart = list(range(2, rows_n))
    groups = [apart[: len(apart) // 2], apart[len(apart) // 2 :]]
    groups = [group for group in groups if group]
    gradients = {}
    for index in near:
        pair = (up_grads[index], down_grads[index])
        gradients[index] = tuple(swap(p, index) for p in pair) if index else pair
    if groups:
        up_far = [swap(raw_ups[index], index) for index in groups[0]]
        grad_back, grad_back_spare, up_far, down_grads = lax.optimization_barrier(
            (grad_back, grad_back_spare, up_far, down_grads)
        )
        down_far = [swap(down_grads[index], index) for index in groups[0]]

    input_rows, blocks, sent_blocks = back_call(
        cols_n,
        rows_n,
        pack_order,
        grad_back,
        grad_back_spare,
        table_cols,
        stats,
        grad_out,
        proj,
        att,
        probs,
        qkv_all,
        out_all,
        norms,
    )
    if groups:
        blocks, sent_blocks, down_far = lax.optimization_barrier((blocks, sent_blocks, down_far))
        for index, pair in zip(groups[0], zip(up_far, down_far)):
            gradients[index] = pair
    experts_new = None
    later = []
    for place, bits in enumerate(reversed(weight_steps())):
        if place == 0:
            blocks = halves_step(blocks, sent_blocks)
        else:
            blocks = scatter_step(blocks, bits)
        if place == 0:
            sent = [gradients[index] for index in near]
            apart_sent = [gradients[index] for index in groups[0]] if groups else []
            blocks, sent, up_grads, down_grads, errors = lax.optimization_barrier(
                (blocks, sent, up_grads, down_grads, errors)
            )

            experts_new = adam_call(places_of(near), sent, arrays, None)
            if len(groups) > 1:
                later = [
                    (swap(up_grads[index], index), swap(down_grads[index], index))
                    for index in groups[1]
                ]
        if place == 1:
            blocks, experts_new, errors, apart_sent = lax.optimization_barrier(
                (blocks, experts_new, errors, apart_sent)
            )
            loss_value = jnp.sum(errors[:, spare - 1, :3].astype(jnp.float32)[order]) / valid_total
            if groups:
                experts_new = adam_call(places_of(groups[0]), apart_sent, arrays, experts_new)
        if place == 2:
            blocks, experts_new, loss_value = lax.optimization_barrier(
                (blocks, experts_new, loss_value)
            )
    if later:
        experts_new = adam_call(places_of(groups[1]), later, arrays, experts_new)
    up_one, up_two, up_new, down_one, down_two, down_new = experts_new
    summed = blocks[0].astype(jnp.float32)
    qkv_rows = qkv_weight.shape[1]
    out_rows = out_weight.shape[0]
    qkv_one, qkv_two, qkv_new = adam_update(
        qkv_weight, qkv_first, qkv_second, jnp.transpose(summed[:qkv_rows]), rate_qkv, decay_matrix
    )
    out_one, out_two, out_new = adam_update(
        out_weight,
        out_first,
        out_second,
        summed[qkv_rows : qkv_rows + out_rows],
        rate_out,
        decay_matrix,
    )
    norm_one, norm_two, norm_new = adam_update(
        norm_params,
        norm_first,
        norm_second,
        summed[qkv_rows + out_rows : qkv_rows + out_rows + 4],
        rate_norm,
        0.0,
    )
    quick = (
        mixed_rows,
        input_rows,
        loss_value,
        norm_one,
        norm_two,
        norm_new,
        qkv_one,
        qkv_two,
        qkv_new,
        out_one,
        out_two,
        out_new,
        up_one,
        up_two,
        up_new,
        down_one,
        down_two,
        down_new,
    )

    def again(state):
        return (jnp.bool_(False), general_body(*args))

    return lax.while_loop(lambda state: state[0], again, (overflow, quick))[1]


def solution(mesh):
    in_specs = (
        P(("col", "row"), None),
        P(("col", "row"), None),
        P(("col", "row"), None),
        P("col"),
        P(),
        P(),
        P(None, "row"),
        P("row", "col"),
        P("col", "row"),
        P("col", "row", None),
        P("col", "row", None),
        P(None, "row"),
        P(None, "row"),
        P("row", "col"),
        P("row", "col"),
        P("col", "row"),
        P("col", "row"),
        P("col", "row", None),
        P("col", "row", None),
        P("col", "row", None),
        P("col", "row", None),
    )
    out_specs = (
        P(("col", "row"), None),
        P(("col", "row"), None),
        P(),
        P(None, "row"),
        P(None, "row"),
        P(None, "row"),
        P("row", "col"),
        P("row", "col"),
        P("row", "col"),
        P("col", "row"),
        P("col", "row"),
        P("col", "row"),
        P("col", "row", None),
        P("col", "row", None),
        P("col", "row", None),
        P("col", "row", None),
        P("col", "row", None),
        P("col", "row", None),
    )
    return jax.shard_map(body, mesh=mesh, in_specs=in_specs, out_specs=out_specs, check_vma=False)
```
